32 devices in a mesh: band: 8 (over z, y), grid: 2 (over x), ham: 2 (over core).
Axes of the slice: x: 2, y: 2, z: 4, core: 2. Of those that a mesh axis runs over, the one named last changes fastest.
Arguments:
- orbitals: bfloat16 [128, 64, 192], P('band', ('grid', 'ham')), may hold values from -6 to 6
- coulomb: float32 [64, 192], P(('grid', 'ham')), may hold values from 0.1 to 10
- occupied: int32 [8], replicated, may hold values from 1 to 16
- owners: int32 [128, 1], P('band'), may hold values from 0 to 3; in each aligned block of 16 rows (0 to 15, 16 to 31, ...) at most 8 rows name the same one
Outputs:
- projectors: bfloat16 [8, 4, 8, 64, 192], P('band', ('grid', 'ham'))
- intersection: float32 [8, 16, 16], P('band')
The draws below stay inside these ranges and needn't reach their ends.
Inputs may be any that keep to these rules, and one draw needn't show every extreme that they name: `owners`: among the 16 bands of one block at most 8 name the same owner; in some blocks one owner is named by exactly 8.
All inputs are finite; a program needn't handle non-finite values.
Results may differ from the reference program's by a relative error of at most 0.0038.
Values may be sent and summed in bfloat16 or wider, within the bound.
No kernel may reach another device: no remote copies, remote signals or barrier semaphores. Data moves between devices by JAX's collectives and lax.ppermute only.
A program may use at most 64 MiB of HBM per device.

```python
import math
import jax
import jax.numpy as jnp
import numpy as np
from jax import lax

BB = 16
NX = 192
CAP = 8
NB = 128
OWNERS = 4
LINES = 64
CELLS = 12288
N_BAND = 8


def place_ends(entries, key, smallest, largest):
    index_at = [jax.random.randint(jax.random.fold_in(key, axis), (), 0, length) for axis, length in enumerate(entries.shape)]
    widest = entries.shape.index(max(entries.shape))
    neighbour = index_at[:widest] + [(index_at[widest] + 1) % entries.shape[widest]] + index_at[widest + 1:]
    return entries.at[tuple(index_at)].set(smallest).at[tuple(neighbour)].set(largest)


def level_of(stream_key, shape, shards, least, largest):
    level, own = 1.0, jax.random.fold_in(stream_key, 6)
    for position, parts in shards:
        draws = jnp.exp(jax.random.uniform(jax.random.fold_in(own, position), (parts,), jnp.float32, least / len(shards), largest / len(shards)))
        level = level * jnp.repeat(draws, shape[position] // parts).reshape([-1 if axis == position else 1 for axis in range(len(shape))])
    return level


def routed_block(stream_key, own, number, rows, amount, top, bound, lean):
    order = jax.random.permutation(stream_key, amount)
    crowded, usual = load_shares(amount, rows * top, bound, lean, True), load_shares(amount, rows * top, bound, lean, False)
    places = jnp.arange(amount)

    def named(tallies, offset_by):
        used = int((tallies > 0).sum())
        fixed = max(1, used // 4)
        moved = fixed + (places - fixed + offset_by * (used - fixed)) % max(1, amount - fixed)
        return jnp.zeros((amount,), jnp.int32).at[order[jnp.where(places < fixed, places, moved)]].set(jnp.asarray(tallies, jnp.int32))

    tallies = jnp.where(number % 4 == 0, named(crowded, number // 4), named(usual, number - number // 4 - 1))
    mixed = jax.random.permutation(jax.random.fold_in(own, 3), amount)
    giver, sink = mixed[0:amount // 2 * 2:2], mixed[1:amount // 2 * 2:2]
    margin = jnp.minimum(tallies[giver] - 1, bound - tallies[sink]) // 2
    margin = jnp.where((giver == order[0]) | (sink == order[0]) | (tallies[sink] == 0), 0, jnp.maximum(margin, 0))
    moved = jax.random.randint(jax.random.fold_in(own, 4), (amount // 2,), 0, 1 << 20) % (margin + 1)
    tallies = tallies.at[giver].add(-moved).at[sink].add(moved)
    labels = jnp.searchsorted(jnp.cumsum(tallies), jnp.arange(rows * top), side="right").astype(jnp.int32)
    grid = labels.reshape(top, rows).T
    grid = grid[jax.random.permutation(jax.random.fold_in(own, 1), rows)]
    offset_by = jax.random.randint(jax.random.fold_in(own, 2), (rows, 1), 0, top)
    return jnp.take_along_axis(grid, (jnp.arange(top)[None, :] + offset_by) % top, axis=1)


def load_shares(amount, total, bound, slope, full):
    weights = [(1 << 20) // math.isqrt(grade ** slope) + 1 for grade in range(1, amount + 1)]
    largest = bound if full else min(bound, max(-(-total // amount), total * weights[0] // sum(weights)))
    least = 1 if total - largest >= amount - 1 else 0
    counts, surplus = [largest] + [least] * (amount - 1), total - largest - least * (amount - 1)
    while surplus > 0:
        free = [i for i in range(1, amount) if counts[i] < largest] or [i for i in range(1, amount) if counts[i] < bound]
        mass, left = sum([weights[i] for i in free]), surplus
        for i in free:
            addition = min(bound - counts[i], max(1, left * weights[i] // mass), surplus)
            counts[i] = counts[i] + addition
            surplus = surplus - addition
    return np.array(counts)


def noise(rng, dims, width, reach, split=(), held_as=jnp.bfloat16):
    gain = level_of(rng, dims, split, -0.22, 0.18) if split else 1.0
    values = jax.random.normal(rng, dims, jnp.float32) * width * gain
    return jnp.minimum(jnp.maximum(values, -reach), reach).astype(held_as)


def setup_inputs(seed: int = 0) -> dict:
    key_of = jax.random.split(jax.random.key(seed), 5)
    orbitals = noise(key_of[0], (NB, LINES, NX), 1.0, 6.0, ((0, 8), (1, 4)))
    coulomb = jnp.clip(jnp.exp(math.log(10.0) - 4.6051702 * jax.random.uniform(key_of[1], (LINES, NX), jnp.float32) ** level_of(key_of[1], (LINES, NX), ((0, 4),), -0.2, 0.2)), 0.1, 10.0)
    occupied = place_ends(jax.random.randint(key_of[2], (N_BAND,), 1, BB + 1), jax.random.fold_in(key_of[2], 1), 1, BB).astype(jnp.int32)
    owners_keys = jax.random.split(jax.random.fold_in(key_of[3], 1), NB // BB)
    owners_turns = jax.random.permutation(jax.random.fold_in(key_of[3], 3), NB // BB)
    owners = jax.vmap(lambda own, number: routed_block(jax.random.fold_in(key_of[3], 2), own, number, BB, OWNERS, 1, CAP, 2))(owners_keys, owners_turns).reshape((NB, 1))
    return dict(orbitals=orbitals, coulomb=coulomb, occupied=occupied, owners=owners)


def spectral_tables(points):
    midpoint = points // 2
    row_ids = jnp.arange(points)
    frequency = jnp.where(row_ids <= midpoint, row_ids, row_ids - midpoint)
    phases = row_ids[:, None] * frequency[None, :] % points
    angles = phases.astype(jnp.float32) * (2.0 * math.pi / points)
    cosine_cols = (row_ids <= midpoint)[None, :]
    forward_t = jnp.where(cosine_cols, jnp.cos(angles), jnp.sin(angles))
    single = (frequency == 0) | (row_ids == midpoint)
    scaling = jnp.where(single, 1.0, 2.0) / points
    inverse_t = forward_t.T * scaling[:, None]
    return (forward_t.astype(jnp.bfloat16), inverse_t.astype(jnp.bfloat16))

def reference(orbitals, coulomb, occupied, owners):
    midpoint = NX // 2
    mirrored = jnp.roll(coulomb[:, ::-1], 1, axis=1)
    kernel = 0.5 * (coulomb + mirrored)
    multiplier = jnp.concatenate([kernel[:, :midpoint + 1], kernel[:, 1:midpoint]], axis=1)
    forward_b, inverse_b = spectral_tables(NX)
    forward_f = forward_b.astype(jnp.float32)
    inverse_f = inverse_b.astype(jnp.float32)
    blocks = orbitals.reshape(N_BAND, BB, LINES, NX)
    positions = jnp.arange(BB)
    occupancy = (positions[None, :] < occupied[:, None]).astype(jnp.float32)
    owner_blocks = owners[:, 0].reshape(N_BAND, BB)
    slot_ids = jnp.arange(OWNERS * CAP)
    owner_ids = jnp.arange(OWNERS)

    def one_block(inputs):
        block_id, owner_row = inputs
        native = blocks[block_id].astype(jnp.float32)

        def visit(running, offset):
            visited = (block_id + offset) % N_BAND
            guests = blocks[visited].astype(jnp.float32)
            weights = occupancy[visited]
            density = (native[:, None] * guests[None]).astype(jnp.bfloat16).astype(jnp.float32)
            density = density.reshape(BB * BB * LINES, NX)
            spectrum = jnp.dot(density, forward_f, precision=lax.Precision.HIGHEST).reshape(BB, BB, LINES, NX)
            spectrum = (spectrum * multiplier[None, None]).astype(jnp.bfloat16).astype(jnp.float32)
            field = jnp.dot(spectrum.reshape(BB * BB * LINES, NX), inverse_f, precision=lax.Precision.HIGHEST)
            field = field.astype(jnp.bfloat16).astype(jnp.float32).reshape(BB, BB, LINES, NX)
            weighted = guests * weights[:, None, None]
            running = running + jnp.einsum('igLx,gLx->iLx', field, weighted, precision=lax.Precision.HIGHEST)
            return (running, None)
        image, _ = lax.scan(visit, jnp.zeros((BB, LINES, NX), jnp.float32), jnp.arange(-2, 3))
        intersection = jnp.einsum('ilx,klx->ik', native, image, precision=lax.Precision.HIGHEST) / CELLS
        factor = jnp.linalg.cholesky(intersection)
        compressed = lax.linalg.triangular_solve(factor, image.reshape(BB, LINES * NX), left_side=True, lower=True).astype(jnp.bfloat16)
        onehot = (owner_row[:, None] == owner_ids[None, :]).astype(jnp.int32)
        ranking = jnp.sum(jnp.cumsum(onehot, axis=0) * onehot, axis=1) - 1
        target = owner_row * CAP + ranking
        placement = (slot_ids[:, None] == target[None, :]).astype(jnp.float32)
        placed = jnp.dot(placement, compressed.astype(jnp.float32), precision=lax.Precision.HIGHEST).astype(jnp.bfloat16)
        return (placed.reshape(OWNERS, CAP, LINES, NX), intersection)
    projectors, intersections = lax.map(one_block, (jnp.arange(N_BAND), owner_blocks))
    return (projectors, intersections)
```

```python
import math

import jax
import jax.numpy as jnp
import numpy as np
from jax import lax
from jax.experimental import pallas as pl
from jax.experimental.pallas import tpu as pltpu
from jax.sharding import PartitionSpec as P

CAP = 8
REACH = 2
LANES = 128
HIGHEST = lax.Precision.HIGHEST
VMEM_LIMIT = 48 * 1024 * 1024


def shifted(value, axis, steps):
    count = lax.axis_size(axis)
    pairs = [(source, (source + steps) % count) for source in range(count)]
    return lax.ppermute(value, axis, pairs)


def swapped(value, flip):
    count = lax.axis_size("grid") * lax.axis_size("ham")
    pairs = [(source, source ^ flip) for source in range(count)]
    return lax.ppermute(value, ("grid", "ham"), pairs)


def spectral_tables(points):
    midpoint = points // 2
    ids = np.arange(points)
    frequency = np.where(ids <= midpoint, ids, ids - midpoint)
    angles = (ids[:, None] * frequency[None, :] % points) * (2.0 * math.pi / points)
    forward = np.where((ids <= midpoint)[None, :], np.cos(angles), np.sin(angles))
    single = (frequency == 0) | (ids == midpoint)
    inverse = forward.T * (np.where(single, 1.0, 2.0) / points)[:, None]
    mirror = np.zeros((points, points))
    mirror[frequency, ids] += 0.5
    mirror[(points - frequency) % points, ids] += 0.5
    return tuple(jnp.asarray(t.astype(np.float32)).astype(jnp.bfloat16) for t in (forward, inverse, mirror))


def halves(value):
    high = value.astype(jnp.bfloat16)
    return high, (value - high.astype(jnp.float32)).astype(jnp.bfloat16)


def dot32(a, b, contract=((1,), (0,))):
    return lax.dot_general(a, b, (contract, ((), ())), preferred_element_type=jnp.float32)


def dot_exact(a, b, contract=((1,), (0,))):
    return lax.dot_general(
        a, b, (contract, ((), ())), precision=HIGHEST, preferred_element_type=jnp.float32
    )


def response_kernel(coulomb_ref, forward_ref, inverse_ref, mirror_ref, out_ref):
    points = coulomb_ref.shape[1]
    multiplier = dot_exact(coulomb_ref[...], mirror_ref[...].astype(jnp.float32))
    forward = forward_ref[...].astype(jnp.float32)
    inverse = inverse_ref[...]
    for line in range(coulomb_ref.shape[0]):
        high, low = halves(forward * multiplier[line : line + 1, :])
        out_ref[line, :, :points] = dot32(high, inverse) + dot32(low, inverse)
        out_ref[line, :, points:] = jnp.zeros((points, out_ref.shape[2] - points), jnp.float32)


def image_kernel(occupied_ref, *refs):
    blocks, (response_ref, wide_ref, narrow_ref, overlap_ref, rows, images) = refs[:-6], refs[-6:]
    members, lines, points = blocks[0].shape
    size = members * lines
    tiles = rows.shape[0]
    spans = [(t, t * LANES, min(LANES, points - t * LANES)) for t in range(tiles)]
    position = lax.axis_index("band")
    total = lax.axis_size("band")
    member_ids = lax.broadcasted_iota(jnp.int32, (members, LANES), 0)
    rows[tiles - 1] = jnp.zeros(rows.shape[1:], jnp.float32)
    masks = []
    for place, block in enumerate(blocks):
        flat = block[...].reshape(size, points).astype(jnp.float32)
        for tile, start, width in spans:
            rows[tile, place * size : (place + 1) * size, :width] = flat[:, start : start + width]
        offset = 0 if place == 0 else OFFSETS[place - 1]
        filled = occupied_ref[lax.rem(position + (offset + total), total)]
        masks.append((member_ids < filled).astype(jnp.float32))
    mask = jnp.concatenate(masks, axis=0)
    overlap = jnp.zeros((members, members), jnp.float32)
    for line in range(lines):
        picked = [
            rows[tile, pl.ds(line, len(blocks) * members, stride=lines), :]
            for tile in range(tiles)
        ]
        masked = jnp.concatenate([(p * mask).astype(jnp.bfloat16) for p in picked], axis=1)
        window = jnp.concatenate([p.astype(jnp.bfloat16) for p in picked], axis=1)
        native = window[:members]
        gram = dot32(masked[:, :points], window, ((0,), (0,)))
        high, low = halves(gram * response_ref[line])
        image = dot32(native[:, :points], high) + dot32(native[:, :points], low)
        for tile in range(tiles):
            images[tile, pl.ds(line, members, stride=lines), :] = image[
                :, tile * LANES : (tile + 1) * LANES
            ]
        high, low = halves(image)
        across = ((1,), (1,))
        overlap = overlap + (dot32(native, high, across) + dot32(native, low, across))
    overlap_ref[...] = overlap
    for tile, start, width in spans:
        piece = images[tile].reshape(members, lines, LANES)[:, :, :width]
        wide_ref[:, :, start : start + width] = piece
        narrow_ref[:, :, start : start + width] = piece.astype(jnp.bfloat16)


def factor_kernel(cells, owners_ref, *refs):
    parts, (overlap_ref, weights_ref) = refs[:-2], refs[-2:]
    members = owners_ref.shape[0]
    sums = [part[...] for part in parts]
    while len(sums) > 1:
        sums = [a + b for a, b in zip(sums[::2], sums[1::2])]
    overlap = sums[0] * (1.0 / cells)
    overlap_ref[...] = overlap
    square = (members, members)
    row_ids = lax.broadcasted_iota(jnp.int32, square, 0)
    col_ids = lax.broadcasted_iota(jnp.int32, square, 1)
    identity = (row_ids == col_ids).astype(jnp.float32)
    upper = 0.5 * (overlap + dot_exact(overlap, identity, ((0,), (0,))))
    lower = identity
    for k in range(members):
        column = jnp.broadcast_to(upper[:, k : k + 1], square)
        pivot = jnp.broadcast_to(column[k : k + 1, :], square)
        scale = jnp.where(row_ids > k, column / pivot, 0.0)
        upper = upper - scale * upper[k : k + 1, :]
        lower = lower - scale * lower[k : k + 1, :]
    diagonal = jnp.sum(upper * identity, axis=1, keepdims=True)
    inverse = lower / jnp.sqrt(diagonal)
    group = lax.axis_index("grid") * lax.axis_size("ham") + lax.axis_index("ham")
    mine = (owners_ref[...] == group).astype(jnp.float32)
    before = (col_ids < row_ids).astype(jnp.float32)
    ranking = dot_exact(before, jnp.broadcast_to(mine, (members, CAP)))
    slots = lax.broadcasted_iota(jnp.int32, (members, CAP), 1).astype(jnp.float32)
    placement = jnp.where(ranking == slots, 1.0, 0.0) * mine
    chosen = dot_exact(placement, inverse, ((0,), (0,)))
    for k in range(members):
        weights_ref[k * CAP : (k + 1) * CAP, :] = jnp.broadcast_to(
            chosen[:, k : k + 1], (CAP, weights_ref.shape[1])
        )


def route_kernel(weights_ref, *refs):
    parts, out_ref = refs[:-1], refs[-1]
    members, lines, _ = parts[0].shape
    group = lax.axis_index("grid") * lax.axis_size("ham") + lax.axis_index("ham")
    for flip, part in enumerate(parts):
        start = pl.multiple_of((group ^ flip) * lines, lines)
        sums = [None] * CAP
        for k in range(members):
            image = part[k].astype(jnp.float32)
            for slot in range(CAP):
                row = k * CAP + slot
                term = weights_ref[row : row + 1, :] * image
                sums[slot] = term if k == 0 else sums[slot] + term
        for slot in range(CAP):
            out_ref[slot, pl.ds(start, lines), :] = sums[slot].astype(jnp.bfloat16)


OFFSETS = tuple(o for d in range(1, REACH + 1) for o in (d, -d))


def call(kernel, name, shapes, flops, moved, scratch=(), scalars=0, operands=0):
    vmem = pl.BlockSpec(memory_space=pltpu.VMEM)
    smem = pl.BlockSpec(memory_space=pltpu.SMEM)
    return pl.pallas_call(
        kernel,
        name=name,
        out_shape=shapes,
        in_specs=[smem] * scalars + [vmem] * operands,
        out_specs=[vmem] * len(shapes),
        scratch_shapes=list(scratch),
        compiler_params=pltpu.CompilerParams(vmem_limit_bytes=VMEM_LIMIT),
        cost_estimate=pl.CostEstimate(flops=flops, bytes_accessed=moved, transcendentals=0),
    )


def local(orbitals, coulomb, occupied, owners):
    members, lines, points = orbitals.shape
    groups = lax.axis_size("grid") * lax.axis_size("ham")
    tiles = -(-points // LANES)
    f32, bf16 = jnp.float32, jnp.bfloat16
    shape = jax.ShapeDtypeStruct
    guests = [shifted(orbitals, "band", -offset) for offset in OFFSETS]
    forward, inverse, mirror = spectral_tables(points)
    (response,) = call(
        response_kernel,
        "response",
        [shape((lines, points, tiles * LANES), f32)],
        4 * lines * points**3,
        4 * lines * points**2,
        operands=4,
    )(coulomb, forward, inverse, mirror)
    blocks = len(guests) + 1
    wide, narrow, overlap = call(
        image_kernel,
        "image",
        [
            shape((members, lines, points), f32),
            shape((members, lines, points), bf16),
            shape((members, members), f32),
        ],
        2 * lines * points**2 * members * (blocks + 2),
        4 * lines * points**2,
        scratch=[
            pltpu.VMEM((tiles, blocks * members * lines, LANES), f32),
            pltpu.VMEM((tiles, members * lines, LANES), f32),
        ],
        scalars=1,
        operands=blocks + 1,
    )(occupied, orbitals, *guests, response)
    flips = range(1, groups)
    overlaps = [overlap] + [swapped(overlap, flip) for flip in flips]
    near = lax.axis_size("ham")
    images = [wide] + [swapped(wide if flip < near else narrow, flip) for flip in flips]
    cells = lines * groups * points

    def factor(*refs):
        factor_kernel(cells, *refs)

    intersection, weights = call(
        factor,
        "factor",
        [shape((members, members), f32), shape((members * CAP, points), f32)],
        members**3,
        members**2 * 4,
        operands=1 + groups,
    )(owners, *overlaps)
    (routed,) = call(
        route_kernel,
        "route",
        [shape((CAP, groups * lines, points), bf16)],
        2 * CAP * members * groups * lines * points,
        6 * members * groups * lines * points,
        operands=1 + groups,
    )(weights, *images)
    return routed[None, None], intersection[None]


def solution(mesh):
    in_specs = (P("band", ("grid", "ham"), None), P(("grid", "ham"), None), P(), P("band", None))
    out_specs = (P("band", ("grid", "ham"), None, None, None), P("band", None, None))
    return jax.shard_map(local, mesh=mesh, in_specs=in_specs, out_specs=out_specs, check_vma=False)
```

```python
import math

import jax
import jax.numpy as jnp
import numpy as np
from jax import lax
from jax.experimental import pallas as pl
from jax.experimental.pallas import tpu as pltpu
from jax.sharding import PartitionSpec as P

CAP = 8
LANES = 128
HIGHEST = lax.Precision.HIGHEST
VMEM_LIMIT = 48 * 1024 * 1024
NT = ((1,), (1,))
F32, BF16 = jnp.float32, jnp.bfloat16


def partners(block, count):
    even, low = block % 2 == 0, block % 4 < 2
    choose = jnp.where if isinstance(block, jax.Array) else (lambda c, a, b: a if c else b)
    steps = (choose(low, -2, 2), choose(even, -1, 1), choose(even, 1, -1), choose(low, 2, -2))
    return [(block + step + count) % count for step in steps]


def exchanged(value):
    count = lax.axis_size("band")
    assert count % 4 == 0
    tables = [partners(block, count) for block in range(count)]
    return [
        lax.ppermute(value, "band", [(block, row[turn]) for block, row in enumerate(tables)])
        for turn in range(4)
    ]


def swapped(value, flip):
    count = lax.axis_size("grid") * lax.axis_size("ham")
    return lax.ppermute(value, ("grid", "ham"), [(group, group ^ flip) for group in range(count)])


def spectral_tables(points):
    midpoint = points // 2
    ids = np.arange(points)
    frequency = np.where(ids <= midpoint, ids, ids - midpoint)
    angles = (ids[:, None] * frequency[None, :] % points) * (2.0 * math.pi / points)
    forward = np.where((ids <= midpoint)[None, :], np.cos(angles), np.sin(angles))
    single = (frequency == 0) | (ids == midpoint)
    inverse = forward.T * (np.where(single, 1.0, 2.0) / points)[:, None]
    mirror = np.zeros((points, points))
    mirror[frequency, ids] += 0.5
    mirror[(points - frequency) % points, ids] += 0.5
    return jnp.asarray(np.stack([forward.T, inverse.T, mirror]).astype(np.float32)).astype(BF16)


def halves(value):
    high = value.astype(BF16)
    return high, (value - high.astype(F32)).astype(BF16)


def dot32(a, b, contract=((1,), (0,))):
    return lax.dot_general(a, b, (contract, ((), ())), preferred_element_type=F32)


def dot_exact(a, b, contract=((1,), (0,))):
    return lax.dot_general(
        a, b, (contract, ((), ())), precision=HIGHEST, preferred_element_type=F32
    )


def ids(shape, axis):
    return lax.broadcasted_iota(jnp.int32, shape, axis)


def rows_of(block, pack, span):
    members, _, points = block.shape
    part = block[:, pack * span : (pack + 1) * span, :]
    return part.reshape(members * span, points)


def pack_kernel(orbitals_ref, out_ref):
    span = LANES // orbitals_ref.shape[0]
    block = orbitals_ref[...].astype(F32)
    for pack in range(out_ref.shape[0]):
        out_ref[pack] = rows_of(block, pack, span).T.astype(BF16)


def response_kernel(coulomb_ref, tables_ref, out_ref):
    points = coulomb_ref.shape[1]
    multiplier = dot_exact(coulomb_ref[...], tables_ref[2].astype(F32))
    forward = tables_ref[0]
    inverse = tables_ref[1].astype(F32)
    pad = jnp.zeros((points, out_ref.shape[2] - points), F32)
    for line in range(coulomb_ref.shape[0]):
        high, low = halves(inverse * multiplier[line : line + 1, :])
        out_ref[line, :, :points] = dot32(high, forward) + dot32(low, forward)
        out_ref[line, :, points:] = pad


def image_kernel(occupied_ref, orbitals_ref, *refs):
    blocks, (response_ref, wide_ref, narrow_ref, overlap_ref, window, masked) = refs[:-6], refs[-6:]
    members, lines, points = orbitals_ref.shape
    packs, padded, width = window.shape
    span = LANES // members
    total = lax.axis_size("band")
    position = lax.axis_index("band")
    places = [position] + partners(position, total)
    lane = ids((1, LANES), 1)
    filled = [(lane // span < occupied_ref[place]).astype(F32) for place in places]
    for place, block in enumerate(blocks):
        window[:, :points, place * LANES : (place + 1) * LANES] = block[...]
    window[:, points:, :] = jnp.zeros((packs, padded - points, width), BF16)
    natives = orbitals_ref[...].astype(F32)
    square = (LANES, LANES)
    same_line = ids(square, 0) % span == ids(square, 1) % span
    cross = jnp.zeros(square, F32)
    for pack in range(packs):
        whole = window[pack, :points, :]
        for line in range(span):
            chosen = (lane % span == line).astype(F32)
            mask = jnp.concatenate([f * chosen for f in filled], axis=1).astype(BF16)
            masked[line * points : (line + 1) * points, :] = whole * mask
        gram = dot32(masked[...], window[pack], NT)
        response = response_ref[pack * span : (pack + 1) * span].reshape(span * points, padded)
        high, low = halves(gram * response)
        native = window[pack, :, :LANES]
        fields = dot32(high, native) + dot32(low, native)
        image = jnp.zeros((points, LANES), F32)
        for line in range(span):
            field = fields[line * points : (line + 1) * points, :]
            image = jnp.where(lane % span == line, field, image)
        wide_ref[pack] = image
        narrow_ref[pack] = image.astype(BF16)
        high, low = halves(image)
        rows = rows_of(natives, pack, span).astype(BF16)
        cross = cross + (dot32(rows, high) + dot32(rows, low))
    cross = jnp.where(same_line, cross, 0.0).reshape(members, span, LANES).sum(axis=1)
    gather = (ids((LANES, members), 0) // span == ids((LANES, members), 1)).astype(F32)
    overlap_ref[...] = dot_exact(cross, gather)


def factor_kernel(cells, owners_ref, *refs):
    parts, (overlap_ref, weights_ref) = refs[:-2], refs[-2:]
    members = owners_ref.shape[0]
    span = LANES // members
    sums = [part[...] for part in parts]
    while len(sums) > 1:
        sums = [a + b for a, b in zip(sums[::2], sums[1::2])]
    overlap = sums[0] * (1.0 / cells)
    overlap_ref[...] = overlap
    square = (members, members)
    row_ids, col_ids = ids(square, 0), ids(square, 1)
    identity = (row_ids == col_ids).astype(F32)
    upper = 0.5 * (overlap + dot_exact(overlap, identity, ((0,), (0,))))
    lower = identity
    for k in range(members):
        column = jnp.broadcast_to(upper[:, k : k + 1], square)
        pivot = jnp.broadcast_to(column[k : k + 1, :], square)
        scale = jnp.where(row_ids > k, column / pivot, 0.0)
        upper = upper - scale * upper[k : k + 1, :]
        lower = lower - scale * lower[k : k + 1, :]
    diagonal = jnp.sum(upper * identity, axis=1, keepdims=True)
    inverse = lower / jnp.sqrt(diagonal)
    group = lax.axis_index("grid") * lax.axis_size("ham") + lax.axis_index("ham")
    mine = (owners_ref[...] == group).astype(F32)
    before = (col_ids < row_ids).astype(F32)
    ranking = dot_exact(before, jnp.broadcast_to(mine, (members, CAP)))
    slots = ids((members, CAP), 1).astype(F32)
    placement = jnp.where(ranking == slots, 1.0, 0.0) * mine
    chosen = dot_exact(placement, inverse, ((0,), (0,)))
    rows = CAP * span
    spread = (ids((members, LANES), 0) == ids((members, LANES), 1) // span).astype(F32)
    repeat = (ids((rows, CAP), 0) // span == ids((rows, CAP), 1)).astype(F32)
    weights = dot_exact(repeat, dot_exact(chosen, spread))
    same_line = ids((rows, LANES), 0) % span == ids((rows, LANES), 1) % span
    high, low = halves(jnp.where(same_line, weights, 0.0))
    weights_ref[:rows, :] = high
    weights_ref[rows:, :] = low


def route_kernel(weights_ref, *refs):
    parts, out_ref = refs[:-1], refs[-1]
    packs, points, _ = parts[0].shape
    weights = weights_ref[...]
    rows = weights.shape[0] // 2
    span = rows // CAP
    lines = packs * span
    group = lax.axis_index("grid") * lax.axis_size("ham") + lax.axis_index("ham")
    for flip, part in enumerate(parts):
        start = pl.multiple_of((group ^ flip) * lines, lines)
        sums = []
        for pack in range(packs):
            if part.dtype == BF16:
                both = dot32(weights, part[pack], NT)
                result = both[:rows] + both[rows:]
            else:
                high, low = halves(part[pack])
                both = dot32(weights, high, NT)
                result = both[:rows] + (both[rows:] + dot32(weights[:rows], low, NT))
            sums.append(result.reshape(CAP, span, points))
        out_ref[:, pl.ds(start, lines), :] = jnp.concatenate(sums, axis=1).astype(BF16)


def call(kernel, name, shapes, flops, moved, scratch=(), scalars=0, operands=0):
    vmem = pl.BlockSpec(memory_space=pltpu.VMEM)
    smem = pl.BlockSpec(memory_space=pltpu.SMEM)
    return pl.pallas_call(
        kernel,
        name=name,
        out_shape=shapes,
        in_specs=[smem] * scalars + [vmem] * operands,
        out_specs=[vmem] * len(shapes),
        scratch_shapes=list(scratch),
        compiler_params=pltpu.CompilerParams(vmem_limit_bytes=VMEM_LIMIT),
        cost_estimate=pl.CostEstimate(flops=flops, bytes_accessed=moved, transcendentals=0),
    )


def local(orbitals, coulomb, occupied, owners):
    members, lines, points = orbitals.shape
    grids, near = lax.axis_size("grid"), lax.axis_size("ham")
    groups = grids * near
    padded = -(-points // LANES) * LANES
    span = LANES // members
    packs = lines // span
    shape = jax.ShapeDtypeStruct
    (packed,) = call(
        pack_kernel,
        "pack",
        [shape((packs, points, LANES), BF16)],
        orbitals.size,
        4 * orbitals.size,
        operands=1,
    )(orbitals)
    guests = exchanged(packed)
    (response,) = call(
        response_kernel,
        "response",
        [shape((lines, points, padded), F32)],
        4 * lines * points**3,
        4 * lines * points**2,
        operands=2,
    )(coulomb, spectral_tables(points))
    blocks = len(guests) + 1
    width = blocks * LANES
    wide, narrow, overlap = call(
        image_kernel,
        "image",
        [
            shape((packs, points, LANES), F32),
            shape((packs, points, LANES), BF16),
            shape((members, members), F32),
        ],
        2 * lines * points * padded * (width + 2 * LANES),
        4 * lines * points**2,
        scratch=[
            pltpu.VMEM((packs, padded, width), BF16),
            pltpu.VMEM((span * points, width), BF16),
        ],
        scalars=1,
        operands=blocks + 2,
    )(occupied, orbitals, packed, *guests, response)

    def gathered(value, far):
        held = [value] + [swapped(value, flip) for flip in range(1, near)]
        for grid in range(1, grids):
            across = swapped(far, grid * near)
            held += [across] + [swapped(across, flip) for flip in range(1, near)]
        return held

    overlaps = gathered(overlap, overlap)
    images = gathered(wide, narrow)
    cells = lines * groups * points

    def factor(*refs):
        factor_kernel(cells, *refs)

    intersection, weights = call(
        factor,
        "factor",
        [shape((members, members), F32), shape((2 * CAP * span, LANES), BF16)],
        members**3,
        members**2 * 4,
        operands=1 + groups,
    )(owners, *overlaps)
    (routed,) = call(
        route_kernel,
        "route",
        [shape((CAP, groups * lines, points), BF16)],
        2 * CAP * members * groups * lines * points,
        6 * members * groups * lines * points,
        operands=1 + groups,
    )(weights, *images)
    return routed[None, None], intersection[None]


def solution(mesh):
    in_specs = (P("band", ("grid", "ham"), None), P(("grid", "ham"), None), P(), P("band", None))
    out_specs = (P("band", ("grid", "ham"), None, None, None), P("band", None, None))
    return jax.shard_map(local, mesh=mesh, in_specs=in_specs, out_specs=out_specs, check_vma=False)
```

```python
import math

import jax
import jax.numpy as jnp
import numpy as np
from jax import lax
from jax.experimental import pallas as pl
from jax.experimental.pallas import tpu as pltpu
from jax.sharding import PartitionSpec as P

CAP = 8
LANES = 128
HIGHEST = lax.Precision.HIGHEST
VMEM_LIMIT = 48 * 1024 * 1024
FACTOR_COST = 3_000_000_000
NT = ((1,), (1,))
F32, BF16 = jnp.float32, jnp.bfloat16


def partners(block, count):
    even, low = block % 2 == 0, block % 4 < 2
    choose = jnp.where if isinstance(block, jax.Array) else (lambda c, a, b: a if c else b)
    steps = (choose(low, -2, 2), choose(even, -1, 1), choose(even, 1, -1), choose(low, 2, -2))
    return [(block + step + count) % count for step in steps]


def exchanged(value):
    count = lax.axis_size("band")
    assert count % 4 == 0
    tables = [partners(block, count) for block in range(count)]
    return [
        lax.ppermute(value, "band", [(block, row[turn]) for block, row in enumerate(tables)])
        for turn in range(4)
    ]


def swapped(value, flip):
    count = lax.axis_size("grid") * lax.axis_size("ham")
    return lax.ppermute(value, ("grid", "ham"), [(group, group ^ flip) for group in range(count)])


def spectral_tables(points):
    midpoint = points // 2
    ids = np.arange(points)
    frequency = np.where(ids <= midpoint, ids, ids - midpoint)
    angles = (ids[:, None] * frequency[None, :] % points) * (2.0 * math.pi / points)
    forward = np.where((ids <= midpoint)[None, :], np.cos(angles), np.sin(angles))
    single = (frequency == 0) | (ids == midpoint)
    inverse = forward.T * (np.where(single, 1.0, 2.0) / points)[:, None]
    mirror = np.zeros((points, points))
    mirror[frequency, ids] += 0.5
    mirror[(points - frequency) % points, ids] += 0.5
    return jnp.asarray(np.stack([forward.T, inverse.T, mirror]).astype(np.float32)).astype(BF16)


def halves(value):
    high = value.astype(BF16)
    return high, (value - high.astype(F32)).astype(BF16)


def dot32(a, b, contract=((1,), (0,))):
    return lax.dot_general(a, b, (contract, ((), ())), preferred_element_type=F32)


def dot_exact(a, b, contract=((1,), (0,))):
    return lax.dot_general(
        a, b, (contract, ((), ())), precision=HIGHEST, preferred_element_type=F32
    )


def ids(shape, axis):
    return lax.broadcasted_iota(jnp.int32, shape, axis)


def lane_member(lane, members):
    return lane % members


def lane_quarter(lane, turn):
    return (lane // (LANES // 4)) ^ turn


def lane_line(lane, turn, members):
    per = LANES // 4 // members
    return lane_quarter(lane, turn) * per + lane % (LANES // 4) // members


def own_turn():
    return lax.axis_index("band") % 4


def rows_of(block, pack, span):
    members, _, points = block.shape
    part = block[:, pack * span : (pack + 1) * span, :]
    return part.reshape(members * span, points)


def pack_kernel(orbitals_ref, out_ref):
    members = orbitals_ref.shape[0]
    span = LANES // members
    block = orbitals_ref[...].astype(F32)
    row, lane = ids((LANES, LANES), 0), ids((LANES, LANES), 1)
    source = lane_member(lane, members) * span + lane_line(lane, own_turn(), members)
    order = (row == source).astype(BF16)
    for pack in range(out_ref.shape[0]):
        rows = rows_of(block, pack, span).T.astype(BF16)
        out_ref[pack] = dot32(rows, order).astype(BF16)


def response_kernel(coulomb_ref, tables_ref, out_ref):
    points = coulomb_ref.shape[1]
    multiplier = dot_exact(coulomb_ref[...], tables_ref[2].astype(F32))
    forward = tables_ref[0]
    inverse = tables_ref[1].astype(F32)
    pad = jnp.zeros((points, out_ref.shape[2] - points), F32)
    for line in range(coulomb_ref.shape[0]):
        high, low = halves(inverse * multiplier[line : line + 1, :])
        out_ref[line, :, :points] = dot32(high, forward) + dot32(low, forward)
        out_ref[line, :, points:] = pad


def image_kernel(occupied_ref, orbitals_ref, *refs):
    blocks, (response_ref, wide_ref, narrow_ref, overlap_ref) = refs[:-4], refs[-4:]
    members, lines, points = orbitals_ref.shape
    packs = blocks[0].shape[0]
    padded = response_ref.shape[2]
    span = LANES // members
    per = span // 4
    total = lax.axis_size("band")
    position = lax.axis_index("band")
    places = [position] + partners(position, total)
    turns = [place % 4 for place in places]
    lane = ids((1, LANES), 1)
    own_line = lane_line(lane, turns[0], members)
    filled = [lane_member(lane, members) < occupied_ref[place] for place in places]
    quarters = [lane_quarter(lane, turn) for turn in turns]
    step = lane % (LANES // 4) // members
    apart, merged = 1, (0, 2, 3, 4)
    natives = orbitals_ref[...].astype(F32)
    square = (LANES, LANES)
    row_line = ids(square, 0) % span
    same_line = row_line == lane_line(ids(square, 1), turns[0], members)
    blank = jnp.zeros((padded - points, 2 * LANES), BF16)
    cross = jnp.zeros(square, F32)
    for pack in range(packs):
        tiles = [block[pack] for block in blocks]
        native = jnp.concatenate([tiles[0], blank[:, :LANES]], axis=0)
        image = jnp.zeros((points, LANES), F32)
        for quarter in range(4):
            here = [(q == quarter) for q in quarters]
            together = sum(tiles[m] * here[m].astype(F32).astype(BF16) for m in merged)
            window = jnp.concatenate([together, tiles[apart]], axis=1)
            occupied = sum((here[m] & filled[m]).astype(F32) for m in merged)
            beside = (here[apart] & filled[apart]).astype(F32)
            both = jnp.concatenate([occupied, beside], axis=1)
            steps = jnp.concatenate([step, step], axis=1)
            masked = jnp.concatenate(
                [window * jnp.where(steps == k, both, 0.0).astype(BF16) for k in range(per)], axis=0
            )
            gram = dot32(masked, jnp.concatenate([window, blank], axis=0), NT)
            first = pack * span + quarter * per
            response = response_ref[first : first + per].reshape(per * points, padded)
            high, low = halves(gram * response)
            fields = dot32(jnp.concatenate([high, low], axis=0), native)
            for k in range(per):
                a, b = k * points, (per + k) * points
                field = fields[a : a + points] + fields[b : b + points]
                image = jnp.where(own_line == quarter * per + k, field, image)
        wide_ref[pack] = image
        narrow_ref[pack] = image.astype(BF16)
        rows = rows_of(natives, pack, span).astype(BF16)
        product = dot32(rows, jnp.concatenate(halves(image), axis=1))
        cross = cross + (product[:, :LANES] + product[:, LANES:])
    cross = jnp.where(same_line, cross, 0.0).reshape(members, span, LANES).sum(axis=1)
    gather = lane_member(ids((LANES, members), 0), members) == ids((LANES, members), 1)
    overlap_ref[...] = dot_exact(cross, gather.astype(F32))


def factor_kernel(cells, owners_ref, *refs):
    parts, (overlap_ref, weights_ref) = refs[:-2], refs[-2:]
    members = owners_ref.shape[0]
    span = LANES // members
    turn = own_turn()
    sums = [part[...] for part in parts]
    while len(sums) > 1:
        sums = [a + b for a, b in zip(sums[::2], sums[1::2])]
    overlap = sums[0] * (1.0 / cells)
    overlap_ref[...] = overlap
    rows = CAP * span
    square = (members, members)
    group = lax.axis_index("grid") * lax.axis_size("ham") + lax.axis_index("ham")
    mine = (owners_ref[...] == group).astype(F32)
    eye = (ids(square, 0) == ids(square, 1)).astype(F32)
    mine_row = jnp.sum(mine * eye, axis=0, keepdims=True)
    before = (ids(square, 0) < ids(square, 1)).astype(F32)
    ranking = jnp.sum(mine * before, axis=0, keepdims=True)
    slot = (ids((rows, members), 0) // span).astype(F32)
    placed = (jnp.where(slot == ranking, 1.0, 0.0) * mine_row).astype(BF16)
    wide = (members, LANES)
    row = ids(wide, 0)
    upper = 0.5 * (overlap + dot_exact(overlap, eye, ((0,), (0,))))
    lower = (row == lane_member(ids(wide, 1), members)).astype(F32)
    for k in range(0, members, 2):
        first = jnp.broadcast_to(upper[:, k : k + 1], wide)
        second = jnp.broadcast_to(upper[:, k + 1 : k + 2], wide)
        a, b, c = first[k : k + 1], first[k + 1 : k + 2], second[k + 1 : k + 2]
        scale = 1.0 / (a * c - b * b)
        below = row > k + 1
        one = jnp.where(below, (first * c - second * b) * scale, 0.0)
        two = jnp.where(below, (second * a - first * b) * scale, 0.0)
        lower = lower - (one * lower[k : k + 1] + two * lower[k + 1 : k + 2])
        one, two = one[:, :members], two[:, :members]
        upper = upper - (one * upper[k : k + 1] + two * upper[k + 1 : k + 2])
    diagonal = jnp.sum(upper * eye, axis=1, keepdims=True)
    beside = (ids(square, 0) == ids(square, 1) + 1) & (ids(square, 0) % 2 == 1)
    share = jnp.sum(jnp.where(beside, upper, 0.0), axis=1, keepdims=True)
    previous = jnp.concatenate([diagonal[:1], diagonal[:-1]], axis=0)
    ratio = share / previous
    above = jnp.concatenate([lower[:1], lower[:-1]], axis=0)
    inverse = (lower - ratio * above) / jnp.sqrt(diagonal - ratio * share)
    high, low = halves(inverse)
    same_line = ids((rows, LANES), 0) % span == lane_line(ids((rows, LANES), 1), turn, members)
    for place, half in ((0, high), (rows, low)):
        chosen = jnp.where(same_line, dot32(placed, half), 0.0)
        weights_ref[place : place + rows, :] = chosen.astype(BF16)


def route_kernel(weights_ref, *refs):
    parts, out_ref = refs[:-1], refs[-1]
    packs, points, _ = parts[0].shape
    weights = weights_ref[...]
    rows = weights.shape[0] // 2
    span = rows // CAP
    lines = packs * span
    group = lax.axis_index("grid") * lax.axis_size("ham") + lax.axis_index("ham")
    for flip, part in enumerate(parts):
        start = pl.multiple_of((group ^ flip) * lines, lines)
        sums = []
        for pack in range(packs):
            if part.dtype == BF16:
                both = dot32(weights, part[pack], NT)
                result = both[:rows] + both[rows:]
            else:
                high, low = halves(part[pack])
                both = dot32(weights, high, NT)
                result = both[:rows] + (both[rows:] + dot32(weights[:rows], low, NT))
            sums.append(result.reshape(CAP, span, points))
        out_ref[:, pl.ds(start, lines), :] = jnp.concatenate(sums, axis=1).astype(BF16)


def call(kernel, name, shapes, flops, moved, scratch=(), scalars=0, operands=0):
    vmem = pl.BlockSpec(memory_space=pltpu.VMEM)
    smem = pl.BlockSpec(memory_space=pltpu.SMEM)
    return pl.pallas_call(
        kernel,
        name=name,
        out_shape=shapes,
        in_specs=[smem] * scalars + [vmem] * operands,
        out_specs=[vmem] * len(shapes),
        scratch_shapes=list(scratch),
        compiler_params=pltpu.CompilerParams(vmem_limit_bytes=VMEM_LIMIT),
        cost_estimate=pl.CostEstimate(flops=flops, bytes_accessed=moved, transcendentals=0),
    )


def local(orbitals, coulomb, occupied, owners):
    members, lines, points = orbitals.shape
    grids, near = lax.axis_size("grid"), lax.axis_size("ham")
    groups = grids * near
    padded = -(-points // LANES) * LANES
    span = LANES // members
    packs = lines // span
    shape = jax.ShapeDtypeStruct
    (packed,) = call(
        pack_kernel,
        "pack",
        [shape((packs, points, LANES), BF16)],
        orbitals.size,
        4 * orbitals.size,
        operands=1,
    )(orbitals)
    guests = exchanged(packed)
    (response,) = call(
        response_kernel,
        "response",
        [shape((lines, points, padded), F32)],
        4 * lines * points**3,
        4 * lines * points**2,
        operands=2,
    )(coulomb, spectral_tables(points))
    blocks = len(guests) + 1
    wide, narrow, overlap = call(
        image_kernel,
        "image",
        [
            shape((packs, points, LANES), F32),
            shape((packs, points, LANES), BF16),
            shape((members, members), F32),
        ],
        2 * lines * points * padded * (4 * LANES),
        4 * lines * points**2,
        scalars=1,
        operands=blocks + 2,
    )(occupied, orbitals, packed, *guests, response)

    overlaps = [overlap] + [swapped(overlap, flip) for flip in range(1, groups)]
    images = [wide] + [swapped(wide, flip) for flip in range(1, near)]
    for grid in range(1, grids):
        across = swapped(narrow, grid * near)
        images += [across] + [swapped(across, flip) for flip in range(1, near)]
    cells = lines * groups * points

    def factor(*refs):
        factor_kernel(cells, *refs)

    intersection, weights = call(
        factor,
        "factor",
        [shape((members, members), F32), shape((2 * CAP * span, LANES), BF16)],
        FACTOR_COST,
        members**2 * 4,
        operands=1 + groups,
    )(owners, *overlaps)
    (routed,) = call(
        route_kernel,
        "route",
        [shape((CAP, groups * lines, points), BF16)],
        2 * CAP * members * groups * lines * points,
        6 * members * groups * lines * points,
        operands=1 + groups,
    )(weights, *images)
    return routed[None, None], intersection[None]


def solution(mesh):
    in_specs = (P("band", ("grid", "ham"), None), P(("grid", "ham"), None), P(), P("band", None))
    out_specs = (P("band", ("grid", "ham"), None, None, None), P("band", None, None))
    return jax.shard_map(local, mesh=mesh, in_specs=in_specs, out_specs=out_specs, check_vma=False)
```

```python
import functools
import math

import jax
import jax.numpy as jnp
import numpy as np
from jax import lax
from jax.experimental import pallas as pl
from jax.experimental.pallas import tpu as pltpu
from jax.sharding import PartitionSpec as P

CAP = 8
LANES = 128
HIGHEST = lax.Precision.HIGHEST
VMEM_LIMIT = 48 * 1024 * 1024
FACTOR_COST = 3_000_000_000
NT = ((1,), (1,))
F32, BF16 = jnp.float32, jnp.bfloat16


def sources(block, count):
    odd = block % 2
    steps = (-2, 2 * odd - 1, 1 - 2 * odd, 2)
    return [(block + step + count) % count for step in steps]


def exchanged(value):
    count = lax.axis_size("band")
    assert count % 4 == 0
    tables = [sources(block, count) for block in range(count)]
    return [
        lax.ppermute(value, "band", [(row[turn], block) for block, row in enumerate(tables)])
        for turn in range(4)
    ]


def swapped(value, flip):
    count = lax.axis_size("grid") * lax.axis_size("ham")
    return lax.ppermute(value, ("grid", "ham"), [(group, group ^ flip) for group in range(count)])


def spectral_tables(points):
    midpoint = points // 2
    ids = np.arange(points)
    frequency = np.where(ids <= midpoint, ids, ids - midpoint)
    angles = (ids[:, None] * frequency[None, :] % points) * (2.0 * math.pi / points)
    forward = np.where((ids <= midpoint)[None, :], np.cos(angles), np.sin(angles))
    single = (frequency == 0) | (ids == midpoint)
    inverse = forward.T * (np.where(single, 1.0, 2.0) / points)[:, None]
    mirror = np.zeros((points, points))
    mirror[frequency, ids] += 0.5
    mirror[(points - frequency) % points, ids] += 0.5
    return jnp.asarray(np.stack([forward.T, inverse.T, mirror]).astype(np.float32)).astype(BF16)


def split(value):
    high = value.astype(BF16)
    return high, value - high.astype(F32)


def halves(value):
    high, rest = split(value)
    return high, rest.astype(BF16)


def dot32(a, b, contract=((1,), (0,))):
    return lax.dot_general(a, b, (contract, ((), ())), preferred_element_type=F32)


def dot_exact(a, b, contract=((1,), (0,))):
    return lax.dot_general(
        a, b, (contract, ((), ())), precision=HIGHEST, preferred_element_type=F32
    )


def ids(shape, axis):
    return lax.broadcasted_iota(jnp.int32, shape, axis)


def lane_member(lane, members):
    return lane % members


def lane_quarter(lane, turn):
    return (lane // (LANES // 4)) ^ turn


def lane_line(lane, turn, members):
    per = LANES // 4 // members
    return lane_quarter(lane, turn) * per + lane % (LANES // 4) // members


def own_turn():
    return lax.axis_index("band") % 4


def rows_of(block, pack, span):
    members, _, points = block.shape
    part = block[:, pack * span : (pack + 1) * span, :]
    return part.reshape(members * span, points)


def pack_kernel(orbitals_ref, out_ref):
    members = orbitals_ref.shape[0]
    span = LANES // members
    block = orbitals_ref[...].astype(F32)
    row, lane = ids((LANES, LANES), 0), ids((LANES, LANES), 1)
    source = lane_member(lane, members) * span + lane_line(lane, own_turn(), members)
    order = (row == source).astype(BF16)
    for pack in range(out_ref.shape[0]):
        rows = rows_of(block, pack, span).T.astype(BF16)
        out_ref[pack] = dot32(rows, order).astype(BF16)


def response_kernel(coulomb_ref, tables_ref, out_ref):
    points = coulomb_ref.shape[1]
    multiplier = dot_exact(coulomb_ref[...], tables_ref[2].astype(F32))
    forward = tables_ref[0]
    inverse = tables_ref[1].astype(F32)
    pad = jnp.zeros((points, out_ref.shape[2] - points), F32)
    for line in range(coulomb_ref.shape[0]):
        high, low = halves(inverse * multiplier[line : line + 1, :])
        out_ref[line, :, :points] = dot32(high, forward) + dot32(low, forward)
        out_ref[line, :, points:] = pad


def image_kernel(members, occupied_ref, *refs):
    blocks, (response_ref, wide_ref, narrow_ref) = refs[:-3], refs[-3:]
    packs, points, _ = blocks[0].shape
    padded = response_ref.shape[2]
    span = LANES // members
    per = span // 4
    total = lax.axis_size("band")
    position = lax.axis_index("band")
    places = [position] + sources(position, total)
    turns = [place % 4 for place in places]
    lane = ids((1, LANES), 1)
    own_line = lane_line(lane, turns[0], members)
    filled = [lane_member(lane, members) < occupied_ref[place] for place in places]
    quarters = [lane_quarter(lane, turn) for turn in turns]
    step = lane % (LANES // 4) // members
    apart, merged = 1, (0, 2, 3, 4)
    blank = jnp.zeros((padded - points, 2 * LANES), BF16)
    for pack in range(packs):
        tiles = [block[pack] for block in blocks]
        native = jnp.concatenate([tiles[0], blank[:, :LANES]], axis=0)
        image = jnp.zeros((points, LANES), F32)
        for quarter in range(4):
            here = [(q == quarter) for q in quarters]
            together = sum(tiles[m] * here[m].astype(F32).astype(BF16) for m in merged)
            window = jnp.concatenate([together, tiles[apart]], axis=1)
            occupied = sum((here[m] & filled[m]).astype(F32) for m in merged)
            beside = (here[apart] & filled[apart]).astype(F32)
            both = jnp.concatenate([occupied, beside], axis=1)
            steps = jnp.concatenate([step, step], axis=1)
            masked = jnp.concatenate(
                [window * jnp.where(steps == k, both, 0.0).astype(BF16) for k in range(per)], axis=0
            )
            gram = dot32(masked, jnp.concatenate([window, blank], axis=0), NT)
            first = pack * span + quarter * per
            response = response_ref[first : first + per].reshape(per * points, padded)
            high, low = halves(gram * response)
            fields = dot32(jnp.concatenate([high, low], axis=0), native)
            for k in range(per):
                a, b = k * points, (per + k) * points
                field = fields[a : a + points] + fields[b : b + points]
                image = jnp.where(own_line == quarter * per + k, field, image)
        wide_ref[pack] = image
        narrow_ref[pack] = image.astype(BF16)


def overlap_kernel(orbitals_ref, image_ref, out_ref):
    members, _, _ = orbitals_ref.shape
    span = LANES // members
    natives = orbitals_ref[...].astype(F32)
    square = (LANES, LANES)
    same_line = ids(square, 0) % span == lane_line(ids(square, 1), own_turn(), members)
    cross = jnp.zeros(square, F32)
    for pack in range(image_ref.shape[0]):
        rows = rows_of(natives, pack, span).astype(BF16)
        product = dot32(rows, jnp.concatenate(halves(image_ref[pack]), axis=1))
        cross = cross + (product[:, :LANES] + product[:, LANES:])
    out_ref[...] = jnp.where(same_line, cross, 0.0).reshape(members, span, LANES).sum(axis=1)


def factor_kernel(cells, owners_ref, *refs):
    parts, (overlap_ref, weights_ref) = refs[:-2], refs[-2:]
    members = owners_ref.shape[0]
    span = LANES // members
    turn = own_turn()
    sums = [part[...] for part in parts]
    while len(sums) > 1:
        sums = [a + b for a, b in zip(sums[::2], sums[1::2])]
    high, rest = split(sums[0])
    pieces = [high, *halves(rest)]
    across = (members, LANES)
    gather = (ids(across, 0) == lane_member(ids(across, 1), members)).astype(BF16)
    overlap = sum(dot32(piece, gather, NT) for piece in pieces) * (1.0 / cells)
    flipped = sum(dot32(gather, piece, NT) for piece in pieces) * (1.0 / cells)
    overlap_ref[...] = overlap
    rows = CAP * span
    square = (members, members)
    group = lax.axis_index("grid") * lax.axis_size("ham") + lax.axis_index("ham")
    mine = (owners_ref[...] == group).astype(F32)
    eye = (ids(square, 0) == ids(square, 1)).astype(F32)
    mine_row = jnp.sum(mine * eye, axis=0, keepdims=True)
    before = (ids(square, 0) < ids(square, 1)).astype(F32)
    ranking = jnp.sum(mine * before, axis=0, keepdims=True)
    slot = (ids((rows, members), 0) // span).astype(F32)
    placed = (jnp.where(slot == ranking, 1.0, 0.0) * mine_row).astype(BF16)
    wide = (members, LANES)
    row = ids(wide, 0)
    upper = 0.5 * (overlap + flipped)
    lower = (row == lane_member(ids(wide, 1), members)).astype(F32)
    for k in range(0, members, 2):
        first = jnp.broadcast_to(upper[:, k : k + 1], wide)
        second = jnp.broadcast_to(upper[:, k + 1 : k + 2], wide)
        a, b, c = first[k : k + 1], first[k + 1 : k + 2], second[k + 1 : k + 2]
        scale = 1.0 / (a * c - b * b)
        below = row > k + 1
        one = jnp.where(below, (first * c - second * b) * scale, 0.0)
        two = jnp.where(below, (second * a - first * b) * scale, 0.0)
        lower = lower - (one * lower[k : k + 1] + two * lower[k + 1 : k + 2])
        one, two = one[:, :members], two[:, :members]
        upper = upper - (one * upper[k : k + 1] + two * upper[k + 1 : k + 2])
    diagonal = jnp.sum(upper * eye, axis=1, keepdims=True)
    beside = (ids(square, 0) == ids(square, 1) + 1) & (ids(square, 0) % 2 == 1)
    share = jnp.sum(jnp.where(beside, upper, 0.0), axis=1, keepdims=True)
    previous = jnp.concatenate([diagonal[:1], diagonal[:-1]], axis=0)
    ratio = share / previous
    above = jnp.concatenate([lower[:1], lower[:-1]], axis=0)
    inverse = (lower - ratio * above) / jnp.sqrt(diagonal - ratio * share)
    high, low = halves(inverse)
    same_line = ids((rows, LANES), 0) % span == lane_line(ids((rows, LANES), 1), turn, members)
    for place, half in ((0, high), (rows, low)):
        chosen = jnp.where(same_line, dot32(placed, half), 0.0)
        weights_ref[place : place + rows, :] = chosen.astype(BF16)


def route_kernel(weights_ref, *refs):
    parts, out_ref = refs[:-1], refs[-1]
    packs, points, _ = parts[0].shape
    weights = weights_ref[...]
    rows = weights.shape[0] // 2
    span = rows // CAP
    lines = packs * span
    group = lax.axis_index("grid") * lax.axis_size("ham") + lax.axis_index("ham")
    for flip, part in enumerate(parts):
        start = pl.multiple_of((group ^ flip) * lines, lines)
        sums = []
        for pack in range(packs):
            if part.dtype == BF16:
                both = dot32(weights, part[pack], NT)
                result = both[:rows] + both[rows:]
            else:
                high, low = halves(part[pack])
                both = dot32(weights, high, NT)
                result = both[:rows] + (both[rows:] + dot32(weights[:rows], low, NT))
            sums.append(result.reshape(CAP, span, points))
        out_ref[:, pl.ds(start, lines), :] = jnp.concatenate(sums, axis=1).astype(BF16)


def call(kernel, name, shapes, flops, moved, scratch=(), scalars=0, operands=0):
    vmem = pl.BlockSpec(memory_space=pltpu.VMEM)
    smem = pl.BlockSpec(memory_space=pltpu.SMEM)
    return pl.pallas_call(
        kernel,
        name=name,
        out_shape=shapes,
        in_specs=[smem] * scalars + [vmem] * operands,
        out_specs=[vmem] * len(shapes),
        scratch_shapes=list(scratch),
        compiler_params=pltpu.CompilerParams(vmem_limit_bytes=VMEM_LIMIT),
        cost_estimate=pl.CostEstimate(flops=flops, bytes_accessed=moved, transcendentals=0),
    )


def local(orbitals, coulomb, occupied, owners):
    members, lines, points = orbitals.shape
    grids, near = lax.axis_size("grid"), lax.axis_size("ham")
    groups = grids * near
    padded = -(-points // LANES) * LANES
    span = LANES // members
    packs = lines // span
    shape = jax.ShapeDtypeStruct
    (packed,) = call(
        pack_kernel,
        "pack",
        [shape((packs, points, LANES), BF16)],
        orbitals.size,
        4 * orbitals.size,
        operands=1,
    )(orbitals)
    guests = exchanged(packed)
    tables = spectral_tables(points)
    (response,) = call(
        response_kernel,
        "response",
        [shape((lines, points, padded), F32)],
        4 * lines * points**3,
        4 * lines * points**2,
        operands=2,
    )(coulomb, tables)
    blocks = len(guests) + 1
    wide, narrow = call(
        functools.partial(image_kernel, members),
        "image",
        [shape((packs, points, LANES), F32), shape((packs, points, LANES), BF16)],
        2 * lines * points * padded * (4 * LANES),
        4 * lines * points**2,
        scalars=1,
        operands=blocks + 1,
    )(occupied, packed, *guests, response)
    (overlap,) = call(
        overlap_kernel,
        "overlap",
        [shape((members, LANES), F32)],
        4 * packs * points * LANES**2,
        8 * orbitals.size,
        operands=2,
    )(orbitals, wide)
    overlaps = [overlap] + [swapped(overlap, flip) for flip in range(1, groups)]
    images = [wide] + [swapped(wide, flip) for flip in range(1, near)]
    for grid in range(1, grids):
        across = swapped(narrow, grid * near)
        images += [across] + [swapped(across, flip) for flip in range(1, near)]
    cells = lines * groups * points

    intersection, weights = call(
        functools.partial(factor_kernel, cells),
        "factor",
        [shape((members, members), F32), shape((2 * CAP * span, LANES), BF16)],
        FACTOR_COST,
        members**2 * 4,
        operands=1 + groups,
    )(owners, *overlaps)
    (routed,) = call(
        route_kernel,
        "route",
        [shape((CAP, groups * lines, points), BF16)],
        2 * CAP * members * groups * lines * points,
        6 * members * groups * lines * points,
        operands=1 + groups,
    )(weights, *images)
    return routed[None, None], intersection[None]


def solution(mesh):
    in_specs = (P("band", ("grid", "ham"), None), P(("grid", "ham"), None), P(), P("band", None))
    out_specs = (P("band", ("grid", "ham"), None, None, None), P("band", None, None))
    return jax.shard_map(local, mesh=mesh, in_specs=in_specs, out_specs=out_specs, check_vma=False)
```

```python
import functools
import math

import jax
import jax.numpy as jnp
import numpy as np
from jax import lax
from jax.experimental import pallas as pl
from jax.experimental.pallas import tpu as pltpu
from jax.sharding import PartitionSpec as P

CAP = 8
LANES = 128
HIGHEST = lax.Precision.HIGHEST
VMEM_LIMIT = 48 * 1024 * 1024
FACTOR_COST = 3_000_000_000
NT = ((1,), (1,))
F32, BF16 = jnp.float32, jnp.bfloat16


def sources(block, count):
    odd = block % 2
    steps = (-2, 2 * odd - 1, 1 - 2 * odd, 2)
    return [(block + step + count) % count for step in steps]


def exchanged(value):
    count = lax.axis_size("band")
    assert count % 4 == 0
    tables = [sources(block, count) for block in range(count)]
    return [
        lax.ppermute(value, "band", [(row[turn], block) for block, row in enumerate(tables)])
        for turn in range(4)
    ]


def swapped(value, flip):
    count = lax.axis_size("grid") * lax.axis_size("ham")
    return lax.ppermute(value, ("grid", "ham"), [(group, group ^ flip) for group in range(count)])


def spectral_tables(points):
    midpoint = points // 2
    ids = np.arange(points)
    frequency = np.where(ids <= midpoint, ids, ids - midpoint)
    angles = (ids[:, None] * frequency[None, :] % points) * (2.0 * math.pi / points)
    forward = np.where((ids <= midpoint)[None, :], np.cos(angles), np.sin(angles))
    single = (frequency == 0) | (ids == midpoint)
    inverse = forward.T * (np.where(single, 1.0, 2.0) / points)[:, None]
    mirror = np.zeros((points, points))
    mirror[frequency, ids] += 0.5
    mirror[(points - frequency) % points, ids] += 0.5
    return jnp.asarray(np.stack([forward.T, inverse.T, mirror]).astype(np.float32)).astype(BF16)


def split(value):
    high = value.astype(BF16)
    return high, value - high.astype(F32)


def halves(value):
    high, rest = split(value)
    return high, rest.astype(BF16)


def dot32(a, b, contract=((1,), (0,))):
    return lax.dot_general(a, b, (contract, ((), ())), preferred_element_type=F32)


def dot_exact(a, b, contract=((1,), (0,))):
    return lax.dot_general(
        a, b, (contract, ((), ())), precision=HIGHEST, preferred_element_type=F32
    )


def ids(shape, axis):
    return lax.broadcasted_iota(jnp.int32, shape, axis)


def lane_member(lane, members):
    return lane % members


def lane_quarter(lane, turn):
    return (lane // (LANES // 4)) ^ turn


def lane_line(lane, turn, members):
    per = LANES // 4 // members
    return lane_quarter(lane, turn) * per + lane % (LANES // 4) // members


def own_turn():
    return lax.axis_index("band") % 4


def rows_of(block, pack, span):
    members, _, points = block.shape
    part = block[:, pack * span : (pack + 1) * span, :]
    return part.reshape(members * span, points)


def pack_kernel(orbitals_ref, out_ref):
    members = orbitals_ref.shape[0]
    span = LANES // members
    block = orbitals_ref[...].astype(F32)
    row, lane = ids((LANES, LANES), 0), ids((LANES, LANES), 1)
    source = lane_member(lane, members) * span + lane_line(lane, own_turn(), members)
    order = (row == source).astype(BF16)
    for pack in range(out_ref.shape[0]):
        rows = rows_of(block, pack, span).T.astype(BF16)
        out_ref[pack] = dot32(rows, order).astype(BF16)


def response_kernel(coulomb_ref, tables_ref, out_ref):
    points = coulomb_ref.shape[1]
    multiplier = dot_exact(coulomb_ref[...], tables_ref[2].astype(F32))
    forward = tables_ref[0]
    inverse = tables_ref[1].astype(F32)
    pad = jnp.zeros((points, out_ref.shape[2] - points), F32)
    for line in range(coulomb_ref.shape[0]):
        high, low = halves(inverse * multiplier[line : line + 1, :])
        out_ref[line, :, :points] = dot32(high, forward) + dot32(low, forward)
        out_ref[line, :, points:] = pad


def image_kernel(occupied_ref, orbitals_ref, *refs):
    blocks, (response_ref, high_ref, halves_ref, cross_ref) = refs[:-4], refs[-4:]
    members = orbitals_ref.shape[0]
    packs, points, _ = blocks[0].shape
    padded = response_ref.shape[2]
    span = LANES // members
    per = span // 4
    total = lax.axis_size("band")
    position = lax.axis_index("band")
    places = [position] + sources(position, total)
    turns = [place % 4 for place in places]
    lane = ids((1, LANES), 1)
    own_line = lane_line(lane, turns[0], members)
    filled = [lane_member(lane, members) < occupied_ref[place] for place in places]
    quarters = [lane_quarter(lane, turn) for turn in turns]
    step = lane % (LANES // 4) // members
    apart, merged = 1, (0, 2, 3, 4)
    blank = jnp.zeros((padded - points, 2 * LANES), BF16)
    natives = orbitals_ref[...].astype(F32)
    square = (LANES, LANES)
    same_line = ids(square, 0) % span == lane_line(ids(square, 1), turns[0], members)
    tiles = [[block[pack] for block in blocks] for pack in range(packs)]

    def weighted(pack, quarter):
        here = [q == quarter for q in quarters]
        together = sum(tiles[pack][m] * here[m].astype(F32).astype(BF16) for m in merged)
        window = jnp.concatenate([together, tiles[pack][apart]], axis=1)
        occupied = sum((here[m] & filled[m]).astype(F32) for m in merged)
        beside = (here[apart] & filled[apart]).astype(F32)
        both = jnp.concatenate([occupied, beside], axis=1)
        steps = jnp.concatenate([step, step], axis=1)
        masked = jnp.concatenate(
            [window * jnp.where(steps == k, both, 0.0).astype(BF16) for k in range(per)], axis=0
        )
        gram = dot32(masked, jnp.concatenate([window, blank], axis=0), NT)
        first = pack * span + quarter * per
        response = response_ref[first : first + per].reshape(per * points, padded)
        return jnp.concatenate(halves(gram * response), axis=0)

    order = [(pack, quarter) for pack in range(packs) for quarter in range(4)]
    ready = weighted(*order[0])
    cross = jnp.zeros(square, F32)
    for place, (pack, quarter) in enumerate(order):
        kernel = ready
        if place + 1 < len(order):
            ready = weighted(*order[place + 1])
        native = jnp.concatenate([tiles[pack][0], blank[:, :LANES]], axis=0)
        fields = dot32(kernel, native)
        if quarter == 0:
            image = jnp.zeros((points, LANES), F32)
        for k in range(per):
            a, b = k * points, (per + k) * points
            field = fields[a : a + points] + fields[b : b + points]
            image = jnp.where(own_line == quarter * per + k, field, image)
        if quarter == 3:
            high, low = halves(image)
            high_ref[pack] = high
            halves_ref[pack] = high
            halves_ref[packs + pack] = low
            rows = rows_of(natives, pack, span).astype(BF16)
            product = dot32(rows, jnp.concatenate([high, low], axis=1))
            cross = cross + (product[:, :LANES] + product[:, LANES:])
    cross_ref[...] = jnp.where(same_line, cross, 0.0).reshape(members, span, LANES).sum(axis=1)


def factor_kernel(cells, owners_ref, *refs):
    parts, (overlap_ref, weights_ref) = refs[:-2], refs[-2:]
    members = owners_ref.shape[0]
    span = LANES // members
    turn = own_turn()
    sums = [part[...] for part in parts]
    while len(sums) > 1:
        sums = [a + b for a, b in zip(sums[::2], sums[1::2])]
    high, rest = split(sums[0])
    pieces = [high, *halves(rest)]
    across = (members, LANES)
    gather = (ids(across, 0) == lane_member(ids(across, 1), members)).astype(BF16)
    overlap = sum(dot32(piece, gather, NT) for piece in pieces) * (1.0 / cells)
    flipped = sum(dot32(gather, piece, NT) for piece in pieces) * (1.0 / cells)
    overlap_ref[...] = overlap
    rows = CAP * span
    square = (members, members)
    group = lax.axis_index("grid") * lax.axis_size("ham") + lax.axis_index("ham")
    mine = (owners_ref[...] == group).astype(F32)
    eye = (ids(square, 0) == ids(square, 1)).astype(F32)
    mine_row = jnp.sum(mine * eye, axis=0, keepdims=True)
    before = (ids(square, 0) < ids(square, 1)).astype(F32)
    ranking = jnp.sum(mine * before, axis=0, keepdims=True)
    slot = (ids((rows, members), 0) // span).astype(F32)
    placed = (jnp.where(slot == ranking, 1.0, 0.0) * mine_row).astype(BF16)
    wide = (members, LANES)
    row = ids(wide, 0)
    upper = 0.5 * (overlap + flipped)
    lower = (row == lane_member(ids(wide, 1), members)).astype(F32)
    for k in range(0, members, 2):
        first = jnp.broadcast_to(upper[:, k : k + 1], wide)
        second = jnp.broadcast_to(upper[:, k + 1 : k + 2], wide)
        a, b, c = first[k : k + 1], first[k + 1 : k + 2], second[k + 1 : k + 2]
        scale = 1.0 / (a * c - b * b)
        below = row > k + 1
        one = jnp.where(below, (first * c - second * b) * scale, 0.0)
        two = jnp.where(below, (second * a - first * b) * scale, 0.0)
        lower = lower - (one * lower[k : k + 1] + two * lower[k + 1 : k + 2])
        one, two = one[:, :members], two[:, :members]
        upper = upper - (one * upper[k : k + 1] + two * upper[k + 1 : k + 2])
    diagonal = jnp.sum(upper * eye, axis=1, keepdims=True)
    beside = (ids(square, 0) == ids(square, 1) + 1) & (ids(square, 0) % 2 == 1)
    share = jnp.sum(jnp.where(beside, upper, 0.0), axis=1, keepdims=True)
    previous = jnp.concatenate([diagonal[:1], diagonal[:-1]], axis=0)
    ratio = share / previous
    above = jnp.concatenate([lower[:1], lower[:-1]], axis=0)
    inverse = (lower - ratio * above) / jnp.sqrt(diagonal - ratio * share)
    high, low = halves(inverse)
    same_line = ids((rows, LANES), 0) % span == lane_line(ids((rows, LANES), 1), turn, members)
    for place, half in ((0, high), (rows, low)):
        chosen = jnp.where(same_line, dot32(placed, half), 0.0)
        weights_ref[place : place + rows, :] = chosen.astype(BF16)


def route_kernel(weights_ref, *refs):
    parts, (out_hbm, staged, semaphores) = refs[:-3], refs[-3:]
    points = staged.shape[3]
    weights = weights_ref[...]
    rows = weights.shape[0] // 2
    span = rows // CAP
    lines = staged.shape[2]
    packs = lines // span
    group = lax.axis_index("grid") * lax.axis_size("ham") + lax.axis_index("ham")
    copies = []
    for flip, part in enumerate(parts):
        sums = []
        for pack in range(packs):
            both = dot32(weights, part[pack], NT)
            result = both[:rows] + both[rows:]
            if part.shape[0] > packs:
                result = result + dot32(weights[:rows], part[packs + pack], NT)
            sums.append(result.reshape(CAP, span, points))
        staged[flip] = jnp.concatenate(sums, axis=1).astype(BF16)
        start = pl.multiple_of((group ^ flip) * lines, lines)
        target = out_hbm.at[:, pl.ds(start, lines), :]
        copies.append(pltpu.make_async_copy(staged.at[flip], target, semaphores.at[flip]))
        copies[-1].start()
    for copy in copies:
        copy.wait()


def call(kernel, name, shapes, flops, moved, scratch=(), scalars=0, operands=0, remote=False):
    vmem = pl.BlockSpec(memory_space=pltpu.VMEM)
    smem = pl.BlockSpec(memory_space=pltpu.SMEM)
    return pl.pallas_call(
        kernel,
        name=name,
        out_shape=shapes,
        in_specs=[smem] * scalars + [vmem] * operands,
        out_specs=[pl.BlockSpec(memory_space=pl.ANY) if remote else vmem] * len(shapes),
        scratch_shapes=list(scratch),
        compiler_params=pltpu.CompilerParams(vmem_limit_bytes=VMEM_LIMIT),
        cost_estimate=pl.CostEstimate(flops=flops, bytes_accessed=moved, transcendentals=0),
    )


def local(orbitals, coulomb, occupied, owners):
    members, lines, points = orbitals.shape
    grids, near = lax.axis_size("grid"), lax.axis_size("ham")
    groups = grids * near
    padded = -(-points // LANES) * LANES
    span = LANES // members
    packs = lines // span
    shape = jax.ShapeDtypeStruct
    (packed,) = call(
        pack_kernel,
        "pack",
        [shape((packs, points, LANES), BF16)],
        orbitals.size,
        4 * orbitals.size,
        operands=1,
    )(orbitals)
    guests = exchanged(packed)
    tables = spectral_tables(points)
    (response,) = call(
        response_kernel,
        "response",
        [shape((lines, points, padded), F32)],
        4 * lines * points**3,
        4 * lines * points**2,
        operands=2,
    )(coulomb, tables)
    blocks = len(guests) + 1
    high, parts, cross = call(
        image_kernel,
        "image",
        [
            shape((packs, points, LANES), BF16),
            shape((2 * packs, points, LANES), BF16),
            shape((members, LANES), F32),
        ],
        2 * lines * points * padded * (4 * LANES),
        4 * lines * points**2,
        scalars=1,
        operands=blocks + 2,
    )(occupied, orbitals, packed, *guests, response)
    for flip in range(near.bit_length() - 1):
        cross = cross + swapped(cross, 1 << flip)
    sums = [cross] + [swapped(cross, grid * near) for grid in range(1, grids)]
    images = [parts] + [swapped(parts, flip) for flip in range(1, near)]
    for grid in range(1, grids):
        across = swapped(high, grid * near)
        images += [across] + [swapped(across, flip) for flip in range(1, near)]
    cells = lines * groups * points

    intersection, weights = call(
        functools.partial(factor_kernel, cells),
        "factor",
        [shape((members, members), F32), shape((2 * CAP * span, LANES), BF16)],
        FACTOR_COST,
        members**2 * 4,
        operands=1 + grids,
    )(owners, *sums)
    (routed,) = call(
        route_kernel,
        "route",
        [shape((CAP, groups * lines, points), BF16)],
        2 * CAP * members * groups * lines * points,
        6 * members * groups * lines * points,
        scratch=[
            pltpu.VMEM((groups, CAP, lines, points), BF16),
            pltpu.SemaphoreType.DMA((groups,)),
        ],
        operands=1 + groups,
        remote=True,
    )(weights, *images)
    return routed[None, None], intersection[None]


def solution(mesh):
    in_specs = (P("band", ("grid", "ham"), None), P(("grid", "ham"), None), P(), P("band", None))
    out_specs = (P("band", ("grid", "ham"), None, None, None), P("band", None, None))
    return jax.shard_map(local, mesh=mesh, in_specs=in_specs, out_specs=out_specs, check_vma=False)
```

```python
import functools
import math

import jax
import jax.numpy as jnp
import numpy as np
from jax import lax
from jax.experimental import pallas as pl
from jax.experimental.pallas import tpu as pltpu
from jax.sharding import PartitionSpec as P

CAP = 8
LANES = 128
HIGHEST = lax.Precision.HIGHEST
VMEM_LIMIT = 48 * 1024 * 1024
FACTOR_COST = 3_000_000_000
NT = ((1,), (1,))
F32, BF16 = jnp.float32, jnp.bfloat16


def sources(block, count):
    odd = block % 2
    steps = (-2, 2 * odd - 1, 1 - 2 * odd, 2)
    return [(block + step + count) % count for step in steps]


def exchanged(value):
    count = lax.axis_size("band")
    assert count % 4 == 0
    tables = [sources(block, count) for block in range(count)]
    return [
        lax.ppermute(value, "band", [(row[turn], block) for block, row in enumerate(tables)])
        for turn in range(4)
    ]


def swapped(value, flip):
    count = lax.axis_size("grid") * lax.axis_size("ham")
    return lax.ppermute(value, ("grid", "ham"), [(group, group ^ flip) for group in range(count)])


def spectral_tables(points):
    midpoint = points // 2
    ids = np.arange(points)
    frequency = np.where(ids <= midpoint, ids, ids - midpoint)
    angles = (ids[:, None] * frequency[None, :] % points) * (2.0 * math.pi / points)
    forward = np.where((ids <= midpoint)[None, :], np.cos(angles), np.sin(angles))
    single = (frequency == 0) | (ids == midpoint)
    inverse = forward.T * (np.where(single, 1.0, 2.0) / points)[:, None]
    mirror = np.zeros((points, points))
    mirror[frequency, ids] += 0.5
    mirror[(points - frequency) % points, ids] += 0.5
    return jnp.asarray(np.stack([forward.T, inverse.T, mirror]).astype(np.float32)).astype(BF16)


def split(value):
    high = value.astype(BF16)
    return high, value - high.astype(F32)


def halves(value):
    high, rest = split(value)
    return high, rest.astype(BF16)


def dot32(a, b, contract=((1,), (0,))):
    return lax.dot_general(a, b, (contract, ((), ())), preferred_element_type=F32)


def dot_exact(a, b, contract=((1,), (0,))):
    return lax.dot_general(
        a, b, (contract, ((), ())), precision=HIGHEST, preferred_element_type=F32
    )


def ids(shape, axis):
    return lax.broadcasted_iota(jnp.int32, shape, axis)


def lane_member(lane, members):
    return lane % members


def lane_quarter(lane, turn):
    return (lane // (LANES // 4)) ^ turn


def lane_line(lane, turn, members):
    per = LANES // 4 // members
    return lane_quarter(lane, turn) * per + lane % (LANES // 4) // members


def own_turn():
    return lax.axis_index("band") % 4


def rows_of(block, pack, span):
    members, _, points = block.shape
    part = block[:, pack * span : (pack + 1) * span, :]
    return part.reshape(members * span, points)


def pack_kernel(orbitals_ref, out_ref):
    members = orbitals_ref.shape[0]
    span = LANES // members
    block = orbitals_ref[...].astype(F32)
    row, lane = ids((LANES, LANES), 0), ids((LANES, LANES), 1)
    source = lane_member(lane, members) * span + lane_line(lane, own_turn(), members)
    order = (row == source).astype(BF16)
    for pack in range(out_ref.shape[0]):
        rows = rows_of(block, pack, span).T.astype(BF16)
        out_ref[pack] = dot32(rows, order).astype(BF16)


def response_kernel(coulomb_ref, tables_ref, out_ref):
    points = coulomb_ref.shape[1]
    multiplier = dot_exact(coulomb_ref[...], tables_ref[2].astype(F32))
    forward = tables_ref[0]
    inverse = tables_ref[1].astype(F32)
    pad = jnp.zeros((points, out_ref.shape[2] - points), F32)
    for line in range(coulomb_ref.shape[0]):
        high, low = halves(inverse * multiplier[line : line + 1, :])
        out_ref[line, :, :points] = dot32(high, forward) + dot32(low, forward)
        out_ref[line, :, points:] = pad


def image_kernel(members, occupied_ref, *refs):
    blocks, (response_ref, high_ref, halves_ref) = refs[:-3], refs[-3:]
    packs, points, _ = blocks[0].shape
    padded = response_ref.shape[2]
    span = LANES // members
    per = span // 4
    total = lax.axis_size("band")
    position = lax.axis_index("band")
    places = [position] + sources(position, total)
    turns = [place % 4 for place in places]
    lane = ids((1, LANES), 1)
    own_line = lane_line(lane, turns[0], members)
    filled = [lane_member(lane, members) < occupied_ref[place] for place in places]
    quarters = [lane_quarter(lane, turn) for turn in turns]
    step = lane % (LANES // 4) // members
    apart, merged = 1, (0, 2, 3, 4)
    blank = jnp.zeros((padded - points, 2 * LANES), BF16)
    for pack in range(packs):
        tiles = [block[pack] for block in blocks]
        native = jnp.concatenate([tiles[0], blank[:, :LANES]], axis=0)
        image = jnp.zeros((points, LANES), F32)
        for quarter in range(4):
            here = [(q == quarter) for q in quarters]
            together = sum(tiles[m] * here[m].astype(F32).astype(BF16) for m in merged)
            window = jnp.concatenate([together, tiles[apart]], axis=1)
            occupied = sum((here[m] & filled[m]).astype(F32) for m in merged)
            beside = (here[apart] & filled[apart]).astype(F32)
            both = jnp.concatenate([occupied, beside], axis=1)
            steps = jnp.concatenate([step, step], axis=1)
            masked = jnp.concatenate(
                [window * jnp.where(steps == k, both, 0.0).astype(BF16) for k in range(per)], axis=0
            )
            gram = dot32(masked, jnp.concatenate([window, blank], axis=0), NT)
            first = pack * span + quarter * per
            response = response_ref[first : first + per].reshape(per * points, padded)
            high, low = halves(gram * response)
            fields = dot32(jnp.concatenate([high, low], axis=0), native)
            for k in range(per):
                a, b = k * points, (per + k) * points
                field = fields[a : a + points] + fields[b : b + points]
                image = jnp.where(own_line == quarter * per + k, field, image)
        high, low = halves(image)
        high_ref[pack] = high
        halves_ref[pack] = high
        halves_ref[packs + pack] = low


def overlap_kernel(orbitals_ref, halves_ref, out_ref):
    members, _, _ = orbitals_ref.shape
    span = LANES // members
    natives = orbitals_ref[...].astype(F32)
    square = (LANES, LANES)
    same_line = ids(square, 0) % span == lane_line(ids(square, 1), own_turn(), members)
    cross = jnp.zeros(square, F32)
    packs = halves_ref.shape[0] // 2
    for pack in range(packs):
        rows = rows_of(natives, pack, span).astype(BF16)
        both = jnp.concatenate([halves_ref[pack], halves_ref[packs + pack]], axis=1)
        product = dot32(rows, both)
        cross = cross + (product[:, :LANES] + product[:, LANES:])
    out_ref[...] = jnp.where(same_line, cross, 0.0).reshape(members, span, LANES).sum(axis=1)


def factor_kernel(cells, owners_ref, *refs):
    parts, (overlap_ref, weights_ref) = refs[:-2], refs[-2:]
    members = owners_ref.shape[0]
    span = LANES // members
    turn = own_turn()
    sums = [part[...] for part in parts]
    while len(sums) > 1:
        sums = [a + b for a, b in zip(sums[::2], sums[1::2])]
    high, rest = split(sums[0])
    pieces = [high, *halves(rest)]
    across = (members, LANES)
    gather = (ids(across, 0) == lane_member(ids(across, 1), members)).astype(BF16)
    overlap = sum(dot32(piece, gather, NT) for piece in pieces) * (1.0 / cells)
    flipped = sum(dot32(gather, piece, NT) for piece in pieces) * (1.0 / cells)
    overlap_ref[...] = overlap
    rows = CAP * span
    square = (members, members)
    group = lax.axis_index("grid") * lax.axis_size("ham") + lax.axis_index("ham")
    mine = (owners_ref[...] == group).astype(F32)
    eye = (ids(square, 0) == ids(square, 1)).astype(F32)
    mine_row = jnp.sum(mine * eye, axis=0, keepdims=True)
    before = (ids(square, 0) < ids(square, 1)).astype(F32)
    ranking = jnp.sum(mine * before, axis=0, keepdims=True)
    slot = (ids((rows, members), 0) // span).astype(F32)
    placed = (jnp.where(slot == ranking, 1.0, 0.0) * mine_row).astype(BF16)
    wide = (members, LANES)
    row = ids(wide, 0)
    upper = 0.5 * (overlap + flipped)
    lower = (row == lane_member(ids(wide, 1), members)).astype(F32)
    for k in range(0, members, 2):
        first = jnp.broadcast_to(upper[:, k : k + 1], wide)
        second = jnp.broadcast_to(upper[:, k + 1 : k + 2], wide)
        a, b, c = first[k : k + 1], first[k + 1 : k + 2], second[k + 1 : k + 2]
        scale = 1.0 / (a * c - b * b)
        below = row > k + 1
        one = jnp.where(below, (first * c - second * b) * scale, 0.0)
        two = jnp.where(below, (second * a - first * b) * scale, 0.0)
        lower = lower - (one * lower[k : k + 1] + two * lower[k + 1 : k + 2])
        one, two = one[:, :members], two[:, :members]
        upper = upper - (one * upper[k : k + 1] + two * upper[k + 1 : k + 2])
    diagonal = jnp.sum(upper * eye, axis=1, keepdims=True)
    beside = (ids(square, 0) == ids(square, 1) + 1) & (ids(square, 0) % 2 == 1)
    share = jnp.sum(jnp.where(beside, upper, 0.0), axis=1, keepdims=True)
    previous = jnp.concatenate([diagonal[:1], diagonal[:-1]], axis=0)
    ratio = share / previous
    above = jnp.concatenate([lower[:1], lower[:-1]], axis=0)
    inverse = (lower - ratio * above) / jnp.sqrt(diagonal - ratio * share)
    high, low = halves(inverse)
    same_line = ids((rows, LANES), 0) % span == lane_line(ids((rows, LANES), 1), turn, members)
    for place, half in ((0, high), (rows, low)):
        chosen = jnp.where(same_line, dot32(placed, half), 0.0)
        weights_ref[place : place + rows, :] = chosen.astype(BF16)


def route_kernel(overlap_ref, weights_ref, *refs):
    parts, (out_hbm, overlap_hbm, staged, semaphores) = refs[:-4], refs[-4:]
    groups = len(parts)
    copies = [pltpu.make_async_copy(overlap_ref, overlap_hbm, semaphores.at[groups])]
    copies[0].start()
    points = staged.shape[3]
    weights = weights_ref[...]
    rows = weights.shape[0] // 2
    span = rows // CAP
    lines = staged.shape[2]
    packs = lines // span
    group = lax.axis_index("grid") * lax.axis_size("ham") + lax.axis_index("ham")
    for flip, part in enumerate(parts):
        sums = []
        for pack in range(packs):
            both = dot32(weights, part[pack], NT)
            result = both[:rows] + both[rows:]
            if part.shape[0] > packs:
                result = result + dot32(weights[:rows], part[packs + pack], NT)
            sums.append(result.reshape(CAP, span, points))
        staged[flip] = jnp.concatenate(sums, axis=1).astype(BF16)
        start = pl.multiple_of((group ^ flip) * lines, lines)
        target = out_hbm.at[:, pl.ds(start, lines), :]
        copies.append(pltpu.make_async_copy(staged.at[flip], target, semaphores.at[flip]))
        copies[-1].start()
    for copy in copies:
        copy.wait()


def call(kernel, name, shapes, flops, moved, scratch=(), scalars=0, operands=0, remote=False):
    vmem = pl.BlockSpec(memory_space=pltpu.VMEM)
    smem = pl.BlockSpec(memory_space=pltpu.SMEM)
    return pl.pallas_call(
        kernel,
        name=name,
        out_shape=shapes,
        in_specs=[smem] * scalars + [vmem] * operands,
        out_specs=[pl.BlockSpec(memory_space=pl.ANY) if remote else vmem] * len(shapes),
        scratch_shapes=list(scratch),
        compiler_params=pltpu.CompilerParams(vmem_limit_bytes=VMEM_LIMIT),
        cost_estimate=pl.CostEstimate(flops=flops, bytes_accessed=moved, transcendentals=0),
    )


def local(orbitals, coulomb, occupied, owners):
    members, lines, points = orbitals.shape
    grids, near = lax.axis_size("grid"), lax.axis_size("ham")
    groups = grids * near
    padded = -(-points // LANES) * LANES
    span = LANES // members
    packs = lines // span
    shape = jax.ShapeDtypeStruct
    (packed,) = call(
        pack_kernel,
        "pack",
        [shape((packs, points, LANES), BF16)],
        orbitals.size,
        4 * orbitals.size,
        operands=1,
    )(orbitals)
    guests = exchanged(packed)
    tables = spectral_tables(points)
    (response,) = call(
        response_kernel,
        "response",
        [shape((lines, points, padded), F32)],
        4 * lines * points**3,
        4 * lines * points**2,
        operands=2,
    )(coulomb, tables)
    blocks = len(guests) + 1
    high, parts = call(
        functools.partial(image_kernel, members),
        "image",
        [
            shape((packs, points, LANES), BF16),
            shape((2 * packs, points, LANES), BF16),
        ],
        2 * lines * points * padded * (4 * LANES),
        4 * lines * points**2,
        scalars=1,
        operands=blocks + 1,
    )(occupied, packed, *guests, response)
    (overlap,) = call(
        overlap_kernel,
        "overlap",
        [shape((members, LANES), F32)],
        4 * packs * points * LANES**2,
        8 * orbitals.size,
        operands=2,
    )(orbitals, parts)
    overlaps = [overlap] + [swapped(overlap, flip) for flip in range(1, groups)]
    images = [parts] + [swapped(parts, flip) for flip in range(1, near)]
    for grid in range(1, grids):
        across = swapped(high, grid * near)
        images += [across] + [swapped(across, flip) for flip in range(1, near)]
    cells = lines * groups * points

    intersection, weights = call(
        functools.partial(factor_kernel, cells),
        "factor",
        [shape((members, members), F32), shape((2 * CAP * span, LANES), BF16)],
        FACTOR_COST,
        members**2 * 4,
        operands=1 + groups,
    )(owners, *overlaps)
    routed, intersection = call(
        route_kernel,
        "route",
        [shape((CAP, groups * lines, points), BF16), shape((members, members), F32)],
        2 * CAP * members * groups * lines * points,
        6 * members * groups * lines * points,
        scratch=[
            pltpu.VMEM((groups, CAP, lines, points), BF16),
            pltpu.SemaphoreType.DMA((groups + 1,)),
        ],
        operands=2 + groups,
        remote=True,
    )(intersection, weights, *images)
    return routed[None, None], intersection[None]


def solution(mesh):
    in_specs = (P("band", ("grid", "ham"), None), P(("grid", "ham"), None), P(), P("band", None))
    out_specs = (P("band", ("grid", "ham"), None, None, None), P("band", None, None))
    return jax.shard_map(local, mesh=mesh, in_specs=in_specs, out_specs=out_specs, check_vma=False)
```

```python
import functools
import math

import jax
import jax.numpy as jnp
import numpy as np
from jax import lax
from jax.experimental import pallas as pl
from jax.experimental.pallas import tpu as pltpu
from jax.sharding import PartitionSpec as P

CAP = 8
LANES = 128
HIGHEST = lax.Precision.HIGHEST
VMEM_LIMIT = 48 * 1024 * 1024
FACTOR_COST = 3_000_000_000
NT = ((1,), (1,))
F32, BF16 = jnp.float32, jnp.bfloat16


def sources(block, count):
    odd = block % 2
    steps = (-2, 2 * odd - 1, 1 - 2 * odd, 2)
    return [(block + step + count) % count for step in steps]


def exchanged(value):
    count = lax.axis_size("band")
    assert count % 4 == 0
    tables = [sources(block, count) for block in range(count)]
    return [
        lax.ppermute(value, "band", [(row[turn], block) for block, row in enumerate(tables)])
        for turn in range(4)
    ]


def swapped(value, flip):
    count = lax.axis_size("grid") * lax.axis_size("ham")
    return lax.ppermute(value, ("grid", "ham"), [(group, group ^ flip) for group in range(count)])


def spectral_tables(points):
    midpoint = points // 2
    ids = np.arange(points)
    frequency = np.where(ids <= midpoint, ids, ids - midpoint)
    angles = (ids[:, None] * frequency[None, :] % points) * (2.0 * math.pi / points)
    forward = np.where((ids <= midpoint)[None, :], np.cos(angles), np.sin(angles))
    single = (frequency == 0) | (ids == midpoint)
    inverse = forward.T * (np.where(single, 1.0, 2.0) / points)[:, None]
    mirror = np.zeros((points, points))
    mirror[frequency, ids] += 0.5
    mirror[(points - frequency) % points, ids] += 0.5
    return jnp.asarray(np.stack([forward.T, inverse.T, mirror]).astype(np.float32)).astype(BF16)


def split(value):
    high = value.astype(BF16)
    return high, value - high.astype(F32)


def halves(value):
    high, rest = split(value)
    return high, rest.astype(BF16)


def dot32(a, b, contract=((1,), (0,))):
    return lax.dot_general(a, b, (contract, ((), ())), preferred_element_type=F32)


def dot_exact(a, b, contract=((1,), (0,))):
    return lax.dot_general(
        a, b, (contract, ((), ())), precision=HIGHEST, preferred_element_type=F32
    )


def ids(shape, axis):
    return lax.broadcasted_iota(jnp.int32, shape, axis)


def lane_member(lane, members):
    return lane % members


def lane_quarter(lane, turn):
    return (lane // (LANES // 4)) ^ turn


def lane_line(lane, turn, members):
    per = LANES // 4 // members
    return lane_quarter(lane, turn) * per + lane % (LANES // 4) // members


def own_turn():
    return lax.axis_index("band") % 4


def rows_of(block, pack, span):
    members, _, points = block.shape
    part = block[:, pack * span : (pack + 1) * span, :]
    return part.reshape(members * span, points)


def pack_kernel(orbitals_ref, out_ref):
    members = orbitals_ref.shape[0]
    span = LANES // members
    block = orbitals_ref[...].astype(F32)
    row, lane = ids((LANES, LANES), 0), ids((LANES, LANES), 1)
    source = lane_member(lane, members) * span + lane_line(lane, own_turn(), members)
    order = (row == source).astype(BF16)
    for pack in range(out_ref.shape[0]):
        rows = rows_of(block, pack, span).T.astype(BF16)
        out_ref[pack] = dot32(rows, order).astype(BF16)


def response_kernel(coulomb_ref, tables_ref, out_ref):
    points = coulomb_ref.shape[1]
    multiplier = dot_exact(coulomb_ref[...], tables_ref[2].astype(F32))
    forward = tables_ref[0]
    inverse = tables_ref[1].astype(F32)
    pad = jnp.zeros((points, out_ref.shape[2] - points), F32)
    for line in range(coulomb_ref.shape[0]):
        high, low = halves(inverse * multiplier[line : line + 1, :])
        out_ref[line, :, :points] = dot32(high, forward) + dot32(low, forward)
        out_ref[line, :, points:] = pad


def image_kernel(members, occupied_ref, *refs):
    blocks, (response_ref, high_ref, halves_ref) = refs[:-3], refs[-3:]
    packs, points, _ = blocks[0].shape
    padded = response_ref.shape[2]
    span = LANES // members
    per = span // 4
    total = lax.axis_size("band")
    position = lax.axis_index("band")
    places = [position] + sources(position, total)
    turns = [place % 4 for place in places]
    lane = ids((1, LANES), 1)
    own_line = lane_line(lane, turns[0], members)
    filled = [lane_member(lane, members) < occupied_ref[place] for place in places]
    quarters = [lane_quarter(lane, turn) for turn in turns]
    step = lane % (LANES // 4) // members
    apart, merged = 1, (0, 2, 3, 4)
    blank = jnp.zeros((padded - points, 2 * LANES), BF16)
    for pack in range(packs):
        tiles = [block[pack] for block in blocks]
        native = jnp.concatenate([tiles[0], blank[:, :LANES]], axis=0)
        image = jnp.zeros((points, LANES), F32)
        for quarter in range(4):
            here = [(q == quarter) for q in quarters]
            together = sum(tiles[m] * here[m].astype(F32).astype(BF16) for m in merged)
            window = jnp.concatenate([together, tiles[apart]], axis=1)
            occupied = sum((here[m] & filled[m]).astype(F32) for m in merged)
            beside = (here[apart] & filled[apart]).astype(F32)
            both = jnp.concatenate([occupied, beside], axis=1)
            steps = jnp.concatenate([step, step], axis=1)
            masked = jnp.concatenate(
                [window * jnp.where(steps == k, both, 0.0).astype(BF16) for k in range(per)], axis=0
            )
            gram = dot32(masked, jnp.concatenate([window, blank], axis=0), NT)
            first = pack * span + quarter * per
            response = response_ref[first : first + per].reshape(per * points, padded)
            high, low = halves(gram * response)
            fields = dot32(jnp.concatenate([high, low], axis=0), native)
            for k in range(per):
                a, b = k * points, (per + k) * points
                field = fields[a : a + points] + fields[b : b + points]
                image = jnp.where(own_line == quarter * per + k, field, image)
        high, low = halves(image)
        high_ref[pack] = high
        halves_ref[pack] = high
        halves_ref[packs + pack] = low


def overlap_kernel(orbitals_ref, halves_ref, out_ref):
    members, _, _ = orbitals_ref.shape
    span = LANES // members
    natives = orbitals_ref[...].astype(F32)
    square = (LANES, LANES)
    same_line = ids(square, 0) % span == lane_line(ids(square, 1), own_turn(), members)
    cross = jnp.zeros(square, F32)
    packs = halves_ref.shape[0] // 2
    for pack in range(packs):
        rows = rows_of(natives, pack, span).astype(BF16)
        both = jnp.concatenate([halves_ref[pack], halves_ref[packs + pack]], axis=1)
        product = dot32(rows, both)
        cross = cross + (product[:, :LANES] + product[:, LANES:])
    out_ref[...] = jnp.where(same_line, cross, 0.0).reshape(members, span, LANES).sum(axis=1)


def factor_kernel(cells, owners_ref, *refs):
    parts, (overlap_ref, weights_ref) = refs[:-2], refs[-2:]
    members = owners_ref.shape[0]
    span = LANES // members
    turn = own_turn()
    sums = [part[...] for part in parts]
    while len(sums) > 1:
        sums = [a + b for a, b in zip(sums[::2], sums[1::2])]
    high, rest = split(sums[0])
    pieces = [high, *halves(rest)]
    across = (members, LANES)
    gather = (ids(across, 0) == lane_member(ids(across, 1), members)).astype(BF16)
    overlap = sum(dot32(piece, gather, NT) for piece in pieces) * (1.0 / cells)
    flipped = sum(dot32(gather, piece, NT) for piece in pieces) * (1.0 / cells)
    overlap_ref[...] = overlap
    rows = CAP * span
    square = (members, members)
    group = lax.axis_index("grid") * lax.axis_size("ham") + lax.axis_index("ham")
    mine = (owners_ref[...] == group).astype(F32)
    eye = (ids(square, 0) == ids(square, 1)).astype(F32)
    mine_row = jnp.sum(mine * eye, axis=0, keepdims=True)
    before = (ids(square, 0) < ids(square, 1)).astype(F32)
    ranking = jnp.sum(mine * before, axis=0, keepdims=True)
    slot = (ids((rows, members), 0) // span).astype(F32)
    placed = (jnp.where(slot == ranking, 1.0, 0.0) * mine_row).astype(BF16)
    wide = (members, LANES)
    row = ids(wide, 0)
    upper = 0.5 * (overlap + flipped)
    columns = [jnp.broadcast_to(upper[:, j : j + 1], wide) for j in range(members)]
    lower = (row == lane_member(ids(wide, 1), members)).astype(F32)
    diagonal = ratio = jnp.zeros(wide, F32)
    for k in range(0, members, 2):
        first, second = columns[k], columns[k + 1]
        a, b, c = first[k : k + 1], first[k + 1 : k + 2], second[k + 1 : k + 2]
        share = b / a
        rest = c - share * b
        diagonal = jnp.where(row == k, a, jnp.where(row == k + 1, rest, diagonal))
        ratio = jnp.where(row == k + 1, share, ratio)
        scale = 1.0 / (a * c - b * b)
        below = row > k + 1
        one = jnp.where(below, (first * c - second * b) * scale, 0.0)
        two = jnp.where(below, (second * a - first * b) * scale, 0.0)
        lower = lower - (one * lower[k : k + 1] + two * lower[k + 1 : k + 2])
        for j in range(k + 2, members):
            column = columns[j]
            columns[j] = column - (one * column[k : k + 1] + two * column[k + 1 : k + 2])
    above = jnp.concatenate([lower[:1], lower[:-1]], axis=0)
    inverse = (lower - ratio * above) / jnp.sqrt(diagonal)
    high, low = halves(inverse)
    same_line = ids((rows, LANES), 0) % span == lane_line(ids((rows, LANES), 1), turn, members)
    blank = jnp.zeros((rows, LANES), BF16)
    chosen = [jnp.where(same_line, dot32(placed, half), 0.0).astype(BF16) for half in (high, low)]
    for i, half in enumerate(chosen + chosen):
        pair = [half, blank] if i < 2 else [blank, half]
        weights_ref[i * rows : (i + 1) * rows, :] = jnp.concatenate(pair, axis=1)


def route_kernel(overlap_ref, weights_ref, *refs):
    parts, (out_hbm, overlap_hbm, staged, semaphores) = refs[:-4], refs[-4:]
    groups = len(parts)
    copies = [pltpu.make_async_copy(overlap_ref, overlap_hbm, semaphores.at[groups])]
    copies[0].start()
    points = staged.shape[3]
    weights = weights_ref[...]
    rows = weights.shape[0] // 4
    span = rows // CAP
    lines = staged.shape[2]
    packs = lines // span
    highs = jnp.concatenate([weights[:rows], weights[2 * rows : 3 * rows]], axis=0)
    group = lax.axis_index("grid") * lax.axis_size("ham") + lax.axis_index("ham")
    for flip, part in enumerate(parts):
        sums = []
        for pack in range(0, packs, 2):
            field = jnp.concatenate([part[pack], part[pack + 1]], axis=1)
            both = dot32(weights, field, NT)
            results = [both[:rows] + both[rows : 2 * rows], both[2 * rows : 3 * rows] + both[3 * rows :]]
            if part.shape[0] > packs:
                place = packs + pack
                rest = dot32(highs, jnp.concatenate([part[place], part[place + 1]], axis=1), NT)
                results = [results[0] + rest[:rows], results[1] + rest[rows:]]
            sums += [result.reshape(CAP, span, points) for result in results]
        staged[flip] = jnp.concatenate(sums, axis=1).astype(BF16)
        start = pl.multiple_of((group ^ flip) * lines, lines)
        target = out_hbm.at[:, pl.ds(start, lines), :]
        copies.append(pltpu.make_async_copy(staged.at[flip], target, semaphores.at[flip]))
        copies[-1].start()
    for copy in copies:
        copy.wait()


def call(kernel, name, shapes, flops, moved, scratch=(), scalars=0, operands=0, remote=False):
    vmem = pl.BlockSpec(memory_space=pltpu.VMEM)
    smem = pl.BlockSpec(memory_space=pltpu.SMEM)
    return pl.pallas_call(
        kernel,
        name=name,
        out_shape=shapes,
        in_specs=[smem] * scalars + [vmem] * operands,
        out_specs=[pl.BlockSpec(memory_space=pl.ANY) if remote else vmem] * len(shapes),
        scratch_shapes=list(scratch),
        compiler_params=pltpu.CompilerParams(vmem_limit_bytes=VMEM_LIMIT),
        cost_estimate=pl.CostEstimate(flops=flops, bytes_accessed=moved, transcendentals=0),
    )


def local(orbitals, coulomb, occupied, owners):
    members, lines, points = orbitals.shape
    grids, near = lax.axis_size("grid"), lax.axis_size("ham")
    groups = grids * near
    padded = -(-points // LANES) * LANES
    span = LANES // members
    packs = lines // span
    assert packs % 2 == 0
    shape = jax.ShapeDtypeStruct
    (packed,) = call(
        pack_kernel,
        "pack",
        [shape((packs, points, LANES), BF16)],
        orbitals.size,
        4 * orbitals.size,
        operands=1,
    )(orbitals)
    guests = exchanged(packed)
    tables = spectral_tables(points)
    (response,) = call(
        response_kernel,
        "response",
        [shape((lines, points, padded), F32)],
        4 * lines * points**3,
        4 * lines * points**2,
        operands=2,
    )(coulomb, tables)
    blocks = len(guests) + 1
    high, parts = call(
        functools.partial(image_kernel, members),
        "image",
        [
            shape((packs, points, LANES), BF16),
            shape((2 * packs, points, LANES), BF16),
        ],
        2 * lines * points * padded * (4 * LANES),
        4 * lines * points**2,
        scalars=1,
        operands=blocks + 1,
    )(occupied, packed, *guests, response)
    (overlap,) = call(
        overlap_kernel,
        "overlap",
        [shape((members, LANES), F32)],
        4 * packs * points * LANES**2,
        8 * orbitals.size,
        operands=2,
    )(orbitals, parts)
    overlaps = [overlap] + [swapped(overlap, flip) for flip in range(1, groups)]
    images = [parts] + [swapped(parts, flip) for flip in range(1, near)]
    for grid in range(1, grids):
        across = swapped(high, grid * near)
        images += [across] + [swapped(across, flip) for flip in range(1, near)]
    cells = lines * groups * points

    intersection, weights = call(
        functools.partial(factor_kernel, cells),
        "factor",
        [shape((members, members), F32), shape((4 * CAP * span, 2 * LANES), BF16)],
        FACTOR_COST,
        members**2 * 4,
        operands=1 + groups,
    )(owners, *overlaps)
    routed, intersection = call(
        route_kernel,
        "route",
        [shape((CAP, groups * lines, points), BF16), shape((members, members), F32)],
        2 * CAP * members * groups * lines * points,
        6 * members * groups * lines * points,
        scratch=[
            pltpu.VMEM((groups, CAP, lines, points), BF16),
            pltpu.SemaphoreType.DMA((groups + 1,)),
        ],
        operands=2 + groups,
        remote=True,
    )(intersection, weights, *images)
    return routed[None, None], intersection[None]


def solution(mesh):
    in_specs = (P("band", ("grid", "ham"), None), P(("grid", "ham"), None), P(), P("band", None))
    out_specs = (P("band", ("grid", "ham"), None, None, None), P("band", None, None))
    return jax.shard_map(local, mesh=mesh, in_specs=in_specs, out_specs=out_specs, check_vma=False)
```

```python
import functools
import math

import jax
import jax.numpy as jnp
import numpy as np
from jax import lax
from jax.experimental import pallas as pl
from jax.experimental.pallas import tpu as pltpu
from jax.sharding import PartitionSpec as P

CAP = 8
LANES = 128
HIGHEST = lax.Precision.HIGHEST
VMEM_LIMIT = 48 * 1024 * 1024
FACTOR_COST = 3_000_000_000
NT = ((1,), (1,))
F32, BF16 = jnp.float32, jnp.bfloat16


def sources(block, count):
    odd = block % 2
    steps = (-2, 2 * odd - 1, 1 - 2 * odd, 2)
    return [(block + step + count) % count for step in steps]


def arrival(value, turn):
    count = lax.axis_size("band")
    assert count % 4 == 0
    pairs = [(sources(block, count)[turn], block) for block in range(count)]
    return lax.ppermute(value, "band", pairs)


def swapped(value, flip):
    count = lax.axis_size("grid") * lax.axis_size("ham")
    return lax.ppermute(value, ("grid", "ham"), [(group, group ^ flip) for group in range(count)])


def spectral_tables(points):
    midpoint = points // 2
    ids = np.arange(points)
    frequency = np.where(ids <= midpoint, ids, ids - midpoint)
    angles = (ids[:, None] * frequency[None, :] % points) * (2.0 * math.pi / points)
    forward = np.where((ids <= midpoint)[None, :], np.cos(angles), np.sin(angles))
    single = (frequency == 0) | (ids == midpoint)
    inverse = forward.T * (np.where(single, 1.0, 2.0) / points)[:, None]
    mirror = np.zeros((points, points))
    mirror[frequency, ids] += 0.5
    mirror[(points - frequency) % points, ids] += 0.5
    return jnp.asarray(np.stack([forward.T, inverse.T, mirror]).astype(np.float32)).astype(BF16)


def split(value):
    high = value.astype(BF16)
    return high, value - high.astype(F32)


def halves(value):
    high, rest = split(value)
    return high, rest.astype(BF16)


def dot32(a, b, contract=((1,), (0,))):
    return lax.dot_general(a, b, (contract, ((), ())), preferred_element_type=F32)


def dot_exact(a, b, contract=((1,), (0,))):
    return lax.dot_general(
        a, b, (contract, ((), ())), precision=HIGHEST, preferred_element_type=F32
    )


def ids(shape, axis):
    return lax.broadcasted_iota(jnp.int32, shape, axis)


def lane_member(lane, members):
    return lane % members


def lane_quarter(lane, turn):
    return (lane // (LANES // 4)) ^ turn


def lane_line(lane, turn, members):
    per = LANES // 4 // members
    return lane_quarter(lane, turn) * per + lane % (LANES // 4) // members


def own_turn(distance=0):
    return (lax.axis_index("band") + (4 - distance)) % 4


def rows_of(block, pack, span):
    members, _, points = block.shape
    part = block[:, pack * span : (pack + 1) * span, :]
    return part.reshape(members * span, points)


def pack_kernel(distance, orbitals_ref, out_ref):
    members = orbitals_ref.shape[0]
    span = LANES // members
    block = orbitals_ref[...].astype(F32)
    row, lane = ids((LANES, LANES), 0), ids((LANES, LANES), 1)
    source = lane_member(lane, members) * span + lane_line(lane, own_turn(distance), members)
    order = (row == source).astype(BF16)
    for pack in range(out_ref.shape[0]):
        rows = rows_of(block, pack, span).T.astype(BF16)
        out_ref[pack] = dot32(rows, order).astype(BF16)


def response_kernel(coulomb_ref, tables_ref, out_ref):
    points = coulomb_ref.shape[1]
    multiplier = dot_exact(coulomb_ref[...], tables_ref[2].astype(F32))
    forward = tables_ref[0]
    inverse = tables_ref[1].astype(F32)
    pad = jnp.zeros((points, out_ref.shape[2] - points), F32)
    for line in range(coulomb_ref.shape[0]):
        high, low = halves(inverse * multiplier[line : line + 1, :])
        out_ref[line, :, :points] = dot32(high, forward) + dot32(low, forward)
        out_ref[line, :, points:] = pad


def image_kernel(members, occupied_ref, *refs):
    blocks, (response_ref, high_ref, halves_ref) = refs[:-3], refs[-3:]
    packs, points, _ = blocks[0].shape
    padded = response_ref.shape[2]
    span = LANES // members
    per = span // 4
    total = lax.axis_size("band")
    position = lax.axis_index("band")
    places = [position] + sources(position, total)
    turns = [place % 4 for place in places]
    lane = ids((1, LANES), 1)
    own_line = lane_line(lane, turns[0], members)
    filled = [lane_member(lane, members) < occupied_ref[place] for place in places]
    quarters = [lane_quarter(lane, turn) for turn in turns]
    step = lane % (LANES // 4) // members
    apart, merged = 1, (0, 2, 3, 4)
    blank = jnp.zeros((padded - points, 2 * LANES), BF16)
    for pack in range(packs):
        tiles = [block[pack] for block in blocks]
        native = jnp.concatenate([tiles[0], blank[:, :LANES]], axis=0)
        image = jnp.zeros((points, LANES), F32)
        for quarter in range(4):
            here = [(q == quarter) for q in quarters]
            together = sum(tiles[m] * here[m].astype(F32).astype(BF16) for m in merged)
            window = jnp.concatenate([together, tiles[apart]], axis=1)
            occupied = sum((here[m] & filled[m]).astype(F32) for m in merged)
            beside = (here[apart] & filled[apart]).astype(F32)
            both = jnp.concatenate([occupied, beside], axis=1)
            steps = jnp.concatenate([step, step], axis=1)
            masked = jnp.concatenate(
                [window * jnp.where(steps == k, both, 0.0).astype(BF16) for k in range(per)], axis=0
            )
            gram = dot32(masked, jnp.concatenate([window, blank], axis=0), NT)
            first = pack * span + quarter * per
            response = response_ref[first : first + per].reshape(per * points, padded)
            high, low = halves(gram * response)
            fields = dot32(jnp.concatenate([high, low], axis=0), native)
            for k in range(per):
                a, b = k * points, (per + k) * points
                field = fields[a : a + points] + fields[b : b + points]
                image = jnp.where(own_line == quarter * per + k, field, image)
        high, low = halves(image)
        high_ref[pack] = high
        halves_ref[pack] = high
        halves_ref[packs + pack] = low


def overlap_kernel(orbitals_ref, halves_ref, out_ref):
    members, _, _ = orbitals_ref.shape
    span = LANES // members
    natives = orbitals_ref[...].astype(F32)
    square = (LANES, LANES)
    same_line = ids(square, 0) % span == lane_line(ids(square, 1), own_turn(), members)
    cross = jnp.zeros(square, F32)
    packs = halves_ref.shape[0] // 2
    for pack in range(packs):
        rows = rows_of(natives, pack, span).astype(BF16)
        both = jnp.concatenate([halves_ref[pack], halves_ref[packs + pack]], axis=1)
        product = dot32(rows, both)
        cross = cross + (product[:, :LANES] + product[:, LANES:])
    out_ref[...] = jnp.where(same_line, cross, 0.0).reshape(members, span, LANES).sum(axis=1)


def factor_kernel(cells, owners_ref, *refs):
    parts, (overlap_ref, weights_ref) = refs[:-2], refs[-2:]
    members = owners_ref.shape[0]
    span = LANES // members
    turn = own_turn()
    sums = [part[...] for part in parts]
    while len(sums) > 1:
        sums = [a + b for a, b in zip(sums[::2], sums[1::2])]
    high, rest = split(sums[0])
    pieces = [high, *halves(rest)]
    across = (members, LANES)
    gather = (ids(across, 0) == lane_member(ids(across, 1), members)).astype(BF16)
    overlap = sum(dot32(piece, gather, NT) for piece in pieces) * (1.0 / cells)
    flipped = sum(dot32(gather, piece, NT) for piece in pieces) * (1.0 / cells)
    overlap_ref[...] = overlap
    rows = CAP * span
    square = (members, members)
    group = lax.axis_index("grid") * lax.axis_size("ham") + lax.axis_index("ham")
    mine = (owners_ref[...] == group).astype(F32)
    eye = (ids(square, 0) == ids(square, 1)).astype(F32)
    mine_row = jnp.sum(mine * eye, axis=0, keepdims=True)
    before = (ids(square, 0) < ids(square, 1)).astype(F32)
    ranking = jnp.sum(mine * before, axis=0, keepdims=True)
    slot = (ids((rows, members), 0) // span).astype(F32)
    placed = (jnp.where(slot == ranking, 1.0, 0.0) * mine_row).astype(BF16)
    wide = (members, LANES)
    row = ids(wide, 0)
    upper = 0.5 * (overlap + flipped)
    columns = [jnp.broadcast_to(upper[:, j : j + 1], wide) for j in range(members)]
    lower = (row == lane_member(ids(wide, 1), members)).astype(F32)
    diagonal = ratio = jnp.zeros(wide, F32)
    for k in range(0, members, 2):
        first, second = columns[k], columns[k + 1]
        a, b, c = first[k : k + 1], first[k + 1 : k + 2], second[k + 1 : k + 2]
        share = b / a
        rest = c - share * b
        diagonal = jnp.where(row == k, a, jnp.where(row == k + 1, rest, diagonal))
        ratio = jnp.where(row == k + 1, share, ratio)
        scale = 1.0 / (a * c - b * b)
        below = row > k + 1
        one = jnp.where(below, (first * c - second * b) * scale, 0.0)
        two = jnp.where(below, (second * a - first * b) * scale, 0.0)
        lower = lower - (one * lower[k : k + 1] + two * lower[k + 1 : k + 2])
        for j in range(k + 2, members):
            column = columns[j]
            columns[j] = column - (one * column[k : k + 1] + two * column[k + 1 : k + 2])
    above = jnp.concatenate([lower[:1], lower[:-1]], axis=0)
    inverse = (lower - ratio * above) / jnp.sqrt(diagonal)
    high, low = halves(inverse)
    same_line = ids((rows, LANES), 0) % span == lane_line(ids((rows, LANES), 1), turn, members)
    blank = jnp.zeros((rows, LANES), BF16)
    chosen = [jnp.where(same_line, dot32(placed, half), 0.0).astype(BF16) for half in (high, low)]
    for i, half in enumerate(chosen + chosen):
        pair = [half, blank] if i < 2 else [blank, half]
        weights_ref[i * rows : (i + 1) * rows, :] = jnp.concatenate(pair, axis=1)


def route_kernel(overlap_ref, weights_ref, *refs):
    parts, (out_hbm, overlap_hbm, staged, semaphores) = refs[:-4], refs[-4:]
    groups = len(parts)
    copies = [pltpu.make_async_copy(overlap_ref, overlap_hbm, semaphores.at[groups])]
    copies[0].start()
    points = staged.shape[3]
    weights = weights_ref[...]
    rows = weights.shape[0] // 4
    span = rows // CAP
    lines = staged.shape[2]
    packs = lines // span
    highs = jnp.concatenate([weights[:rows], weights[2 * rows : 3 * rows]], axis=0)
    group = lax.axis_index("grid") * lax.axis_size("ham") + lax.axis_index("ham")
    for flip, part in enumerate(parts):
        sums = []
        for pack in range(0, packs, 2):
            field = jnp.concatenate([part[pack], part[pack + 1]], axis=1)
            both = dot32(weights, field, NT)
            results = [both[:rows] + both[rows : 2 * rows], both[2 * rows : 3 * rows] + both[3 * rows :]]
            if part.shape[0] > packs:
                place = packs + pack
                rest = dot32(highs, jnp.concatenate([part[place], part[place + 1]], axis=1), NT)
                results = [results[0] + rest[:rows], results[1] + rest[rows:]]
            sums += [result.reshape(CAP, span, points) for result in results]
        staged[flip] = jnp.concatenate(sums, axis=1).astype(BF16)
        start = pl.multiple_of((group ^ flip) * lines, lines)
        target = out_hbm.at[:, pl.ds(start, lines), :]
        copies.append(pltpu.make_async_copy(staged.at[flip], target, semaphores.at[flip]))
        copies[-1].start()
    for copy in copies:
        copy.wait()


def call(kernel, name, shapes, flops, moved, scratch=(), scalars=0, operands=0, remote=False):
    vmem = pl.BlockSpec(memory_space=pltpu.VMEM)
    smem = pl.BlockSpec(memory_space=pltpu.SMEM)
    return pl.pallas_call(
        kernel,
        name=name,
        out_shape=shapes,
        in_specs=[smem] * scalars + [vmem] * operands,
        out_specs=[pl.BlockSpec(memory_space=pl.ANY) if remote else vmem] * len(shapes),
        scratch_shapes=list(scratch),
        compiler_params=pltpu.CompilerParams(vmem_limit_bytes=VMEM_LIMIT),
        cost_estimate=pl.CostEstimate(flops=flops, bytes_accessed=moved, transcendentals=0),
    )


def local(orbitals, coulomb, occupied, owners):
    members, lines, points = orbitals.shape
    grids, near = lax.axis_size("grid"), lax.axis_size("ham")
    groups = grids * near
    padded = -(-points // LANES) * LANES
    span = LANES // members
    packs = lines // span
    assert packs % 2 == 0
    shape = jax.ShapeDtypeStruct

    def pack(block, distance):
        return call(
            functools.partial(pack_kernel, distance),
            "pack",
            [shape((packs, points, LANES), BF16)],
            orbitals.size,
            4 * orbitals.size,
            operands=1,
        )(block)[0]

    farthest = arrival(orbitals, 0)
    packed = pack(orbitals, 0)
    guests = [pack(farthest, 2)] + [arrival(packed, turn) for turn in range(1, 4)]
    tables = spectral_tables(points)
    (response,) = call(
        response_kernel,
        "response",
        [shape((lines, points, padded), F32)],
        4 * lines * points**3,
        4 * lines * points**2,
        operands=2,
    )(coulomb, tables)
    blocks = len(guests) + 1
    high, parts = call(
        functools.partial(image_kernel, members),
        "image",
        [
            shape((packs, points, LANES), BF16),
            shape((2 * packs, points, LANES), BF16),
        ],
        2 * lines * points * padded * (4 * LANES),
        4 * lines * points**2,
        scalars=1,
        operands=blocks + 1,
    )(occupied, packed, *guests, response)
    (overlap,) = call(
        overlap_kernel,
        "overlap",
        [shape((members, LANES), F32)],
        4 * packs * points * LANES**2,
        8 * orbitals.size,
        operands=2,
    )(orbitals, parts)
    overlaps = [overlap] + [swapped(overlap, flip) for flip in range(1, groups)]
    images = [parts] + [swapped(parts, flip) for flip in range(1, near)]
    for grid in range(1, grids):
        across = swapped(high, grid * near)
        images += [across] + [swapped(across, flip) for flip in range(1, near)]
    cells = lines * groups * points

    intersection, weights = call(
        functools.partial(factor_kernel, cells),
        "factor",
        [shape((members, members), F32), shape((4 * CAP * span, 2 * LANES), BF16)],
        FACTOR_COST,
        members**2 * 4,
        operands=1 + groups,
    )(owners, *overlaps)
    routed, intersection = call(
        route_kernel,
        "route",
        [shape((CAP, groups * lines, points), BF16), shape((members, members), F32)],
        2 * CAP * members * groups * lines * points,
        6 * members * groups * lines * points,
        scratch=[
            pltpu.VMEM((groups, CAP, lines, points), BF16),
            pltpu.SemaphoreType.DMA((groups + 1,)),
        ],
        operands=2 + groups,
        remote=True,
    )(intersection, weights, *images)
    return routed[None, None], intersection[None]


def solution(mesh):
    in_specs = (P("band", ("grid", "ham"), None), P(("grid", "ham"), None), P(), P("band", None))
    out_specs = (P("band", ("grid", "ham"), None, None, None), P("band", None, None))
    return jax.shard_map(local, mesh=mesh, in_specs=in_specs, out_specs=out_specs, check_vma=False)
```

```python
import functools
import math

import jax
import jax.numpy as jnp
import numpy as np
from jax import lax
from jax.experimental import pallas as pl
from jax.experimental.pallas import tpu as pltpu
from jax.sharding import PartitionSpec as P

CAP = 8
LANES = 128
HIGHEST = lax.Precision.HIGHEST
VMEM_LIMIT = 48 * 1024 * 1024
FACTOR_COST = 3_000_000_000
NT = ((1,), (1,))
F32, BF16 = jnp.float32, jnp.bfloat16


def sources(block, count):
    odd = block % 2
    steps = (-2, 2 * odd - 1, 1 - 2 * odd, 2)
    return [(block + step + count) % count for step in steps]


def exchanged(value):
    count = lax.axis_size("band")
    assert count % 4 == 0
    tables = [sources(block, count) for block in range(count)]
    return [
        lax.ppermute(value, "band", [(row[turn], block) for block, row in enumerate(tables)])
        for turn in range(4)
    ]


def swapped(value, flip):
    count = lax.axis_size("grid") * lax.axis_size("ham")
    return lax.ppermute(value, ("grid", "ham"), [(group, group ^ flip) for group in range(count)])


def spectral_tables(points):
    midpoint = points // 2
    ids = np.arange(points)
    frequency = np.where(ids <= midpoint, ids, ids - midpoint)
    angles = (ids[:, None] * frequency[None, :] % points) * (2.0 * math.pi / points)
    forward = np.where((ids <= midpoint)[None, :], np.cos(angles), np.sin(angles))
    single = (frequency == 0) | (ids == midpoint)
    inverse = forward.T * (np.where(single, 1.0, 2.0) / points)[:, None]
    mirror = np.zeros((points, points))
    mirror[frequency, ids] += 0.5
    mirror[(points - frequency) % points, ids] += 0.5
    rounded = [np.asarray(t, np.float32).astype(jnp.bfloat16) for t in (forward.T, inverse.T, mirror)]
    product = rounded[0].T.astype(np.float32) * rounded[1].astype(np.float32)
    high = product.astype(jnp.bfloat16)
    low = (product - high.astype(np.float32)).astype(jnp.bfloat16)
    return jnp.asarray(np.stack([*rounded, high, low]))


def split(value):
    high = value.astype(BF16)
    return high, value - high.astype(F32)


def halves(value):
    high, rest = split(value)
    return high, rest.astype(BF16)


def dot32(a, b, contract=((1,), (0,))):
    return lax.dot_general(a, b, (contract, ((), ())), preferred_element_type=F32)


def dot_exact(a, b, contract=((1,), (0,))):
    return lax.dot_general(
        a, b, (contract, ((), ())), precision=HIGHEST, preferred_element_type=F32
    )


def ids(shape, axis):
    return lax.broadcasted_iota(jnp.int32, shape, axis)


def lane_member(lane, members):
    return lane % members


def lane_quarter(lane, turn):
    return (lane // (LANES // 4)) ^ turn


def lane_line(lane, turn, members):
    per = LANES // 4 // members
    return lane_quarter(lane, turn) * per + lane % (LANES // 4) // members


def own_turn():
    return lax.axis_index("band") % 4


def rows_of(block, pack, span):
    members, _, points = block.shape
    part = block[:, pack * span : (pack + 1) * span, :]
    return part.reshape(members * span, points)


def pack_kernel(orbitals_ref, out_ref):
    members = orbitals_ref.shape[0]
    span = LANES // members
    block = orbitals_ref[...].astype(F32)
    row, lane = ids((LANES, LANES), 0), ids((LANES, LANES), 1)
    source = lane_member(lane, members) * span + lane_line(lane, own_turn(), members)
    order = (row == source).astype(BF16)
    for pack in range(out_ref.shape[0]):
        rows = rows_of(block, pack, span).T.astype(BF16)
        out_ref[pack] = dot32(rows, order).astype(BF16)


def response_kernel(members, coulomb_ref, tables_ref, out_ref, diagonal_ref):
    points = coulomb_ref.shape[1]
    lines = coulomb_ref.shape[0]
    span = LANES // members
    multiplier = dot_exact(coulomb_ref[...], tables_ref[2].astype(F32))
    forward = tables_ref[0]
    inverse = tables_ref[1].astype(F32)
    pad = jnp.zeros((points, out_ref.shape[2] - points), F32)
    apart = ids((points, points), 0) != ids((points, points), 1)
    for line in range(lines):
        high, low = halves(inverse * multiplier[line : line + 1, :])
        whole = dot32(high, forward) + dot32(low, forward)
        out_ref[line, :, :points] = jnp.where(apart, whole, 0.0)
        out_ref[line, :, points:] = pad
    parts = halves(multiplier)
    for pack in range(diagonal_ref.shape[0]):
        line = ids((LANES, lines), 1) - pack * span
        repeat = (lane_line(ids((LANES, lines), 0), own_turn(), members) == line).astype(BF16)
        high, low = [dot32(repeat, part).astype(BF16) for part in parts]
        diagonal_ref[pack] = dot32(tables_ref[3], high, NT) + (
            dot32(tables_ref[3], low, NT) + dot32(tables_ref[4], high, NT)
        )


def image_kernel(members, occupied_ref, *refs):
    blocks, (response_ref, diagonal_ref, high_ref, halves_ref) = refs[:-4], refs[-4:]
    packs, points, _ = blocks[0].shape
    padded = response_ref.shape[2]
    span = LANES // members
    per = span // 4
    total = lax.axis_size("band")
    position = lax.axis_index("band")
    places = [position] + sources(position, total)
    turns = [place % 4 for place in places]
    lane = ids((1, LANES), 1)
    own_line = lane_line(lane, turns[0], members)
    filled = [lane_member(lane, members) < occupied_ref[place] for place in places]
    quarters = [lane_quarter(lane, turn) for turn in turns]
    step = lane % (LANES // 4) // members
    steps = jnp.concatenate([step, step], axis=1)
    pair = (2 * LANES, LANES)
    same_step = (
        ids(pair, 0) % (LANES // 4) // members == ids(pair, 1) % (LANES // 4) // members
    ).astype(BF16)
    apart, merged = 1, (0, 2, 3, 4)
    blank = jnp.zeros((padded - points, 2 * LANES), BF16)
    for pack in range(packs):
        tiles = [block[pack] for block in blocks]
        native = jnp.concatenate([tiles[0], blank[:, :LANES]], axis=0)
        image = jnp.zeros((points, LANES), F32)
        squares = jnp.zeros((points, LANES), F32)
        for quarter in range(4):
            here = [(q == quarter) for q in quarters]
            together = sum(tiles[m] * here[m].astype(F32).astype(BF16) for m in merged)
            window = jnp.concatenate([together, tiles[apart]], axis=1)
            occupied = sum((here[m] & filled[m]).astype(F32) for m in merged)
            beside = (here[apart] & filled[apart]).astype(F32)
            both = jnp.concatenate([occupied, beside], axis=1)
            used = window * both.astype(BF16)
            square = dot32(used * window, same_step)
            squares = jnp.where(own_line // per == quarter, square, squares)
            masked = jnp.concatenate(
                [used * (steps == k).astype(F32).astype(BF16) for k in range(per)], axis=0
            )
            gram = dot32(masked, jnp.concatenate([window, blank], axis=0), NT)
            first = pack * span + quarter * per
            response = response_ref[first : first + per].reshape(per * points, padded)
            fields = dot32((gram * response).astype(BF16), native)
            for k in range(per):
                field = fields[k * points : (k + 1) * points]
                image = jnp.where(own_line == quarter * per + k, field, image)
        image = image + tiles[0].astype(F32) * (diagonal_ref[pack] * squares)
        high, low = halves(image)
        high_ref[pack] = high
        halves_ref[pack] = high
        halves_ref[packs + pack] = low


def overlap_kernel(orbitals_ref, halves_ref, out_ref):
    members, _, _ = orbitals_ref.shape
    span = LANES // members
    natives = orbitals_ref[...].astype(F32)
    square = (LANES, LANES)
    same_line = ids(square, 0) % span == lane_line(ids(square, 1), own_turn(), members)
    cross = jnp.zeros(square, F32)
    packs = halves_ref.shape[0] // 2
    for pack in range(packs):
        rows = rows_of(natives, pack, span).astype(BF16)
        both = jnp.concatenate([halves_ref[pack], halves_ref[packs + pack]], axis=1)
        product = dot32(rows, both)
        cross = cross + (product[:, :LANES] + product[:, LANES:])
    out_ref[...] = jnp.where(same_line, cross, 0.0).reshape(members, span, LANES).sum(axis=1)


def factor_kernel(cells, owners_ref, *refs):
    parts, (overlap_ref, weights_ref) = refs[:-2], refs[-2:]
    members = owners_ref.shape[0]
    span = LANES // members
    turn = own_turn()
    sums = [part[...] for part in parts]
    while len(sums) > 1:
        sums = [a + b for a, b in zip(sums[::2], sums[1::2])]
    high, rest = split(sums[0])
    pieces = [high, *halves(rest)]
    across = (members, LANES)
    gather = (ids(across, 0) == lane_member(ids(across, 1), members)).astype(BF16)
    overlap = sum(dot32(piece, gather, NT) for piece in pieces) * (1.0 / cells)
    flipped = sum(dot32(gather, piece, NT) for piece in pieces) * (1.0 / cells)
    overlap_ref[...] = overlap
    rows = CAP * span
    square = (members, members)
    group = lax.axis_index("grid") * lax.axis_size("ham") + lax.axis_index("ham")
    mine = (owners_ref[...] == group).astype(F32)
    eye = (ids(square, 0) == ids(square, 1)).astype(F32)
    mine_row = jnp.sum(mine * eye, axis=0, keepdims=True)
    before = (ids(square, 0) < ids(square, 1)).astype(F32)
    ranking = jnp.sum(mine * before, axis=0, keepdims=True)
    slot = (ids((rows, members), 0) // span).astype(F32)
    placed = (jnp.where(slot == ranking, 1.0, 0.0) * mine_row).astype(BF16)
    wide = (members, LANES)
    row = ids(wide, 0)
    upper = 0.5 * (overlap + flipped)
    columns = [jnp.broadcast_to(upper[:, j : j + 1], wide) for j in range(members)]
    lower = (row == lane_member(ids(wide, 1), members)).astype(F32)
    diagonal = ratio = jnp.zeros(wide, F32)
    for k in range(0, members, 2):
        first, second = columns[k], columns[k + 1]
        a, b, c = first[k : k + 1], first[k + 1 : k + 2], second[k + 1 : k + 2]
        share = b / a
        rest = c - share * b
        diagonal = jnp.where(row == k, a, jnp.where(row == k + 1, rest, diagonal))
        ratio = jnp.where(row == k + 1, share, ratio)
        scale = 1.0 / (a * c - b * b)
        below = row > k + 1
        one = jnp.where(below, (first * c - second * b) * scale, 0.0)
        two = jnp.where(below, (second * a - first * b) * scale, 0.0)
        lower = lower - (one * lower[k : k + 1] + two * lower[k + 1 : k + 2])
        for j in range(k + 2, members):
            column = columns[j]
            columns[j] = column - (one * column[k : k + 1] + two * column[k + 1 : k + 2])
    above = jnp.concatenate([lower[:1], lower[:-1]], axis=0)
    inverse = (lower - ratio * above) / jnp.sqrt(diagonal)
    high, low = halves(inverse)
    same_line = ids((rows, LANES), 0) % span == lane_line(ids((rows, LANES), 1), turn, members)
    blank = jnp.zeros((rows, LANES), BF16)
    chosen = [jnp.where(same_line, dot32(placed, half), 0.0).astype(BF16) for half in (high, low)]
    for i, half in enumerate(chosen + chosen):
        pair = [half, blank] if i < 2 else [blank, half]
        weights_ref[i * rows : (i + 1) * rows, :] = jnp.concatenate(pair, axis=1)


def route_kernel(overlap_ref, weights_ref, *refs):
    parts, (out_hbm, overlap_hbm, staged, semaphores) = refs[:-4], refs[-4:]
    groups = len(parts)
    copies = [pltpu.make_async_copy(overlap_ref, overlap_hbm, semaphores.at[groups])]
    copies[0].start()
    points = staged.shape[3]
    weights = weights_ref[...]
    rows = weights.shape[0] // 4
    span = rows // CAP
    lines = staged.shape[2]
    packs = lines // span
    highs = jnp.concatenate([weights[:rows], weights[2 * rows : 3 * rows]], axis=0)
    group = lax.axis_index("grid") * lax.axis_size("ham") + lax.axis_index("ham")
    for flip, part in enumerate(parts):
        sums = []
        for pack in range(0, packs, 2):
            field = jnp.concatenate([part[pack], part[pack + 1]], axis=1)
            both = dot32(weights, field, NT)
            results = [both[:rows] + both[rows : 2 * rows], both[2 * rows : 3 * rows] + both[3 * rows :]]
            if part.shape[0] > packs:
                place = packs + pack
                rest = dot32(highs, jnp.concatenate([part[place], part[place + 1]], axis=1), NT)
                results = [results[0] + rest[:rows], results[1] + rest[rows:]]
            sums += [result.reshape(CAP, span, points) for result in results]
        staged[flip] = jnp.concatenate(sums, axis=1).astype(BF16)
        start = pl.multiple_of((group ^ flip) * lines, lines)
        target = out_hbm.at[:, pl.ds(start, lines), :]
        copies.append(pltpu.make_async_copy(staged.at[flip], target, semaphores.at[flip]))
        copies[-1].start()
    for copy in copies:
        copy.wait()


def call(kernel, name, shapes, flops, moved, scratch=(), scalars=0, operands=0, remote=False):
    vmem = pl.BlockSpec(memory_space=pltpu.VMEM)
    smem = pl.BlockSpec(memory_space=pltpu.SMEM)
    return pl.pallas_call(
        kernel,
        name=name,
        out_shape=shapes,
        in_specs=[smem] * scalars + [vmem] * operands,
        out_specs=[pl.BlockSpec(memory_space=pl.ANY) if remote else vmem] * len(shapes),
        scratch_shapes=list(scratch),
        compiler_params=pltpu.CompilerParams(vmem_limit_bytes=VMEM_LIMIT),
        cost_estimate=pl.CostEstimate(flops=flops, bytes_accessed=moved, transcendentals=0),
    )


def local(orbitals, coulomb, occupied, owners):
    members, lines, points = orbitals.shape
    grids, near = lax.axis_size("grid"), lax.axis_size("ham")
    groups = grids * near
    padded = -(-points // LANES) * LANES
    span = LANES // members
    packs = lines // span
    assert packs % 2 == 0
    shape = jax.ShapeDtypeStruct
    (packed,) = call(
        pack_kernel,
        "pack",
        [shape((packs, points, LANES), BF16)],
        orbitals.size,
        4 * orbitals.size,
        operands=1,
    )(orbitals)
    guests = exchanged(packed)
    tables = spectral_tables(points)
    response, diagonal = call(
        functools.partial(response_kernel, members),
        "response",
        [shape((lines, points, padded), F32), shape((packs, points, LANES), F32)],
        4 * lines * points**3,
        4 * lines * points**2,
        operands=2,
    )(coulomb, tables)
    blocks = len(guests) + 1
    high, parts = call(
        functools.partial(image_kernel, members),
        "image",
        [
            shape((packs, points, LANES), BF16),
            shape((2 * packs, points, LANES), BF16),
        ],
        2 * lines * points * padded * (3 * LANES),
        4 * lines * points**2,
        scalars=1,
        operands=blocks + 2,
    )(occupied, packed, *guests, response, diagonal)
    (overlap,) = call(
        overlap_kernel,
        "overlap",
        [shape((members, LANES), F32)],
        4 * packs * points * LANES**2,
        8 * orbitals.size,
        operands=2,
    )(orbitals, parts)
    overlaps = [overlap] + [swapped(overlap, flip) for flip in range(1, groups)]
    images = [parts] + [swapped(parts, flip) for flip in range(1, near)]
    for grid in range(1, grids):
        across = swapped(high, grid * near)
        images += [across] + [swapped(across, flip) for flip in range(1, near)]
    cells = lines * groups * points

    intersection, weights = call(
        functools.partial(factor_kernel, cells),
        "factor",
        [shape((members, members), F32), shape((4 * CAP * span, 2 * LANES), BF16)],
        FACTOR_COST,
        members**2 * 4,
        operands=1 + groups,
    )(owners, *overlaps)
    routed, intersection = call(
        route_kernel,
        "route",
        [shape((CAP, groups * lines, points), BF16), shape((members, members), F32)],
        2 * CAP * members * groups * lines * points,
        6 * members * groups * lines * points,
        scratch=[
            pltpu.VMEM((groups, CAP, lines, points), BF16),
            pltpu.SemaphoreType.DMA((groups + 1,)),
        ],
        operands=2 + groups,
        remote=True,
    )(intersection, weights, *images)
    return routed[None, None], intersection[None]


def solution(mesh):
    in_specs = (P("band", ("grid", "ham"), None), P(("grid", "ham"), None), P(), P("band", None))
    out_specs = (P("band", ("grid", "ham"), None, None, None), P("band", None, None))
    return jax.shard_map(local, mesh=mesh, in_specs=in_specs, out_specs=out_specs, check_vma=False)
```

```python
import functools
import math

import jax
import jax.numpy as jnp
import numpy as np
from jax import lax
from jax.experimental import pallas as pl
from jax.experimental.pallas import tpu as pltpu
from jax.sharding import PartitionSpec as P

CAP = 8
LANES = 128
HIGHEST = lax.Precision.HIGHEST
VMEM_LIMIT = 48 * 1024 * 1024
FACTOR_COST = 3_000_000_000
NT = ((1,), (1,))
F32, BF16 = jnp.float32, jnp.bfloat16


def sources(block, count):
    odd = block % 2
    steps = (-2, 2 * odd - 1, 1 - 2 * odd, 2)
    return [(block + step + count) % count for step in steps]


def exchanged(value):
    count = lax.axis_size("band")
    assert count % 4 == 0
    tables = [sources(block, count) for block in range(count)]
    return [
        lax.ppermute(value, "band", [(row[turn], block) for block, row in enumerate(tables)])
        for turn in range(4)
    ]


def swapped(value, flip):
    count = lax.axis_size("grid") * lax.axis_size("ham")
    return lax.ppermute(value, ("grid", "ham"), [(group, group ^ flip) for group in range(count)])


def spectral_tables(points):
    midpoint = points // 2
    ids = np.arange(points)
    frequency = np.where(ids <= midpoint, ids, ids - midpoint)
    angles = (ids[:, None] * frequency[None, :] % points) * (2.0 * math.pi / points)
    forward = np.where((ids <= midpoint)[None, :], np.cos(angles), np.sin(angles))
    single = (frequency == 0) | (ids == midpoint)
    inverse = forward.T * (np.where(single, 1.0, 2.0) / points)[:, None]
    mirror = np.zeros((points, points))
    mirror[frequency, ids] += 0.5
    mirror[(points - frequency) % points, ids] += 0.5
    return jnp.asarray(np.stack([forward.T, inverse.T, mirror]).astype(np.float32)).astype(BF16)


def split(value):
    high = value.astype(BF16)
    return high, value - high.astype(F32)


def halves(value):
    high, rest = split(value)
    return high, rest.astype(BF16)


def dot32(a, b, contract=((1,), (0,))):
    return lax.dot_general(a, b, (contract, ((), ())), preferred_element_type=F32)


def dot_exact(a, b, contract=((1,), (0,))):
    return lax.dot_general(
        a, b, (contract, ((), ())), precision=HIGHEST, preferred_element_type=F32
    )


def ids(shape, axis):
    return lax.broadcasted_iota(jnp.int32, shape, axis)


def lane_member(lane, members):
    return lane % members


def lane_quarter(lane, turn):
    return (lane // (LANES // 4)) ^ turn


def lane_line(lane, turn, members):
    per = LANES // 4 // members
    return lane_quarter(lane, turn) * per + lane % (LANES // 4) // members


def own_turn():
    return lax.axis_index("band") % 4


def rows_of(block, pack, span):
    members, _, points = block.shape
    part = block[:, pack * span : (pack + 1) * span, :]
    return part.reshape(members * span, points)


def pack_kernel(orbitals_ref, out_ref):
    members = orbitals_ref.shape[0]
    span = LANES // members
    block = orbitals_ref[...].astype(F32)
    row, lane = ids((LANES, LANES), 0), ids((LANES, LANES), 1)
    source = lane_member(lane, members) * span + lane_line(lane, own_turn(), members)
    order = (row == source).astype(BF16)
    for pack in range(out_ref.shape[0]):
        rows = rows_of(block, pack, span).T.astype(BF16)
        out_ref[pack] = dot32(rows, order).astype(BF16)


def response_kernel(coulomb_ref, tables_ref, out_ref):
    points = coulomb_ref.shape[1]
    multiplier = dot_exact(coulomb_ref[...], tables_ref[2].astype(F32))
    forward = tables_ref[0]
    inverse = tables_ref[1].astype(F32)
    pad = jnp.zeros((points, out_ref.shape[2] - points), F32)
    for line in range(coulomb_ref.shape[0]):
        high, low = halves(inverse * multiplier[line : line + 1, :])
        out_ref[line, :, :points] = dot32(high, forward) + dot32(low, forward)
        out_ref[line, :, points:] = pad


def image_kernel(members, occupied_ref, *refs):
    blocks, (response_ref, high_ref, halves_ref) = refs[:-3], refs[-3:]
    packs, points, _ = blocks[0].shape
    padded = response_ref.shape[2]
    span = LANES // members
    per = span // 4
    total = lax.axis_size("band")
    position = lax.axis_index("band")
    places = [position] + sources(position, total)
    turns = [place % 4 for place in places]
    lane = ids((1, LANES), 1)
    own_line = lane_line(lane, turns[0], members)
    filled = [lane_member(lane, members) < occupied_ref[place] for place in places]
    quarters = [lane_quarter(lane, turn) for turn in turns]
    step = lane % (LANES // 4) // members
    apart, merged = 1, (0, 2, 3, 4)
    blank = jnp.zeros((padded - points, 2 * LANES), BF16)
    for pack in range(packs):
        tiles = [block[pack] for block in blocks]
        native = jnp.concatenate([tiles[0], blank[:, :LANES]], axis=0)
        kernels = []
        for quarter in range(4):
            here = [(q == quarter) for q in quarters]
            together = sum(tiles[m] * here[m].astype(F32).astype(BF16) for m in merged)
            window = jnp.concatenate([together, tiles[apart]], axis=1)
            occupied = sum((here[m] & filled[m]).astype(F32) for m in merged)
            beside = (here[apart] & filled[apart]).astype(F32)
            both = jnp.concatenate([occupied, beside], axis=1)
            steps = jnp.concatenate([step, step], axis=1)
            masked = jnp.concatenate(
                [window * jnp.where(steps == k, both, 0.0).astype(BF16) for k in range(per)], axis=0
            )
            gram = dot32(masked, jnp.concatenate([window, blank], axis=0), NT)
            first = pack * span + quarter * per
            response = response_ref[first : first + per].reshape(per * points, padded)
            kernels += halves(gram * response)
        fields = dot32(jnp.concatenate(kernels, axis=0), native)
        image = jnp.zeros((points, LANES), F32)
        for line in range(span):
            a = (line // per * 2 * per + line % per) * points
            b = a + per * points
            field = fields[a : a + points] + fields[b : b + points]
            image = jnp.where(own_line == line, field, image)
        high, low = halves(image)
        high_ref[pack] = high
        halves_ref[pack] = high
        halves_ref[packs + pack] = low


def overlap_kernel(orbitals_ref, halves_ref, out_ref):
    members, _, _ = orbitals_ref.shape
    span = LANES // members
    natives = orbitals_ref[...].astype(F32)
    square = (LANES, LANES)
    same_line = ids(square, 0) % span == lane_line(ids(square, 1), own_turn(), members)
    cross = jnp.zeros(square, F32)
    packs = halves_ref.shape[0] // 2
    for pack in range(packs):
        rows = rows_of(natives, pack, span).astype(BF16)
        both = jnp.concatenate([halves_ref[pack], halves_ref[packs + pack]], axis=1)
        product = dot32(rows, both)
        cross = cross + (product[:, :LANES] + product[:, LANES:])
    out_ref[...] = jnp.where(same_line, cross, 0.0).reshape(members, span, LANES).sum(axis=1)


def factor_kernel(cells, owners_ref, *refs):
    parts, (overlap_ref, weights_ref) = refs[:-2], refs[-2:]
    members = owners_ref.shape[0]
    span = LANES // members
    turn = own_turn()
    sums = [part[...] for part in parts]
    while len(sums) > 1:
        sums = [a + b for a, b in zip(sums[::2], sums[1::2])]
    high, rest = split(sums[0])
    pieces = [high, *halves(rest)]
    across = (members, LANES)
    gather = (ids(across, 0) == lane_member(ids(across, 1), members)).astype(BF16)
    overlap = sum(dot32(piece, gather, NT) for piece in pieces) * (1.0 / cells)
    flipped = sum(dot32(gather, piece, NT) for piece in pieces) * (1.0 / cells)
    overlap_ref[...] = overlap
    rows = CAP * span
    square = (members, members)
    group = lax.axis_index("grid") * lax.axis_size("ham") + lax.axis_index("ham")
    mine = (owners_ref[...] == group).astype(F32)
    eye = (ids(square, 0) == ids(square, 1)).astype(F32)
    mine_row = jnp.sum(mine * eye, axis=0, keepdims=True)
    before = (ids(square, 0) < ids(square, 1)).astype(F32)
    ranking = jnp.sum(mine * before, axis=0, keepdims=True)
    slot = (ids((rows, members), 0) // span).astype(F32)
    placed = (jnp.where(slot == ranking, 1.0, 0.0) * mine_row).astype(BF16)
    wide = (members, LANES)
    row = ids(wide, 0)
    upper = 0.5 * (overlap + flipped)
    columns = [jnp.broadcast_to(upper[:, j : j + 1], wide) for j in range(members)]
    lower = (row == lane_member(ids(wide, 1), members)).astype(F32)
    diagonal = ratio = jnp.zeros(wide, F32)
    for k in range(0, members, 2):
        first, second = columns[k], columns[k + 1]
        a, b, c = first[k : k + 1], first[k + 1 : k + 2], second[k + 1 : k + 2]
        share = b / a
        rest = c - share * b
        diagonal = jnp.where(row == k, a, jnp.where(row == k + 1, rest, diagonal))
        ratio = jnp.where(row == k + 1, share, ratio)
        scale = 1.0 / (a * c - b * b)
        below = row > k + 1
        one = jnp.where(below, (first * c - second * b) * scale, 0.0)
        two = jnp.where(below, (second * a - first * b) * scale, 0.0)
        lower = lower - (one * lower[k : k + 1] + two * lower[k + 1 : k + 2])
        for j in range(k + 2, members):
            column = columns[j]
            columns[j] = column - (one * column[k : k + 1] + two * column[k + 1 : k + 2])
    above = jnp.concatenate([lower[:1], lower[:-1]], axis=0)
    inverse = (lower - ratio * above) / jnp.sqrt(diagonal)
    high, low = halves(inverse)
    same_line = ids((rows, LANES), 0) % span == lane_line(ids((rows, LANES), 1), turn, members)
    blank = jnp.zeros((rows, LANES), BF16)
    chosen = [jnp.where(same_line, dot32(placed, half), 0.0).astype(BF16) for half in (high, low)]
    for i, half in enumerate(chosen + chosen):
        pair = [half, blank] if i < 2 else [blank, half]
        weights_ref[i * rows : (i + 1) * rows, :] = jnp.concatenate(pair, axis=1)


def route_kernel(overlap_ref, weights_ref, *refs):
    parts, (out_hbm, overlap_hbm, staged, semaphores) = refs[:-4], refs[-4:]
    groups = len(parts)
    copies = [pltpu.make_async_copy(overlap_ref, overlap_hbm, semaphores.at[groups])]
    copies[0].start()
    points = staged.shape[3]
    weights = weights_ref[...]
    rows = weights.shape[0] // 4
    span = rows // CAP
    lines = staged.shape[2]
    packs = lines // span
    highs = jnp.concatenate([weights[:rows], weights[2 * rows : 3 * rows]], axis=0)
    group = lax.axis_index("grid") * lax.axis_size("ham") + lax.axis_index("ham")
    for flip, part in enumerate(parts):
        sums = []
        for pack in range(0, packs, 2):
            field = jnp.concatenate([part[pack], part[pack + 1]], axis=1)
            both = dot32(weights, field, NT)
            results = [both[:rows] + both[rows : 2 * rows], both[2 * rows : 3 * rows] + both[3 * rows :]]
            if part.shape[0] > packs:
                place = packs + pack
                rest = dot32(highs, jnp.concatenate([part[place], part[place + 1]], axis=1), NT)
                results = [results[0] + rest[:rows], results[1] + rest[rows:]]
            sums += [result.reshape(CAP, span, points) for result in results]
        staged[flip] = jnp.concatenate(sums, axis=1).astype(BF16)
        start = pl.multiple_of((group ^ flip) * lines, lines)
        target = out_hbm.at[:, pl.ds(start, lines), :]
        copies.append(pltpu.make_async_copy(staged.at[flip], target, semaphores.at[flip]))
        copies[-1].start()
    for copy in copies:
        copy.wait()


def call(kernel, name, shapes, flops, moved, scratch=(), scalars=0, operands=0, remote=False):
    vmem = pl.BlockSpec(memory_space=pltpu.VMEM)
    smem = pl.BlockSpec(memory_space=pltpu.SMEM)
    return pl.pallas_call(
        kernel,
        name=name,
        out_shape=shapes,
        in_specs=[smem] * scalars + [vmem] * operands,
        out_specs=[pl.BlockSpec(memory_space=pl.ANY) if remote else vmem] * len(shapes),
        scratch_shapes=list(scratch),
        compiler_params=pltpu.CompilerParams(vmem_limit_bytes=VMEM_LIMIT),
        cost_estimate=pl.CostEstimate(flops=flops, bytes_accessed=moved, transcendentals=0),
    )


def local(orbitals, coulomb, occupied, owners):
    members, lines, points = orbitals.shape
    grids, near = lax.axis_size("grid"), lax.axis_size("ham")
    groups = grids * near
    padded = -(-points // LANES) * LANES
    span = LANES // members
    packs = lines // span
    assert packs % 2 == 0
    shape = jax.ShapeDtypeStruct
    (packed,) = call(
        pack_kernel,
        "pack",
        [shape((packs, points, LANES), BF16)],
        orbitals.size,
        4 * orbitals.size,
        operands=1,
    )(orbitals)
    guests = exchanged(packed)
    tables = spectral_tables(points)
    (response,) = call(
        response_kernel,
        "response",
        [shape((lines, points, padded), F32)],
        4 * lines * points**3,
        4 * lines * points**2,
        operands=2,
    )(coulomb, tables)
    blocks = len(guests) + 1
    high, parts = call(
        functools.partial(image_kernel, members),
        "image",
        [
            shape((packs, points, LANES), BF16),
            shape((2 * packs, points, LANES), BF16),
        ],
        2 * lines * points * padded * (4 * LANES),
        4 * lines * points**2,
        scalars=1,
        operands=blocks + 1,
    )(occupied, packed, *guests, response)
    (overlap,) = call(
        overlap_kernel,
        "overlap",
        [shape((members, LANES), F32)],
        4 * packs * points * LANES**2,
        8 * orbitals.size,
        operands=2,
    )(orbitals, parts)
    overlaps = [overlap] + [swapped(overlap, flip) for flip in range(1, groups)]
    images = [parts] + [swapped(parts, flip) for flip in range(1, near)]
    for grid in range(1, grids):
        across = swapped(high, grid * near)
        images += [across] + [swapped(across, flip) for flip in range(1, near)]
    cells = lines * groups * points

    intersection, weights = call(
        functools.partial(factor_kernel, cells),
        "factor",
        [shape((members, members), F32), shape((4 * CAP * span, 2 * LANES), BF16)],
        FACTOR_COST,
        members**2 * 4,
        operands=1 + groups,
    )(owners, *overlaps)
    routed, intersection = call(
        route_kernel,
        "route",
        [shape((CAP, groups * lines, points), BF16), shape((members, members), F32)],
        2 * CAP * members * groups * lines * points,
        6 * members * groups * lines * points,
        scratch=[
            pltpu.VMEM((groups, CAP, lines, points), BF16),
            pltpu.SemaphoreType.DMA((groups + 1,)),
        ],
        operands=2 + groups,
        remote=True,
    )(intersection, weights, *images)
    return routed[None, None], intersection[None]


def solution(mesh):
    in_specs = (P("band", ("grid", "ham"), None), P(("grid", "ham"), None), P(), P("band", None))
    out_specs = (P("band", ("grid", "ham"), None, None, None), P("band", None, None))
    return jax.shard_map(local, mesh=mesh, in_specs=in_specs, out_specs=out_specs, check_vma=False)
```

```python
import functools
import math

import jax
import jax.numpy as jnp
import numpy as np
from jax import lax
from jax.experimental import pallas as pl
from jax.experimental.pallas import tpu as pltpu
from jax.sharding import PartitionSpec as P

CAP = 8
LANES = 128
PIECES = 4
HIGHEST = lax.Precision.HIGHEST
VMEM_LIMIT = 48 * 1024 * 1024
PACK_LIMIT = 55040 * 1024
FACTOR_COST = 3_000_000_000
NT = ((1,), (1,))
F32, BF16 = jnp.float32, jnp.bfloat16


def sources(block, count):
    odd = block % 2
    steps = (-2, 2 * odd - 1, 1 - 2 * odd, 2)
    return [(block + step + count) % count for step in steps]


def exchanged(value):
    count = lax.axis_size("band")
    assert count % 4 == 0
    tables = [sources(block, count) for block in range(count)]
    return [
        lax.ppermute(value, "band", [(row[turn], block) for block, row in enumerate(tables)])
        for turn in range(4)
    ]


def swapped(value, flip):
    count = lax.axis_size("grid") * lax.axis_size("ham")
    return lax.ppermute(value, ("grid", "ham"), [(group, group ^ flip) for group in range(count)])


def spectral_tables(points):
    midpoint = points // 2
    ids = np.arange(points)
    frequency = np.where(ids <= midpoint, ids, ids - midpoint)
    angles = (ids[:, None] * frequency[None, :] % points) * (2.0 * math.pi / points)
    forward = np.where((ids <= midpoint)[None, :], np.cos(angles), np.sin(angles))
    single = (frequency == 0) | (ids == midpoint)
    inverse = forward.T * (np.where(single, 1.0, 2.0) / points)[:, None]
    mirror = np.zeros((points, points))
    mirror[frequency, ids] += 0.5
    mirror[(points - frequency) % points, ids] += 0.5
    return jnp.asarray(np.stack([forward.T, inverse.T, mirror]).astype(np.float32)).astype(BF16)


def split(value):
    high = value.astype(BF16)
    return high, value - high.astype(F32)


def halves(value):
    high, rest = split(value)
    return high, rest.astype(BF16)


def dot32(a, b, contract=((1,), (0,))):
    return lax.dot_general(a, b, (contract, ((), ())), preferred_element_type=F32)


def dot_exact(a, b, contract=((1,), (0,))):
    return lax.dot_general(
        a, b, (contract, ((), ())), precision=HIGHEST, preferred_element_type=F32
    )


def ids(shape, axis):
    return lax.broadcasted_iota(jnp.int32, shape, axis)


def lane_member(lane, members):
    return lane % members


def lane_quarter(lane, turn):
    return (lane // (LANES // 4)) ^ turn


def lane_line(lane, turn, members):
    per = LANES // 4 // members
    return lane_quarter(lane, turn) * per + lane % (LANES // 4) // members


def own_turn():
    return lax.axis_index("band") % 4


def rows_of(block, pack, span):
    members, _, points = block.shape
    part = block[:, pack * span : (pack + 1) * span, :]
    return part.reshape(members * span, points)


def pack_kernel(orbitals_hbm, out_ref, orbitals_ref, semaphores):
    members = orbitals_ref.shape[0]
    span = LANES // members
    row, lane = ids((LANES, LANES), 0), ids((LANES, LANES), 1)
    source = lane_member(lane, members) * span + lane_line(lane, own_turn(), members)
    order = (row == source).astype(BF16)
    copies = []
    for pack in range(out_ref.shape[0]):
        for part in range(PIECES):
            size = members // PIECES
            place = (pl.ds(part * size, size), pl.ds(pack * span, span))
            semaphore = semaphores.at[pack * PIECES + part]
            copies.append(
                pltpu.make_async_copy(orbitals_hbm.at[place], orbitals_ref.at[place], semaphore)
            )
            copies[-1].start()
    for pack in range(out_ref.shape[0]):
        for copy in copies[pack * PIECES : (pack + 1) * PIECES]:
            copy.wait()
        block = orbitals_ref[:, pack * span : (pack + 1) * span, :].astype(F32)
        rows = block.reshape(members * span, -1).T.astype(BF16)
        out_ref[pack] = dot32(rows, order).astype(BF16)


def response_kernel(coulomb_ref, tables_ref, out_ref):
    points = coulomb_ref.shape[1]
    multiplier = dot_exact(coulomb_ref[...], tables_ref[2].astype(F32))
    forward = tables_ref[0]
    inverse = tables_ref[1].astype(F32)
    pad = jnp.zeros((points, out_ref.shape[2] - points), F32)
    for line in range(coulomb_ref.shape[0]):
        high, low = halves(inverse * multiplier[line : line + 1, :])
        out_ref[line, :, :points] = dot32(high, forward) + dot32(low, forward)
        out_ref[line, :, points:] = pad


def image_kernel(members, occupied_ref, *refs):
    blocks, (response_ref, high_ref, halves_ref) = refs[:-3], refs[-3:]
    packs, points, _ = blocks[0].shape
    padded = response_ref.shape[2]
    span = LANES // members
    per = span // 4
    total = lax.axis_size("band")
    position = lax.axis_index("band")
    places = [position] + sources(position, total)
    turns = [place % 4 for place in places]
    lane = ids((1, LANES), 1)
    own_line = lane_line(lane, turns[0], members)
    filled = [lane_member(lane, members) < occupied_ref[place] for place in places]
    quarters = [lane_quarter(lane, turn) for turn in turns]
    step = lane % (LANES // 4) // members
    apart, merged = 1, (0, 2, 3, 4)
    blank = jnp.zeros((padded - points, 2 * LANES), BF16)
    for pack in range(packs):
        tiles = [block[pack] for block in blocks]
        native = jnp.concatenate([tiles[0], blank[:, :LANES]], axis=0)
        kernels = []
        for quarter in range(4):
            here = [(q == quarter) for q in quarters]
            together = sum(tiles[m] * here[m].astype(F32).astype(BF16) for m in merged)
            window = jnp.concatenate([together, tiles[apart]], axis=1)
            occupied = sum((here[m] & filled[m]).astype(F32) for m in merged)
            beside = (here[apart] & filled[apart]).astype(F32)
            both = jnp.concatenate([occupied, beside], axis=1)
            steps = jnp.concatenate([step, step], axis=1)
            masked = jnp.concatenate(
                [window * jnp.where(steps == k, both, 0.0).astype(BF16) for k in range(per)], axis=0
            )
            gram = dot32(masked, jnp.concatenate([window, blank], axis=0), NT)
            first = pack * span + quarter * per
            response = response_ref[first : first + per].reshape(per * points, padded)
            kernels += halves(gram * response)
        fields = dot32(jnp.concatenate(kernels, axis=0), native)
        image = jnp.zeros((points, LANES), F32)
        for line in range(span):
            a = (line // per * 2 * per + line % per) * points
            b = a + per * points
            field = fields[a : a + points] + fields[b : b + points]
            image = jnp.where(own_line == line, field, image)
        high, low = halves(image)
        high_ref[pack] = high
        halves_ref[pack] = high
        halves_ref[packs + pack] = low


def overlap_kernel(orbitals_ref, halves_ref, out_ref):
    members, _, _ = orbitals_ref.shape
    span = LANES // members
    natives = orbitals_ref[...].astype(F32)
    square = (LANES, LANES)
    same_line = ids(square, 0) % span == lane_line(ids(square, 1), own_turn(), members)
    cross = jnp.zeros(square, F32)
    packs = halves_ref.shape[0] // 2
    for pack in range(packs):
        rows = rows_of(natives, pack, span).astype(BF16)
        both = jnp.concatenate([halves_ref[pack], halves_ref[packs + pack]], axis=1)
        product = dot32(rows, both)
        cross = cross + (product[:, :LANES] + product[:, LANES:])
    out_ref[...] = jnp.where(same_line, cross, 0.0).reshape(members, span, LANES).sum(axis=1)


def factor_kernel(cells, owners_ref, *refs):
    parts, (overlap_ref, weights_ref) = refs[:-2], refs[-2:]
    members = owners_ref.shape[0]
    span = LANES // members
    turn = own_turn()
    sums = [part[...] for part in parts]
    while len(sums) > 1:
        sums = [a + b for a, b in zip(sums[::2], sums[1::2])]
    high, rest = split(sums[0])
    pieces = [high, *halves(rest)]
    across = (members, LANES)
    gather = (ids(across, 0) == lane_member(ids(across, 1), members)).astype(BF16)
    overlap = sum(dot32(piece, gather, NT) for piece in pieces) * (1.0 / cells)
    flipped = sum(dot32(gather, piece, NT) for piece in pieces) * (1.0 / cells)
    overlap_ref[...] = overlap
    rows = CAP * span
    square = (members, members)
    group = lax.axis_index("grid") * lax.axis_size("ham") + lax.axis_index("ham")
    mine = (owners_ref[...] == group).astype(F32)
    eye = (ids(square, 0) == ids(square, 1)).astype(F32)
    mine_row = jnp.sum(mine * eye, axis=0, keepdims=True)
    before = (ids(square, 0) < ids(square, 1)).astype(F32)
    ranking = jnp.sum(mine * before, axis=0, keepdims=True)
    slot = (ids((rows, members), 0) // span).astype(F32)
    placed = (jnp.where(slot == ranking, 1.0, 0.0) * mine_row).astype(BF16)
    wide = (members, LANES)
    row = ids(wide, 0)
    upper = 0.5 * (overlap + flipped)
    columns = [jnp.broadcast_to(upper[:, j : j + 1], wide) for j in range(members)]
    lower = (row == lane_member(ids(wide, 1), members)).astype(F32)
    diagonal = ratio = jnp.zeros(wide, F32)
    for k in range(0, members, 2):
        first, second = columns[k], columns[k + 1]
        a, b, c = first[k : k + 1], first[k + 1 : k + 2], second[k + 1 : k + 2]
        share = b / a
        rest = c - share * b
        diagonal = jnp.where(row == k, a, jnp.where(row == k + 1, rest, diagonal))
        ratio = jnp.where(row == k + 1, share, ratio)
        scale = 1.0 / (a * c - b * b)
        below = row > k + 1
        one = jnp.where(below, (first * c - second * b) * scale, 0.0)
        two = jnp.where(below, (second * a - first * b) * scale, 0.0)
        lower = lower - (one * lower[k : k + 1] + two * lower[k + 1 : k + 2])
        for j in range(k + 2, members):
            column = columns[j]
            columns[j] = column - (one * column[k : k + 1] + two * column[k + 1 : k + 2])
    above = jnp.concatenate([lower[:1], lower[:-1]], axis=0)
    inverse = (lower - ratio * above) / jnp.sqrt(diagonal)
    high, low = halves(inverse)
    same_line = ids((rows, LANES), 0) % span == lane_line(ids((rows, LANES), 1), turn, members)
    blank = jnp.zeros((rows, LANES), BF16)
    chosen = [jnp.where(same_line, dot32(placed, half), 0.0).astype(BF16) for half in (high, low)]
    for i, half in enumerate(chosen + chosen):
        pair = [half, blank] if i < 2 else [blank, half]
        weights_ref[i * rows : (i + 1) * rows, :] = jnp.concatenate(pair, axis=1)


def route_kernel(overlap_ref, weights_ref, *refs):
    parts, (out_hbm, overlap_hbm, staged, semaphores) = refs[:-4], refs[-4:]
    groups = len(parts)
    copies = [pltpu.make_async_copy(overlap_ref, overlap_hbm, semaphores.at[groups])]
    copies[0].start()
    points = staged.shape[3]
    weights = weights_ref[...]
    rows = weights.shape[0] // 4
    span = rows // CAP
    lines = staged.shape[2]
    packs = lines // span
    highs = jnp.concatenate([weights[:rows], weights[2 * rows : 3 * rows]], axis=0)
    group = lax.axis_index("grid") * lax.axis_size("ham") + lax.axis_index("ham")
    for flip, part in enumerate(parts):
        sums = []
        for pack in range(0, packs, 2):
            field = jnp.concatenate([part[pack], part[pack + 1]], axis=1)
            both = dot32(weights, field, NT)
            results = [both[:rows] + both[rows : 2 * rows], both[2 * rows : 3 * rows] + both[3 * rows :]]
            if part.shape[0] > packs:
                place = packs + pack
                rest = dot32(highs, jnp.concatenate([part[place], part[place + 1]], axis=1), NT)
                results = [results[0] + rest[:rows], results[1] + rest[rows:]]
            sums += [result.reshape(CAP, span, points) for result in results]
        staged[flip] = jnp.concatenate(sums, axis=1).astype(BF16)
        start = pl.multiple_of((group ^ flip) * lines, lines)
        target = out_hbm.at[:, pl.ds(start, lines), :]
        copies.append(pltpu.make_async_copy(staged.at[flip], target, semaphores.at[flip]))
        copies[-1].start()
    for copy in copies:
        copy.wait()


def call(kernel, name, shapes, flops, moved, scratch=(), scalars=0, operands=0, remote=False, distant=0, limit=VMEM_LIMIT):
    vmem = pl.BlockSpec(memory_space=pltpu.VMEM)
    smem = pl.BlockSpec(memory_space=pltpu.SMEM)
    return pl.pallas_call(
        kernel,
        name=name,
        out_shape=shapes,
        in_specs=[smem] * scalars + [pl.BlockSpec(memory_space=pl.ANY)] * distant + [vmem] * operands,
        out_specs=[pl.BlockSpec(memory_space=pl.ANY) if remote else vmem] * len(shapes),
        scratch_shapes=list(scratch),
        compiler_params=pltpu.CompilerParams(vmem_limit_bytes=limit),
        cost_estimate=pl.CostEstimate(flops=flops, bytes_accessed=moved, transcendentals=0),
    )


def local(orbitals, coulomb, occupied, owners):
    members, lines, points = orbitals.shape
    grids, near = lax.axis_size("grid"), lax.axis_size("ham")
    groups = grids * near
    padded = -(-points // LANES) * LANES
    span = LANES // members
    packs = lines // span
    assert packs % 2 == 0
    shape = jax.ShapeDtypeStruct
    (packed,) = call(
        pack_kernel,
        "pack",
        [shape((packs, points, LANES), BF16)],
        orbitals.size,
        4 * orbitals.size,
        scratch=[
            pltpu.VMEM(orbitals.shape, BF16),
            pltpu.SemaphoreType.DMA((packs * PIECES,)),
        ],
        distant=1,
        limit=PACK_LIMIT,
    )(orbitals)
    guests = exchanged(packed)
    tables = spectral_tables(points)
    (response,) = call(
        response_kernel,
        "response",
        [shape((lines, points, padded), F32)],
        4 * lines * points**3,
        4 * lines * points**2,
        operands=2,
    )(coulomb, tables)
    blocks = len(guests) + 1
    high, parts = call(
        functools.partial(image_kernel, members),
        "image",
        [
            shape((packs, points, LANES), BF16),
            shape((2 * packs, points, LANES), BF16),
        ],
        2 * lines * points * padded * (4 * LANES),
        4 * lines * points**2,
        scalars=1,
        operands=blocks + 1,
    )(occupied, packed, *guests, response)
    (overlap,) = call(
        overlap_kernel,
        "overlap",
        [shape((members, LANES), F32)],
        4 * packs * points * LANES**2,
        8 * orbitals.size,
        operands=2,
    )(orbitals, parts)
    overlaps = [overlap] + [swapped(overlap, flip) for flip in range(1, groups)]
    images = [parts] + [swapped(parts, flip) for flip in range(1, near)]
    for grid in range(1, grids):
        across = swapped(high, grid * near)
        images += [across] + [swapped(across, flip) for flip in range(1, near)]
    cells = lines * groups * points

    intersection, weights = call(
        functools.partial(factor_kernel, cells),
        "factor",
        [shape((members, members), F32), shape((4 * CAP * span, 2 * LANES), BF16)],
        FACTOR_COST,
        members**2 * 4,
        operands=1 + groups,
    )(owners, *overlaps)
    routed, intersection = call(
        route_kernel,
        "route",
        [shape((CAP, groups * lines, points), BF16), shape((members, members), F32)],
        2 * CAP * members * groups * lines * points,
        6 * members * groups * lines * points,
        scratch=[
            pltpu.VMEM((groups, CAP, lines, points), BF16),
            pltpu.SemaphoreType.DMA((groups + 1,)),
        ],
        operands=2 + groups,
        remote=True,
    )(intersection, weights, *images)
    return routed[None, None], intersection[None]


def solution(mesh):
    in_specs = (P("band", ("grid", "ham"), None), P(("grid", "ham"), None), P(), P("band", None))
    out_specs = (P("band", ("grid", "ham"), None, None, None), P("band", None, None))
    return jax.shard_map(local, mesh=mesh, in_specs=in_specs, out_specs=out_specs, check_vma=False)
```

```python
import functools
import math

import jax
import jax.numpy as jnp
import numpy as np
from jax import lax
from jax.experimental import pallas as pl
from jax.experimental.pallas import tpu as pltpu
from jax.sharding import PartitionSpec as P

CAP = 8
LANES = 128
HIGHEST = lax.Precision.HIGHEST
VMEM_LIMIT = 48 * 1024 * 1024
FACTOR_COST = 3_000_000_000
NT = ((1,), (1,))
F32, BF16 = jnp.float32, jnp.bfloat16


STEPS = (-2, -1, 1, 2)


def sources(block, count):
    return [(block + step + count) % count for step in STEPS]


def exchanged(value):
    count = lax.axis_size("band")
    assert count % 4 == 0
    tables = [sources(block, count) for block in range(count)]
    return [
        lax.ppermute(value, "band", [(row[turn], block) for block, row in enumerate(tables)])
        for turn in range(4)
    ]


def swapped(value, flip):
    count = lax.axis_size("grid") * lax.axis_size("ham")
    return lax.ppermute(value, ("grid", "ham"), [(group, group ^ flip) for group in range(count)])


def spectral_tables(points):
    midpoint = points // 2
    ids = np.arange(points)
    frequency = np.where(ids <= midpoint, ids, ids - midpoint)
    angles = (ids[:, None] * frequency[None, :] % points) * (2.0 * math.pi / points)
    forward = np.where((ids <= midpoint)[None, :], np.cos(angles), np.sin(angles))
    single = (frequency == 0) | (ids == midpoint)
    inverse = forward.T * (np.where(single, 1.0, 2.0) / points)[:, None]
    mirror = np.zeros((points, points))
    mirror[frequency, ids] += 0.5
    mirror[(points - frequency) % points, ids] += 0.5
    return jnp.asarray(np.stack([forward.T, inverse.T, mirror]).astype(np.float32)).astype(BF16)


def split(value):
    high = value.astype(BF16)
    return high, value - high.astype(F32)


def halves(value):
    high, rest = split(value)
    return high, rest.astype(BF16)


def dot32(a, b, contract=((1,), (0,))):
    return lax.dot_general(a, b, (contract, ((), ())), preferred_element_type=F32)


def dot_exact(a, b, contract=((1,), (0,))):
    return lax.dot_general(
        a, b, (contract, ((), ())), precision=HIGHEST, preferred_element_type=F32
    )


def ids(shape, axis):
    return lax.broadcasted_iota(jnp.int32, shape, axis)


def lane_member(lane, members):
    return lane % members


def lane_quarter(lane, turn):
    return (lane // (LANES // 4)) ^ turn


def lane_line(lane, turn, members):
    per = LANES // 4 // members
    return lane_quarter(lane, turn) * per + lane % (LANES // 4) // members


def own_turn():
    return lax.axis_index("band") % 4


def rows_of(block, pack, span):
    members, _, points = block.shape
    part = block[:, pack * span : (pack + 1) * span, :]
    return part.reshape(members * span, points)


def pack_kernel(orbitals_ref, out_ref):
    members = orbitals_ref.shape[0]
    span = LANES // members
    block = orbitals_ref[...].astype(F32)
    row, lane = ids((LANES, LANES), 0), ids((LANES, LANES), 1)
    source = lane_member(lane, members) * span + lane_line(lane, own_turn(), members)
    order = (row == source).astype(BF16)
    for pack in range(out_ref.shape[0]):
        rows = rows_of(block, pack, span).T.astype(BF16)
        out_ref[pack] = dot32(rows, order).astype(BF16)


def response_kernel(coulomb_ref, tables_ref, out_ref):
    points = coulomb_ref.shape[1]
    multiplier = dot_exact(coulomb_ref[...], tables_ref[2].astype(F32))
    forward = tables_ref[0]
    inverse = tables_ref[1].astype(F32)
    pad = jnp.zeros((points, out_ref.shape[2] - points), F32)
    for line in range(coulomb_ref.shape[0]):
        high, low = halves(inverse * multiplier[line : line + 1, :])
        out_ref[line, :, :points] = dot32(high, forward) + dot32(low, forward)
        out_ref[line, :, points:] = pad


def image_kernel(members, occupied_ref, *refs):
    blocks, (response_ref, high_ref, halves_ref) = refs[:-3], refs[-3:]
    packs, points, _ = blocks[0].shape
    padded = response_ref.shape[2]
    span = LANES // members
    per = span // 4
    total = lax.axis_size("band")
    position = lax.axis_index("band")
    places = [position] + sources(position, total)
    turns = [place % 4 for place in places]
    lane = ids((1, LANES), 1)
    own_line = lane_line(lane, turns[0], members)
    filled = [lane_member(lane, members) < occupied_ref[place] for place in places]
    quarters = [lane_quarter(lane, turn) for turn in turns]
    step = lane % (LANES // 4) // members
    apart, merged = 1, (0, 2, 3, 4)
    blank = jnp.zeros((padded - points, 2 * LANES), BF16)
    for pack in range(packs):
        tiles = [block[pack] for block in blocks]
        native = jnp.concatenate([tiles[0], blank[:, :LANES]], axis=0)
        kernels = []
        for quarter in range(4):
            here = [(q == quarter) for q in quarters]
            together = sum(tiles[m] * here[m].astype(F32).astype(BF16) for m in merged)
            window = jnp.concatenate([together, tiles[apart]], axis=1)
            occupied = sum((here[m] & filled[m]).astype(F32) for m in merged)
            beside = (here[apart] & filled[apart]).astype(F32)
            both = jnp.concatenate([occupied, beside], axis=1)
            steps = jnp.concatenate([step, step], axis=1)
            masked = jnp.concatenate(
                [window * jnp.where(steps == k, both, 0.0).astype(BF16) for k in range(per)], axis=0
            )
            gram = dot32(masked, jnp.concatenate([window, blank], axis=0), NT)
            first = pack * span + quarter * per
            response = response_ref[first : first + per].reshape(per * points, padded)
            kernels += halves(gram * response)
        fields = dot32(jnp.concatenate(kernels, axis=0), native)
        image = jnp.zeros((points, LANES), F32)
        for line in range(span):
            a = (line // per * 2 * per + line % per) * points
            b = a + per * points
            field = fields[a : a + points] + fields[b : b + points]
            image = jnp.where(own_line == line, field, image)
        high, low = halves(image)
        high_ref[pack] = high
        halves_ref[pack] = high
        halves_ref[packs + pack] = low


def overlap_kernel(orbitals_ref, halves_ref, out_ref):
    members, _, _ = orbitals_ref.shape
    span = LANES // members
    natives = orbitals_ref[...].astype(F32)
    square = (LANES, LANES)
    same_line = ids(square, 0) % span == lane_line(ids(square, 1), own_turn(), members)
    cross = jnp.zeros(square, F32)
    packs = halves_ref.shape[0] // 2
    for pack in range(packs):
        rows = rows_of(natives, pack, span).astype(BF16)
        both = jnp.concatenate([halves_ref[pack], halves_ref[packs + pack]], axis=1)
        product = dot32(rows, both)
        cross = cross + (product[:, :LANES] + product[:, LANES:])
    out_ref[...] = jnp.where(same_line, cross, 0.0).reshape(members, span, LANES).sum(axis=1)


def factor_kernel(cells, owners_ref, *refs):
    parts, (overlap_ref, weights_ref) = refs[:-2], refs[-2:]
    members = owners_ref.shape[0]
    span = LANES // members
    turn = own_turn()
    sums = [part[...] for part in parts]
    while len(sums) > 1:
        sums = [a + b for a, b in zip(sums[::2], sums[1::2])]
    high, rest = split(sums[0])
    pieces = [high, *halves(rest)]
    across = (members, LANES)
    gather = (ids(across, 0) == lane_member(ids(across, 1), members)).astype(BF16)
    overlap = sum(dot32(piece, gather, NT) for piece in pieces) * (1.0 / cells)
    flipped = sum(dot32(gather, piece, NT) for piece in pieces) * (1.0 / cells)
    overlap_ref[...] = overlap
    rows = CAP * span
    square = (members, members)
    group = lax.axis_index("grid") * lax.axis_size("ham") + lax.axis_index("ham")
    mine = (owners_ref[...] == group).astype(F32)
    eye = (ids(square, 0) == ids(square, 1)).astype(F32)
    mine_row = jnp.sum(mine * eye, axis=0, keepdims=True)
    before = (ids(square, 0) < ids(square, 1)).astype(F32)
    ranking = jnp.sum(mine * before, axis=0, keepdims=True)
    slot = (ids((rows, members), 0) // span).astype(F32)
    placed = (jnp.where(slot == ranking, 1.0, 0.0) * mine_row).astype(BF16)
    wide = (members, LANES)
    row = ids(wide, 0)
    upper = 0.5 * (overlap + flipped)
    columns = [jnp.broadcast_to(upper[:, j : j + 1], wide) for j in range(members)]
    lower = (row == lane_member(ids(wide, 1), members)).astype(F32)
    diagonal = ratio = jnp.zeros(wide, F32)
    for k in range(0, members, 2):
        first, second = columns[k], columns[k + 1]
        a, b, c = first[k : k + 1], first[k + 1 : k + 2], second[k + 1 : k + 2]
        share = b / a
        rest = c - share * b
        diagonal = jnp.where(row == k, a, jnp.where(row == k + 1, rest, diagonal))
        ratio = jnp.where(row == k + 1, share, ratio)
        scale = 1.0 / (a * c - b * b)
        below = row > k + 1
        one = jnp.where(below, (first * c - second * b) * scale, 0.0)
        two = jnp.where(below, (second * a - first * b) * scale, 0.0)
        lower = lower - (one * lower[k : k + 1] + two * lower[k + 1 : k + 2])
        for j in range(k + 2, members):
            column = columns[j]
            columns[j] = column - (one * column[k : k + 1] + two * column[k + 1 : k + 2])
    above = jnp.concatenate([lower[:1], lower[:-1]], axis=0)
    inverse = (lower - ratio * above) / jnp.sqrt(diagonal)
    high, low = halves(inverse)
    same_line = ids((rows, LANES), 0) % span == lane_line(ids((rows, LANES), 1), turn, members)
    blank = jnp.zeros((rows, LANES), BF16)
    chosen = [jnp.where(same_line, dot32(placed, half), 0.0).astype(BF16) for half in (high, low)]
    for i, half in enumerate(chosen + chosen):
        pair = [half, blank] if i < 2 else [blank, half]
        weights_ref[i * rows : (i + 1) * rows, :] = jnp.concatenate(pair, axis=1)


def route_kernel(overlap_ref, weights_ref, *refs):
    parts, (out_hbm, overlap_hbm, staged, semaphores) = refs[:-4], refs[-4:]
    groups = len(parts)
    copies = [pltpu.make_async_copy(overlap_ref, overlap_hbm, semaphores.at[groups])]
    copies[0].start()
    points = staged.shape[3]
    weights = weights_ref[...]
    rows = weights.shape[0] // 4
    span = rows // CAP
    lines = staged.shape[2]
    packs = lines // span
    highs = jnp.concatenate([weights[:rows], weights[2 * rows : 3 * rows]], axis=0)
    group = lax.axis_index("grid") * lax.axis_size("ham") + lax.axis_index("ham")
    for flip, part in enumerate(parts):
        sums = []
        for pack in range(0, packs, 2):
            field = jnp.concatenate([part[pack], part[pack + 1]], axis=1)
            both = dot32(weights, field, NT)
            results = [both[:rows] + both[rows : 2 * rows], both[2 * rows : 3 * rows] + both[3 * rows :]]
            if part.shape[0] > packs:
                place = packs + pack
                rest = dot32(highs, jnp.concatenate([part[place], part[place + 1]], axis=1), NT)
                results = [results[0] + rest[:rows], results[1] + rest[rows:]]
            sums += [result.reshape(CAP, span, points) for result in results]
        staged[flip] = jnp.concatenate(sums, axis=1).astype(BF16)
        start = pl.multiple_of((group ^ flip) * lines, lines)
        target = out_hbm.at[:, pl.ds(start, lines), :]
        copies.append(pltpu.make_async_copy(staged.at[flip], target, semaphores.at[flip]))
        copies[-1].start()
    for copy in copies:
        copy.wait()


def call(kernel, name, shapes, flops, moved, scratch=(), scalars=0, operands=0, remote=False):
    vmem = pl.BlockSpec(memory_space=pltpu.VMEM)
    smem = pl.BlockSpec(memory_space=pltpu.SMEM)
    return pl.pallas_call(
        kernel,
        name=name,
        out_shape=shapes,
        in_specs=[smem] * scalars + [vmem] * operands,
        out_specs=[pl.BlockSpec(memory_space=pl.ANY) if remote else vmem] * len(shapes),
        scratch_shapes=list(scratch),
        compiler_params=pltpu.CompilerParams(vmem_limit_bytes=VMEM_LIMIT),
        cost_estimate=pl.CostEstimate(flops=flops, bytes_accessed=moved, transcendentals=0),
    )


def local(orbitals, coulomb, occupied, owners):
    members, lines, points = orbitals.shape
    grids, near = lax.axis_size("grid"), lax.axis_size("ham")
    groups = grids * near
    padded = -(-points // LANES) * LANES
    span = LANES // members
    packs = lines // span
    assert packs % 2 == 0
    shape = jax.ShapeDtypeStruct
    (packed,) = call(
        pack_kernel,
        "pack",
        [shape((packs, points, LANES), BF16)],
        orbitals.size,
        4 * orbitals.size,
        operands=1,
    )(orbitals)
    guests = exchanged(packed)
    tables = spectral_tables(points)
    (response,) = call(
        response_kernel,
        "response",
        [shape((lines, points, padded), F32)],
        4 * lines * points**3,
        4 * lines * points**2,
        operands=2,
    )(coulomb, tables)
    blocks = len(guests) + 1
    high, parts = call(
        functools.partial(image_kernel, members),
        "image",
        [
            shape((packs, points, LANES), BF16),
            shape((2 * packs, points, LANES), BF16),
        ],
        2 * lines * points * padded * (4 * LANES),
        4 * lines * points**2,
        scalars=1,
        operands=blocks + 1,
    )(occupied, packed, *guests, response)
    (overlap,) = call(
        overlap_kernel,
        "overlap",
        [shape((members, LANES), F32)],
        4 * packs * points * LANES**2,
        8 * orbitals.size,
        operands=2,
    )(orbitals, parts)
    overlaps = [overlap] + [swapped(overlap, flip) for flip in range(1, groups)]
    images = [parts] + [swapped(parts, flip) for flip in range(1, near)]
    for grid in range(1, grids):
        across = swapped(high, grid * near)
        images += [across] + [swapped(across, flip) for flip in range(1, near)]
    cells = lines * groups * points

    intersection, weights = call(
        functools.partial(factor_kernel, cells),
        "factor",
        [shape((members, members), F32), shape((4 * CAP * span, 2 * LANES), BF16)],
        FACTOR_COST,
        members**2 * 4,
        operands=1 + groups,
    )(owners, *overlaps)
    routed, intersection = call(
        route_kernel,
        "route",
        [shape((CAP, groups * lines, points), BF16), shape((members, members), F32)],
        2 * CAP * members * groups * lines * points,
        6 * members * groups * lines * points,
        scratch=[
            pltpu.VMEM((groups, CAP, lines, points), BF16),
            pltpu.SemaphoreType.DMA((groups + 1,)),
        ],
        operands=2 + groups,
        remote=True,
    )(intersection, weights, *images)
    return routed[None, None], intersection[None]


def solution(mesh):
    in_specs = (P("band", ("grid", "ham"), None), P(("grid", "ham"), None), P(), P("band", None))
    out_specs = (P("band", ("grid", "ham"), None, None, None), P("band", None, None))
    return jax.shard_map(local, mesh=mesh, in_specs=in_specs, out_specs=out_specs, check_vma=False)
```

```python
import functools
import math

import jax
import jax.numpy as jnp
import numpy as np
from jax import lax
from jax.experimental import pallas as pl
from jax.experimental.pallas import tpu as pltpu
from jax.sharding import PartitionSpec as P

CAP = 8
LANES = 128
HIGHEST = lax.Precision.HIGHEST
VMEM_LIMIT = 48 * 1024 * 1024
FACTOR_COST = 3_000_000_000
NT = ((1,), (1,))
F32, BF16 = jnp.float32, jnp.bfloat16


def sources(block, count):
    odd = block % 2
    steps = (-2, 2 * odd - 1, 1 - 2 * odd, 2)
    return [(block + step + count) % count for step in steps]


def exchanged(value):
    count = lax.axis_size("band")
    assert count % 4 == 0
    tables = [sources(block, count) for block in range(count)]
    return [
        lax.ppermute(value, "band", [(row[turn], block) for block, row in enumerate(tables)])
        for turn in range(4)
    ]


def swapped(value, flip):
    count = lax.axis_size("grid") * lax.axis_size("ham")
    return lax.ppermute(value, ("grid", "ham"), [(group, group ^ flip) for group in range(count)])


def spectral_tables(points):
    midpoint = points // 2
    ids = np.arange(points)
    frequency = np.where(ids <= midpoint, ids, ids - midpoint)
    angles = (ids[:, None] * frequency[None, :] % points) * (2.0 * math.pi / points)
    forward = np.where((ids <= midpoint)[None, :], np.cos(angles), np.sin(angles))
    single = (frequency == 0) | (ids == midpoint)
    inverse = forward.T * (np.where(single, 1.0, 2.0) / points)[:, None]
    mirror = np.zeros((points, points))
    mirror[frequency, ids] += 0.5
    mirror[(points - frequency) % points, ids] += 0.5
    return jnp.asarray(np.stack([forward.T, inverse.T, mirror]).astype(np.float32)).astype(BF16)


def split(value):
    high = value.astype(BF16)
    return high, value - high.astype(F32)


def halves(value):
    high, rest = split(value)
    return high, rest.astype(BF16)


def dot32(a, b, contract=((1,), (0,))):
    return lax.dot_general(a, b, (contract, ((), ())), preferred_element_type=F32)


def dot_exact(a, b, contract=((1,), (0,))):
    return lax.dot_general(
        a, b, (contract, ((), ())), precision=HIGHEST, preferred_element_type=F32
    )


def ids(shape, axis):
    return lax.broadcasted_iota(jnp.int32, shape, axis)


def lane_member(lane, members):
    return lane % members


def lane_quarter(lane, turn):
    return (lane // (LANES // 4)) ^ turn


def lane_line(lane, turn, members):
    per = LANES // 4 // members
    return lane_quarter(lane, turn) * per + lane % (LANES // 4) // members


def own_turn():
    return lax.axis_index("band") % 4


def rows_of(block, pack, span):
    members, _, points = block.shape
    part = block[:, pack * span : (pack + 1) * span, :]
    return part.reshape(members * span, points)


def pack_kernel(orbitals_ref, out_ref):
    members = orbitals_ref.shape[0]
    span = LANES // members
    block = orbitals_ref[...].astype(F32)
    row, lane = ids((LANES, LANES), 0), ids((LANES, LANES), 1)
    source = lane_member(lane, members) * span + lane_line(lane, own_turn(), members)
    order = (row == source).astype(BF16)
    for pack in range(out_ref.shape[0]):
        rows = rows_of(block, pack, span).T.astype(BF16)
        out_ref[pack] = dot32(rows, order).astype(BF16)


def response_kernel(coulomb_ref, tables_ref, out_ref):
    points = coulomb_ref.shape[1]
    multiplier = dot_exact(coulomb_ref[...], tables_ref[2].astype(F32))
    forward = tables_ref[0]
    inverse = tables_ref[1].astype(F32)
    pad = jnp.zeros((points, out_ref.shape[2] - points), F32)
    for line in range(coulomb_ref.shape[0]):
        high, low = halves(inverse * multiplier[line : line + 1, :])
        out_ref[line, :, :points] = dot32(high, forward) + dot32(low, forward)
        out_ref[line, :, points:] = pad


def image_kernel(members, occupied_ref, *refs):
    blocks, (response_ref, high_ref, halves_ref) = refs[:-3], refs[-3:]
    packs, points, _ = blocks[0].shape
    padded = response_ref.shape[2]
    span = LANES // members
    per = span // 4
    total = lax.axis_size("band")
    position = lax.axis_index("band")
    places = [position] + sources(position, total)
    turns = [place % 4 for place in places]
    lane = ids((1, LANES), 1)
    own_line = lane_line(lane, turns[0], members)
    filled = [lane_member(lane, members) < occupied_ref[place] for place in places]
    quarters = [lane_quarter(lane, turn) for turn in turns]
    step = lane % (LANES // 4) // members
    apart, merged = 1, (0, 2, 3, 4)
    spare = padded - points
    cuts = points // spare
    assert cuts * spare == points and LANES % spare == 0
    blank = jnp.zeros((spare, 2 * LANES), BF16)
    for pack in range(packs):
        tiles = [block[pack] for block in blocks]
        kernels = [[] for _ in range(cuts)]
        for quarter in range(4):
            here = [(q == quarter) for q in quarters]
            together = sum(tiles[m] * here[m].astype(F32).astype(BF16) for m in merged)
            window = jnp.concatenate([together, tiles[apart]], axis=1)
            occupied = sum((here[m] & filled[m]).astype(F32) for m in merged)
            beside = (here[apart] & filled[apart]).astype(F32)
            both = jnp.concatenate([occupied, beside], axis=1)
            steps = jnp.concatenate([step, step], axis=1)
            masked = jnp.concatenate(
                [window * jnp.where(steps == k, both, 0.0).astype(BF16) for k in range(per)], axis=0
            )
            gram = dot32(masked, jnp.concatenate([window, blank], axis=0), NT)
            first = pack * span + quarter * per
            response = response_ref[first : first + per].reshape(per * points, padded)
            weighted = gram * response
            for place in range(0, per * points, spare):
                cut = place // spare % cuts
                part = weighted[place : place + spare]
                tile = cut * spare // LANES * LANES
                _, low = split(part[:, tile : tile + LANES])
                shift = LANES - spare - cut * spare % LANES
                low = pltpu.roll(low, shift, axis=1) if shift else low
                last = jnp.where(lane < LANES - spare, part[:, -LANES:], low)
                part = jnp.concatenate([part[:, :-LANES], last], axis=1)
                kernels[cut].append(part.astype(BF16))
        image = []
        for cut in range(cuts):
            native = jnp.concatenate([tiles[0], tiles[0][cut * spare : (cut + 1) * spare]], axis=0)
            fields = dot32(jnp.concatenate(kernels[cut], axis=0), native)
            rows = jnp.zeros((spare, LANES), F32)
            for line in range(span):
                rows = jnp.where(own_line == line, fields[line * spare : (line + 1) * spare], rows)
            image.append(rows)
        image = jnp.concatenate(image, axis=0)
        high, low = halves(image)
        high_ref[pack] = high
        halves_ref[pack] = high
        halves_ref[packs + pack] = low


def overlap_kernel(orbitals_ref, halves_ref, out_ref):
    members, _, _ = orbitals_ref.shape
    span = LANES // members
    natives = orbitals_ref[...].astype(F32)
    square = (LANES, LANES)
    same_line = ids(square, 0) % span == lane_line(ids(square, 1), own_turn(), members)
    cross = jnp.zeros(square, F32)
    packs = halves_ref.shape[0] // 2
    for pack in range(packs):
        rows = rows_of(natives, pack, span).astype(BF16)
        both = jnp.concatenate([halves_ref[pack], halves_ref[packs + pack]], axis=1)
        product = dot32(rows, both)
        cross = cross + (product[:, :LANES] + product[:, LANES:])
    out_ref[...] = jnp.where(same_line, cross, 0.0).reshape(members, span, LANES).sum(axis=1)


def factor_kernel(cells, owners_ref, *refs):
    parts, (overlap_ref, weights_ref) = refs[:-2], refs[-2:]
    members = owners_ref.shape[0]
    span = LANES // members
    turn = own_turn()
    sums = [part[...] for part in parts]
    while len(sums) > 1:
        sums = [a + b for a, b in zip(sums[::2], sums[1::2])]
    high, rest = split(sums[0])
    pieces = [high, *halves(rest)]
    across = (members, LANES)
    gather = (ids(across, 0) == lane_member(ids(across, 1), members)).astype(BF16)
    overlap = sum(dot32(piece, gather, NT) for piece in pieces) * (1.0 / cells)
    flipped = sum(dot32(gather, piece, NT) for piece in pieces) * (1.0 / cells)
    overlap_ref[...] = overlap
    rows = CAP * span
    square = (members, members)
    group = lax.axis_index("grid") * lax.axis_size("ham") + lax.axis_index("ham")
    mine = (owners_ref[...] == group).astype(F32)
    eye = (ids(square, 0) == ids(square, 1)).astype(F32)
    mine_row = jnp.sum(mine * eye, axis=0, keepdims=True)
    before = (ids(square, 0) < ids(square, 1)).astype(F32)
    ranking = jnp.sum(mine * before, axis=0, keepdims=True)
    slot = (ids((rows, members), 0) // span).astype(F32)
    placed = (jnp.where(slot == ranking, 1.0, 0.0) * mine_row).astype(BF16)
    wide = (members, LANES)
    row = ids(wide, 0)
    upper = 0.5 * (overlap + flipped)
    columns = [jnp.broadcast_to(upper[:, j : j + 1], wide) for j in range(members)]
    lower = (row == lane_member(ids(wide, 1), members)).astype(F32)
    diagonal = ratio = jnp.zeros(wide, F32)
    for k in range(0, members, 2):
        first, second = columns[k], columns[k + 1]
        a, b, c = first[k : k + 1], first[k + 1 : k + 2], second[k + 1 : k + 2]
        share = b / a
        rest = c - share * b
        diagonal = jnp.where(row == k, a, jnp.where(row == k + 1, rest, diagonal))
        ratio = jnp.where(row == k + 1, share, ratio)
        scale = 1.0 / (a * c - b * b)
        below = row > k + 1
        one = jnp.where(below, (first * c - second * b) * scale, 0.0)
        two = jnp.where(below, (second * a - first * b) * scale, 0.0)
        lower = lower - (one * lower[k : k + 1] + two * lower[k + 1 : k + 2])
        for j in range(k + 2, members):
            column = columns[j]
            columns[j] = column - (one * column[k : k + 1] + two * column[k + 1 : k + 2])
    above = jnp.concatenate([lower[:1], lower[:-1]], axis=0)
    inverse = (lower - ratio * above) / jnp.sqrt(diagonal)
    high, low = halves(inverse)
    same_line = ids((rows, LANES), 0) % span == lane_line(ids((rows, LANES), 1), turn, members)
    blank = jnp.zeros((rows, LANES), BF16)
    chosen = [jnp.where(same_line, dot32(placed, half), 0.0).astype(BF16) for half in (high, low)]
    for i, half in enumerate(chosen + chosen):
        pair = [half, blank] if i < 2 else [blank, half]
        weights_ref[i * rows : (i + 1) * rows, :] = jnp.concatenate(pair, axis=1)


def route_kernel(overlap_ref, weights_ref, *refs):
    parts, (out_hbm, overlap_hbm, staged, semaphores) = refs[:-4], refs[-4:]
    groups = len(parts)
    copies = [pltpu.make_async_copy(overlap_ref, overlap_hbm, semaphores.at[groups])]
    copies[0].start()
    points = staged.shape[3]
    weights = weights_ref[...]
    rows = weights.shape[0] // 4
    span = rows // CAP
    lines = staged.shape[2]
    packs = lines // span
    highs = jnp.concatenate([weights[:rows], weights[2 * rows : 3 * rows]], axis=0)
    group = lax.axis_index("grid") * lax.axis_size("ham") + lax.axis_index("ham")
    for flip, part in enumerate(parts):
        sums = []
        for pack in range(0, packs, 2):
            field = jnp.concatenate([part[pack], part[pack + 1]], axis=1)
            both = dot32(weights, field, NT)
            results = [both[:rows] + both[rows : 2 * rows], both[2 * rows : 3 * rows] + both[3 * rows :]]
            if part.shape[0] > packs:
                place = packs + pack
                rest = dot32(highs, jnp.concatenate([part[place], part[place + 1]], axis=1), NT)
                results = [results[0] + rest[:rows], results[1] + rest[rows:]]
            sums += [result.reshape(CAP, span, points) for result in results]
        staged[flip] = jnp.concatenate(sums, axis=1).astype(BF16)
        start = pl.multiple_of((group ^ flip) * lines, lines)
        target = out_hbm.at[:, pl.ds(start, lines), :]
        copies.append(pltpu.make_async_copy(staged.at[flip], target, semaphores.at[flip]))
        copies[-1].start()
    for copy in copies:
        copy.wait()


def call(kernel, name, shapes, flops, moved, scratch=(), scalars=0, operands=0, remote=False):
    vmem = pl.BlockSpec(memory_space=pltpu.VMEM)
    smem = pl.BlockSpec(memory_space=pltpu.SMEM)
    return pl.pallas_call(
        kernel,
        name=name,
        out_shape=shapes,
        in_specs=[smem] * scalars + [vmem] * operands,
        out_specs=[pl.BlockSpec(memory_space=pl.ANY) if remote else vmem] * len(shapes),
        scratch_shapes=list(scratch),
        compiler_params=pltpu.CompilerParams(vmem_limit_bytes=VMEM_LIMIT),
        cost_estimate=pl.CostEstimate(flops=flops, bytes_accessed=moved, transcendentals=0),
    )


def local(orbitals, coulomb, occupied, owners):
    members, lines, points = orbitals.shape
    grids, near = lax.axis_size("grid"), lax.axis_size("ham")
    groups = grids * near
    padded = -(-points // LANES) * LANES
    span = LANES // members
    packs = lines // span
    assert packs % 2 == 0
    shape = jax.ShapeDtypeStruct
    (packed,) = call(
        pack_kernel,
        "pack",
        [shape((packs, points, LANES), BF16)],
        orbitals.size,
        4 * orbitals.size,
        operands=1,
    )(orbitals)
    guests = exchanged(packed)
    tables = spectral_tables(points)
    (response,) = call(
        response_kernel,
        "response",
        [shape((lines, points, padded), F32)],
        4 * lines * points**3,
        4 * lines * points**2,
        operands=2,
    )(coulomb, tables)
    blocks = len(guests) + 1
    high, parts = call(
        functools.partial(image_kernel, members),
        "image",
        [
            shape((packs, points, LANES), BF16),
            shape((2 * packs, points, LANES), BF16),
        ],
        2 * lines * points * padded * (4 * LANES),
        4 * lines * points**2,
        scalars=1,
        operands=blocks + 1,
    )(occupied, packed, *guests, response)
    (overlap,) = call(
        overlap_kernel,
        "overlap",
        [shape((members, LANES), F32)],
        4 * packs * points * LANES**2,
        8 * orbitals.size,
        operands=2,
    )(orbitals, parts)
    overlaps = [overlap] + [swapped(overlap, flip) for flip in range(1, groups)]
    images = [parts] + [swapped(parts, flip) for flip in range(1, near)]
    for grid in range(1, grids):
        across = swapped(high, grid * near)
        images += [across] + [swapped(across, flip) for flip in range(1, near)]
    cells = lines * groups * points

    intersection, weights = call(
        functools.partial(factor_kernel, cells),
        "factor",
        [shape((members, members), F32), shape((4 * CAP * span, 2 * LANES), BF16)],
        FACTOR_COST,
        members**2 * 4,
        operands=1 + groups,
    )(owners, *overlaps)
    routed, intersection = call(
        route_kernel,
        "route",
        [shape((CAP, groups * lines, points), BF16), shape((members, members), F32)],
        2 * CAP * members * groups * lines * points,
        6 * members * groups * lines * points,
        scratch=[
            pltpu.VMEM((groups, CAP, lines, points), BF16),
            pltpu.SemaphoreType.DMA((groups + 1,)),
        ],
        operands=2 + groups,
        remote=True,
    )(intersection, weights, *images)
    return routed[None, None], intersection[None]


def solution(mesh):
    in_specs = (P("band", ("grid", "ham"), None), P(("grid", "ham"), None), P(), P("band", None))
    out_specs = (P("band", ("grid", "ham"), None, None, None), P("band", None, None))
    return jax.shard_map(local, mesh=mesh, in_specs=in_specs, out_specs=out_specs, check_vma=False)
```

```python
import functools
import math

import jax
import jax.numpy as jnp
import numpy as np
from jax import lax
from jax.experimental import pallas as pl
from jax.experimental.pallas import tpu as pltpu
from jax.sharding import PartitionSpec as P

CAP = 8
LANES = 128
HIGHEST = lax.Precision.HIGHEST
VMEM_LIMIT = 48 * 1024 * 1024
FACTOR_COST = 3_000_000_000
NT = ((1,), (1,))
F32, BF16 = jnp.float32, jnp.bfloat16


def sources(block, count):
    odd = block % 2
    steps = (-2, 2 * odd - 1, 1 - 2 * odd, 2)
    return [(block + step + count) % count for step in steps]


def exchanged(value):
    count = lax.axis_size("band")
    assert count % 4 == 0
    tables = [sources(block, count) for block in range(count)]
    return [
        lax.ppermute(value, "band", [(row[turn], block) for block, row in enumerate(tables)])
        for turn in range(4)
    ]


def swapped(value, flip):
    count = lax.axis_size("grid") * lax.axis_size("ham")
    return lax.ppermute(value, ("grid", "ham"), [(group, group ^ flip) for group in range(count)])


def spectral_tables(points):
    midpoint = points // 2
    ids = np.arange(points)
    frequency = np.where(ids <= midpoint, ids, ids - midpoint)
    angles = (ids[:, None] * frequency[None, :] % points) * (2.0 * math.pi / points)
    forward = np.where((ids <= midpoint)[None, :], np.cos(angles), np.sin(angles))
    single = (frequency == 0) | (ids == midpoint)
    inverse = forward.T * (np.where(single, 1.0, 2.0) / points)[:, None]
    mirror = np.zeros((points, points))
    mirror[frequency, ids] += 0.5
    mirror[(points - frequency) % points, ids] += 0.5
    return jnp.asarray(np.stack([forward.T, inverse.T, mirror]).astype(np.float32)).astype(BF16)


def split(value):
    high = value.astype(BF16)
    return high, value - high.astype(F32)


def halves(value):
    high, rest = split(value)
    return high, rest.astype(BF16)


def dot32(a, b, contract=((1,), (0,))):
    return lax.dot_general(a, b, (contract, ((), ())), preferred_element_type=F32)


def dot_exact(a, b, contract=((1,), (0,))):
    return lax.dot_general(
        a, b, (contract, ((), ())), precision=HIGHEST, preferred_element_type=F32
    )


def ids(shape, axis):
    return lax.broadcasted_iota(jnp.int32, shape, axis)


def lane_member(lane, members):
    return lane % members


def lane_quarter(lane, turn):
    return (lane // (LANES // 4)) ^ turn


def lane_line(lane, turn, members):
    per = LANES // 4 // members
    return lane_quarter(lane, turn) * per + lane % (LANES // 4) // members


def own_turn():
    return lax.axis_index("band") % 4


def rows_of(block, pack, span):
    members, _, points = block.shape
    part = block[:, pack * span : (pack + 1) * span, :]
    return part.reshape(members * span, points)


def pack_kernel(orbitals_ref, out_ref):
    members = orbitals_ref.shape[0]
    span = LANES // members
    block = orbitals_ref[...].astype(F32)
    row, lane = ids((LANES, LANES), 0), ids((LANES, LANES), 1)
    source = lane_member(lane, members) * span + lane_line(lane, own_turn(), members)
    order = (row == source).astype(BF16)
    for pack in range(out_ref.shape[0]):
        rows = rows_of(block, pack, span).T.astype(BF16)
        out_ref[pack] = dot32(rows, order).astype(BF16)


def response_kernel(coulomb_ref, tables_ref, out_ref):
    points = coulomb_ref.shape[1]
    multiplier = dot_exact(coulomb_ref[...], tables_ref[2].astype(F32))
    forward = tables_ref[0]
    inverse = tables_ref[1].astype(F32)
    pad = jnp.zeros((points, out_ref.shape[2] - points), F32)
    for line in range(coulomb_ref.shape[0]):
        high, low = halves(inverse * multiplier[line : line + 1, :])
        out_ref[line, :, :points] = dot32(high, forward) + dot32(low, forward)
        out_ref[line, :, points:] = pad


def image_kernel(members, occupied_ref, *refs):
    blocks, (response_ref, high_ref, halves_ref) = refs[:-3], refs[-3:]
    packs, points, _ = blocks[0].shape
    padded = response_ref.shape[2]
    span = LANES // members
    per = span // 4
    total = lax.axis_size("band")
    position = lax.axis_index("band")
    places = [position] + sources(position, total)
    turns = [place % 4 for place in places]
    lane = ids((1, LANES), 1)
    own_line = lane_line(lane, turns[0], members)
    filled = [lane_member(lane, members) < occupied_ref[place] for place in places]
    quarters = [lane_quarter(lane, turn) for turn in turns]
    step = lane % (LANES // 4) // members
    apart, merged = 1, (0, 2, 3, 4)
    spare = padded - points
    cuts = points // spare
    assert cuts * spare == points and LANES % spare == 0
    blank = jnp.zeros((spare, 2 * LANES), BF16)
    kernels = [[[] for _ in range(cuts)] for _ in range(packs)]
    for pack in range(packs):
        tiles = [block[pack] for block in blocks]
        for quarter in range(4):
            here = [(q == quarter) for q in quarters]
            together = sum(tiles[m] * here[m].astype(F32).astype(BF16) for m in merged)
            window = jnp.concatenate([together, tiles[apart]], axis=1)
            occupied = sum((here[m] & filled[m]).astype(F32) for m in merged)
            beside = (here[apart] & filled[apart]).astype(F32)
            both = jnp.concatenate([occupied, beside], axis=1)
            steps = jnp.concatenate([step, step], axis=1)
            masked = jnp.concatenate(
                [window * jnp.where(steps == k, both, 0.0).astype(BF16) for k in range(per)], axis=0
            )
            gram = dot32(masked, jnp.concatenate([window, blank], axis=0), NT)
            first = pack * span + quarter * per
            response = response_ref[first : first + per].reshape(per * points, padded)
            weighted = gram * response
            for place in range(0, per * points, spare):
                cut = place // spare % cuts
                part = weighted[place : place + spare]
                tile = cut * spare // LANES * LANES
                _, low = split(part[:, tile : tile + LANES])
                shift = LANES - spare - cut * spare % LANES
                low = pltpu.roll(low, shift, axis=1) if shift else low
                last = jnp.where(lane < LANES - spare, part[:, -LANES:], low)
                part = jnp.concatenate([part[:, :-LANES], last], axis=1)
                kernels[pack][cut].append(part.astype(BF16))
    for pack in range(packs):
        tile = blocks[0][pack]
        image = []
        for cut in range(cuts):
            native = jnp.concatenate([tile, tile[cut * spare : (cut + 1) * spare]], axis=0)
            fields = dot32(jnp.concatenate(kernels[pack][cut], axis=0), native)
            rows = jnp.zeros((spare, LANES), F32)
            for line in range(span):
                rows = jnp.where(own_line == line, fields[line * spare : (line + 1) * spare], rows)
            image.append(rows)
        image = jnp.concatenate(image, axis=0)
        high, low = halves(image)
        high_ref[pack] = high
        halves_ref[pack] = high
        halves_ref[packs + pack] = low


def overlap_kernel(orbitals_ref, halves_ref, out_ref):
    members, _, _ = orbitals_ref.shape
    span = LANES // members
    natives = orbitals_ref[...].astype(F32)
    square = (LANES, LANES)
    same_line = ids(square, 0) % span == lane_line(ids(square, 1), own_turn(), members)
    cross = jnp.zeros(square, F32)
    packs = halves_ref.shape[0] // 2
    for pack in range(packs):
        rows = rows_of(natives, pack, span).astype(BF16)
        both = jnp.concatenate([halves_ref[pack], halves_ref[packs + pack]], axis=1)
        product = dot32(rows, both)
        cross = cross + (product[:, :LANES] + product[:, LANES:])
    out_ref[...] = jnp.where(same_line, cross, 0.0).reshape(members, span, LANES).sum(axis=1)


def factor_kernel(cells, owners_ref, *refs):
    parts, (overlap_ref, weights_ref) = refs[:-2], refs[-2:]
    members = owners_ref.shape[0]
    span = LANES // members
    turn = own_turn()
    sums = [part[...] for part in parts]
    while len(sums) > 1:
        sums = [a + b for a, b in zip(sums[::2], sums[1::2])]
    high, rest = split(sums[0])
    pieces = [high, *halves(rest)]
    across = (members, LANES)
    gather = (ids(across, 0) == lane_member(ids(across, 1), members)).astype(BF16)
    overlap = sum(dot32(piece, gather, NT) for piece in pieces) * (1.0 / cells)
    flipped = sum(dot32(gather, piece, NT) for piece in pieces) * (1.0 / cells)
    overlap_ref[...] = overlap
    rows = CAP * span
    square = (members, members)
    group = lax.axis_index("grid") * lax.axis_size("ham") + lax.axis_index("ham")
    mine = (owners_ref[...] == group).astype(F32)
    eye = (ids(square, 0) == ids(square, 1)).astype(F32)
    mine_row = jnp.sum(mine * eye, axis=0, keepdims=True)
    before = (ids(square, 0) < ids(square, 1)).astype(F32)
    ranking = jnp.sum(mine * before, axis=0, keepdims=True)
    slot = (ids((rows, members), 0) // span).astype(F32)
    placed = (jnp.where(slot == ranking, 1.0, 0.0) * mine_row).astype(BF16)
    wide = (members, LANES)
    row = ids(wide, 0)
    upper = 0.5 * (overlap + flipped)
    columns = [jnp.broadcast_to(upper[:, j : j + 1], wide) for j in range(members)]
    lower = (row == lane_member(ids(wide, 1), members)).astype(F32)
    diagonal = ratio = jnp.zeros(wide, F32)
    for k in range(0, members, 2):
        first, second = columns[k], columns[k + 1]
        a, b, c = first[k : k + 1], first[k + 1 : k + 2], second[k + 1 : k + 2]
        share = b / a
        rest = c - share * b
        diagonal = jnp.where(row == k, a, jnp.where(row == k + 1, rest, diagonal))
        ratio = jnp.where(row == k + 1, share, ratio)
        scale = 1.0 / (a * c - b * b)
        below = row > k + 1
        one = jnp.where(below, (first * c - second * b) * scale, 0.0)
        two = jnp.where(below, (second * a - first * b) * scale, 0.0)
        lower = lower - (one * lower[k : k + 1] + two * lower[k + 1 : k + 2])
        for j in range(k + 2, members):
            column = columns[j]
            columns[j] = column - (one * column[k : k + 1] + two * column[k + 1 : k + 2])
    above = jnp.concatenate([lower[:1], lower[:-1]], axis=0)
    inverse = (lower - ratio * above) / jnp.sqrt(diagonal)
    high, low = halves(inverse)
    same_line = ids((rows, LANES), 0) % span == lane_line(ids((rows, LANES), 1), turn, members)
    blank = jnp.zeros((rows, LANES), BF16)
    chosen = [jnp.where(same_line, dot32(placed, half), 0.0).astype(BF16) for half in (high, low)]
    for i, half in enumerate(chosen + chosen):
        pair = [half, blank] if i < 2 else [blank, half]
        weights_ref[i * rows : (i + 1) * rows, :] = jnp.concatenate(pair, axis=1)


def route_kernel(overlap_ref, weights_ref, *refs):
    parts, (out_hbm, overlap_hbm, staged, semaphores) = refs[:-4], refs[-4:]
    groups = len(parts)
    copies = [pltpu.make_async_copy(overlap_ref, overlap_hbm, semaphores.at[groups])]
    copies[0].start()
    points = staged.shape[3]
    weights = weights_ref[...]
    rows = weights.shape[0] // 4
    span = rows // CAP
    lines = staged.shape[2]
    packs = lines // span
    highs = jnp.concatenate([weights[:rows], weights[2 * rows : 3 * rows]], axis=0)
    group = lax.axis_index("grid") * lax.axis_size("ham") + lax.axis_index("ham")
    for flip, part in enumerate(parts):
        sums = []
        for pack in range(0, packs, 2):
            field = jnp.concatenate([part[pack], part[pack + 1]], axis=1)
            both = dot32(weights, field, NT)
            results = [both[:rows] + both[rows : 2 * rows], both[2 * rows : 3 * rows] + both[3 * rows :]]
            if part.shape[0] > packs:
                place = packs + pack
                rest = dot32(highs, jnp.concatenate([part[place], part[place + 1]], axis=1), NT)
                results = [results[0] + rest[:rows], results[1] + rest[rows:]]
            sums += [result.reshape(CAP, span, points) for result in results]
        staged[flip] = jnp.concatenate(sums, axis=1).astype(BF16)
        start = pl.multiple_of((group ^ flip) * lines, lines)
        target = out_hbm.at[:, pl.ds(start, lines), :]
        copies.append(pltpu.make_async_copy(staged.at[flip], target, semaphores.at[flip]))
        copies[-1].start()
    for copy in copies:
        copy.wait()


def call(kernel, name, shapes, flops, moved, scratch=(), scalars=0, operands=0, remote=False):
    vmem = pl.BlockSpec(memory_space=pltpu.VMEM)
    smem = pl.BlockSpec(memory_space=pltpu.SMEM)
    return pl.pallas_call(
        kernel,
        name=name,
        out_shape=shapes,
        in_specs=[smem] * scalars + [vmem] * operands,
        out_specs=[pl.BlockSpec(memory_space=pl.ANY) if remote else vmem] * len(shapes),
        scratch_shapes=list(scratch),
        compiler_params=pltpu.CompilerParams(vmem_limit_bytes=VMEM_LIMIT),
        cost_estimate=pl.CostEstimate(flops=flops, bytes_accessed=moved, transcendentals=0),
    )


def local(orbitals, coulomb, occupied, owners):
    members, lines, points = orbitals.shape
    grids, near = lax.axis_size("grid"), lax.axis_size("ham")
    groups = grids * near
    padded = -(-points // LANES) * LANES
    span = LANES // members
    packs = lines // span
    assert packs % 2 == 0
    shape = jax.ShapeDtypeStruct
    (packed,) = call(
        pack_kernel,
        "pack",
        [shape((packs, points, LANES), BF16)],
        orbitals.size,
        4 * orbitals.size,
        operands=1,
    )(orbitals)
    guests = exchanged(packed)
    tables = spectral_tables(points)
    (response,) = call(
        response_kernel,
        "response",
        [shape((lines, points, padded), F32)],
        4 * lines * points**3,
        4 * lines * points**2,
        operands=2,
    )(coulomb, tables)
    blocks = len(guests) + 1
    high, parts = call(
        functools.partial(image_kernel, members),
        "image",
        [
            shape((packs, points, LANES), BF16),
            shape((2 * packs, points, LANES), BF16),
        ],
        2 * lines * points * padded * (4 * LANES),
        4 * lines * points**2,
        scalars=1,
        operands=blocks + 1,
    )(occupied, packed, *guests, response)
    (overlap,) = call(
        overlap_kernel,
        "overlap",
        [shape((members, LANES), F32)],
        4 * packs * points * LANES**2,
        8 * orbitals.size,
        operands=2,
    )(orbitals, parts)
    overlaps = [overlap] + [swapped(overlap, flip) for flip in range(1, groups)]
    images = [parts] + [swapped(parts, flip) for flip in range(1, near)]
    for grid in range(1, grids):
        across = swapped(high, grid * near)
        images += [across] + [swapped(across, flip) for flip in range(1, near)]
    cells = lines * groups * points

    intersection, weights = call(
        functools.partial(factor_kernel, cells),
        "factor",
        [shape((members, members), F32), shape((4 * CAP * span, 2 * LANES), BF16)],
        FACTOR_COST,
        members**2 * 4,
        operands=1 + groups,
    )(owners, *overlaps)
    routed, intersection = call(
        route_kernel,
        "route",
        [shape((CAP, groups * lines, points), BF16), shape((members, members), F32)],
        2 * CAP * members * groups * lines * points,
        6 * members * groups * lines * points,
        scratch=[
            pltpu.VMEM((groups, CAP, lines, points), BF16),
            pltpu.SemaphoreType.DMA((groups + 1,)),
        ],
        operands=2 + groups,
        remote=True,
    )(intersection, weights, *images)
    return routed[None, None], intersection[None]


def solution(mesh):
    in_specs = (P("band", ("grid", "ham"), None), P(("grid", "ham"), None), P(), P("band", None))
    out_specs = (P("band", ("grid", "ham"), None, None, None), P("band", None, None))
    return jax.shard_map(local, mesh=mesh, in_specs=in_specs, out_specs=out_specs, check_vma=False)
```

```python
import functools
import math

import jax
import jax.numpy as jnp
import numpy as np
from jax import lax
from jax.experimental import pallas as pl
from jax.experimental.pallas import tpu as pltpu
from jax.sharding import PartitionSpec as P

CAP = 8
LANES = 128
HIGHEST = lax.Precision.HIGHEST
VMEM_LIMIT = 48 * 1024 * 1024
FACTOR_COST = 3_000_000_000
NT = ((1,), (1,))
F32, BF16 = jnp.float32, jnp.bfloat16


def sources(block, count):
    odd = block % 2
    steps = (-2, 2 * odd - 1, 1 - 2 * odd, 2)
    return [(block + step + count) % count for step in steps]


def exchanged(value):
    count = lax.axis_size("band")
    assert count % 4 == 0
    tables = [sources(block, count) for block in range(count)]
    return [
        lax.ppermute(value, "band", [(row[turn], block) for block, row in enumerate(tables)])
        for turn in range(4)
    ]


def swapped(value, flip):
    count = lax.axis_size("grid") * lax.axis_size("ham")
    return lax.ppermute(value, ("grid", "ham"), [(group, group ^ flip) for group in range(count)])


def spectral_tables(points):
    midpoint = points // 2
    ids = np.arange(points)
    frequency = np.where(ids <= midpoint, ids, ids - midpoint)
    angles = (ids[:, None] * frequency[None, :] % points) * (2.0 * math.pi / points)
    forward = np.where((ids <= midpoint)[None, :], np.cos(angles), np.sin(angles))
    single = (frequency == 0) | (ids == midpoint)
    inverse = forward.T * (np.where(single, 1.0, 2.0) / points)[:, None]
    mirror = np.zeros((points, points))
    mirror[frequency, ids] += 0.5
    mirror[(points - frequency) % points, ids] += 0.5
    return jnp.asarray(np.stack([forward.T, inverse.T, mirror]).astype(np.float32)).astype(BF16)


def split(value):
    high = value.astype(BF16)
    return high, value - high.astype(F32)


def halves(value):
    high, rest = split(value)
    return high, rest.astype(BF16)


def dot32(a, b, contract=((1,), (0,))):
    return lax.dot_general(a, b, (contract, ((), ())), preferred_element_type=F32)


def dot_exact(a, b, contract=((1,), (0,))):
    return lax.dot_general(
        a, b, (contract, ((), ())), precision=HIGHEST, preferred_element_type=F32
    )


def ids(shape, axis):
    return lax.broadcasted_iota(jnp.int32, shape, axis)


def lane_member(lane, members):
    return lane % members


def lane_quarter(lane, turn):
    return (lane // (LANES // 4)) ^ turn


def lane_line(lane, turn, members):
    per = LANES // 4 // members
    return lane_quarter(lane, turn) * per + lane % (LANES // 4) // members


def own_turn():
    return lax.axis_index("band") % 4


def rows_of(block, pack, span):
    members, _, points = block.shape
    part = block[:, pack * span : (pack + 1) * span, :]
    return part.reshape(members * span, points)


def pack_kernel(orbitals_ref, out_ref):
    members = orbitals_ref.shape[0]
    span = LANES // members
    block = orbitals_ref[...].astype(F32)
    row, lane = ids((LANES, LANES), 0), ids((LANES, LANES), 1)
    source = lane_member(lane, members) * span + lane_line(lane, own_turn(), members)
    order = (row == source).astype(BF16)
    for pack in range(out_ref.shape[0]):
        rows = rows_of(block, pack, span).T.astype(BF16)
        out_ref[pack] = dot32(rows, order).astype(BF16)


def response_kernel(coulomb_ref, tables_ref, out_ref):
    points = coulomb_ref.shape[1]
    multiplier = dot_exact(coulomb_ref[...], tables_ref[2].astype(F32))
    forward = tables_ref[0]
    inverse = tables_ref[1].astype(F32)
    pad = jnp.zeros((points, out_ref.shape[2] - points), F32)
    for line in range(coulomb_ref.shape[0]):
        high, low = halves(inverse * multiplier[line : line + 1, :])
        out_ref[line, :, :points] = dot32(high, forward) + dot32(low, forward)
        out_ref[line, :, points:] = pad


def image_kernel(members, occupied_ref, *refs):
    blocks, (response_ref, high_ref, halves_ref) = refs[:-3], refs[-3:]
    packs, points, _ = blocks[0].shape
    padded = response_ref.shape[2]
    span = LANES // members
    per = span // 4
    total = lax.axis_size("band")
    position = lax.axis_index("band")
    places = [position] + sources(position, total)
    turns = [place % 4 for place in places]
    lane = ids((1, LANES), 1)
    own_line = lane_line(lane, turns[0], members)
    filled = [lane_member(lane, members) < occupied_ref[place] for place in places]
    quarters = [lane_quarter(lane, turn) for turn in turns]
    step = lane % (LANES // 4) // members
    apart, merged = 1, (0, 2, 3, 4)
    spare = padded - points
    cuts = points // spare
    assert cuts * spare == points and LANES % spare == 0
    blank = jnp.zeros((spare, 2 * LANES), BF16)
    kernels = [[[] for _ in range(cuts)] for _ in range(packs)]
    for pack in range(packs):
        tiles = [block[pack] for block in blocks]
        for quarter in range(4):
            here = [(q == quarter) for q in quarters]
            together = tiles[merged[0]]
            for m in merged[1:]:
                together = jnp.where(here[m], tiles[m], together)
            window = jnp.concatenate([together, tiles[apart]], axis=1)
            occupied = sum((here[m] & filled[m]).astype(F32) for m in merged)
            beside = (here[apart] & filled[apart]).astype(F32)
            both = jnp.concatenate([occupied, beside], axis=1)
            steps = jnp.concatenate([step, step], axis=1)
            masked = jnp.concatenate(
                [window * jnp.where(steps == k, both, 0.0).astype(BF16) for k in range(per)], axis=0
            )
            gram = dot32(masked, jnp.concatenate([window, blank], axis=0), NT)
            first = pack * span + quarter * per
            response = response_ref[first : first + per].reshape(per * points, padded)
            weighted = gram * response
            for place in range(0, per * points, spare):
                cut = place // spare % cuts
                part = weighted[place : place + spare]
                tile = cut * spare // LANES * LANES
                _, low = split(part[:, tile : tile + LANES])
                shift = LANES - spare - cut * spare % LANES
                low = pltpu.roll(low, shift, axis=1) if shift else low
                last = jnp.where(lane < LANES - spare, part[:, -LANES:], low)
                part = jnp.concatenate([part[:, :-LANES], last], axis=1)
                kernels[pack][cut].append(part.astype(BF16))
    for pack in range(packs):
        tile = blocks[0][pack]
        image = []
        for cut in range(cuts):
            native = jnp.concatenate([tile, tile[cut * spare : (cut + 1) * spare]], axis=0)
            fields = dot32(jnp.concatenate(kernels[pack][cut], axis=0), native)
            rows = jnp.zeros((spare, LANES), F32)
            for line in range(span):
                rows = jnp.where(own_line == line, fields[line * spare : (line + 1) * spare], rows)
            image.append(rows)
        image = jnp.concatenate(image, axis=0)
        high, low = halves(image)
        high_ref[pack] = high
        halves_ref[pack] = high
        halves_ref[packs + pack] = low


def overlap_kernel(orbitals_ref, halves_ref, out_ref):
    members, _, _ = orbitals_ref.shape
    span = LANES // members
    natives = orbitals_ref[...].astype(F32)
    square = (LANES, LANES)
    same_line = ids(square, 0) % span == lane_line(ids(square, 1), own_turn(), members)
    cross = jnp.zeros(square, F32)
    packs = halves_ref.shape[0] // 2
    for pack in range(packs):
        rows = rows_of(natives, pack, span).astype(BF16)
        both = jnp.concatenate([halves_ref[pack], halves_ref[packs + pack]], axis=1)
        product = dot32(rows, both)
        cross = cross + (product[:, :LANES] + product[:, LANES:])
    out_ref[...] = jnp.where(same_line, cross, 0.0).reshape(members, span, LANES).sum(axis=1)


def factor_kernel(cells, owners_ref, *refs):
    parts, (overlap_ref, weights_ref) = refs[:-2], refs[-2:]
    members = owners_ref.shape[0]
    span = LANES // members
    turn = own_turn()
    sums = [part[...] for part in parts]
    while len(sums) > 1:
        sums = [a + b for a, b in zip(sums[::2], sums[1::2])]
    high, rest = split(sums[0])
    pieces = [high, *halves(rest)]
    across = (members, LANES)
    gather = (ids(across, 0) == lane_member(ids(across, 1), members)).astype(BF16)
    overlap = sum(dot32(piece, gather, NT) for piece in pieces) * (1.0 / cells)
    flipped = sum(dot32(gather, piece, NT) for piece in pieces) * (1.0 / cells)
    overlap_ref[...] = overlap
    rows = CAP * span
    square = (members, members)
    group = lax.axis_index("grid") * lax.axis_size("ham") + lax.axis_index("ham")
    mine = (owners_ref[...] == group).astype(F32)
    eye = (ids(square, 0) == ids(square, 1)).astype(F32)
    mine_row = jnp.sum(mine * eye, axis=0, keepdims=True)
    before = (ids(square, 0) < ids(square, 1)).astype(F32)
    ranking = jnp.sum(mine * before, axis=0, keepdims=True)
    slot = (ids((rows, members), 0) // span).astype(F32)
    placed = (jnp.where(slot == ranking, 1.0, 0.0) * mine_row).astype(BF16)
    wide = (members, LANES)
    row = ids(wide, 0)
    upper = 0.5 * (overlap + flipped)
    columns = [jnp.broadcast_to(upper[:, j : j + 1], wide) for j in range(members)]
    lower = (row == lane_member(ids(wide, 1), members)).astype(F32)
    diagonal = ratio = jnp.zeros(wide, F32)
    for k in range(0, members, 2):
        first, second = columns[k], columns[k + 1]
        a, b, c = first[k : k + 1], first[k + 1 : k + 2], second[k + 1 : k + 2]
        share = b / a
        rest = c - share * b
        diagonal = jnp.where(row == k, a, jnp.where(row == k + 1, rest, diagonal))
        ratio = jnp.where(row == k + 1, share, ratio)
        scale = 1.0 / (a * c - b * b)
        below = row > k + 1
        one = jnp.where(below, (first * c - second * b) * scale, 0.0)
        two = jnp.where(below, (second * a - first * b) * scale, 0.0)
        lower = lower - (one * lower[k : k + 1] + two * lower[k + 1 : k + 2])
        for j in range(k + 2, members):
            column = columns[j]
            columns[j] = column - (one * column[k : k + 1] + two * column[k + 1 : k + 2])
    above = jnp.concatenate([lower[:1], lower[:-1]], axis=0)
    inverse = (lower - ratio * above) / jnp.sqrt(diagonal)
    high, low = halves(inverse)
    same_line = ids((rows, LANES), 0) % span == lane_line(ids((rows, LANES), 1), turn, members)
    blank = jnp.zeros((rows, LANES), BF16)
    chosen = [jnp.where(same_line, dot32(placed, half), 0.0).astype(BF16) for half in (high, low)]
    for i, half in enumerate(chosen + chosen):
        pair = [half, blank] if i < 2 else [blank, half]
        weights_ref[i * rows : (i + 1) * rows, :] = jnp.concatenate(pair, axis=1)


def route_kernel(overlap_ref, weights_ref, *refs):
    parts, (out_hbm, overlap_hbm, staged, semaphores) = refs[:-4], refs[-4:]
    groups = len(parts)
    copies = [pltpu.make_async_copy(overlap_ref, overlap_hbm, semaphores.at[groups])]
    copies[0].start()
    points = staged.shape[3]
    weights = weights_ref[...]
    rows = weights.shape[0] // 4
    span = rows // CAP
    lines = staged.shape[2]
    packs = lines // span
    highs = jnp.concatenate([weights[:rows], weights[2 * rows : 3 * rows]], axis=0)
    group = lax.axis_index("grid") * lax.axis_size("ham") + lax.axis_index("ham")
    for flip, part in enumerate(parts):
        sums = []
        for pack in range(0, packs, 2):
            field = jnp.concatenate([part[pack], part[pack + 1]], axis=1)
            both = dot32(weights, field, NT)
            results = [both[:rows] + both[rows : 2 * rows], both[2 * rows : 3 * rows] + both[3 * rows :]]
            if part.shape[0] > packs:
                place = packs + pack
                rest = dot32(highs, jnp.concatenate([part[place], part[place + 1]], axis=1), NT)
                results = [results[0] + rest[:rows], results[1] + rest[rows:]]
            sums += [result.reshape(CAP, span, points) for result in results]
        staged[flip] = jnp.concatenate(sums, axis=1).astype(BF16)
        start = pl.multiple_of((group ^ flip) * lines, lines)
        target = out_hbm.at[:, pl.ds(start, lines), :]
        copies.append(pltpu.make_async_copy(staged.at[flip], target, semaphores.at[flip]))
        copies[-1].start()
    for copy in copies:
        copy.wait()


def call(kernel, name, shapes, flops, moved, scratch=(), scalars=0, operands=0, remote=False):
    vmem = pl.BlockSpec(memory_space=pltpu.VMEM)
    smem = pl.BlockSpec(memory_space=pltpu.SMEM)
    return pl.pallas_call(
        kernel,
        name=name,
        out_shape=shapes,
        in_specs=[smem] * scalars + [vmem] * operands,
        out_specs=[pl.BlockSpec(memory_space=pl.ANY) if remote else vmem] * len(shapes),
        scratch_shapes=list(scratch),
        compiler_params=pltpu.CompilerParams(vmem_limit_bytes=VMEM_LIMIT),
        cost_estimate=pl.CostEstimate(flops=flops, bytes_accessed=moved, transcendentals=0),
    )


def local(orbitals, coulomb, occupied, owners):
    members, lines, points = orbitals.shape
    grids, near = lax.axis_size("grid"), lax.axis_size("ham")
    groups = grids * near
    padded = -(-points // LANES) * LANES
    span = LANES // members
    packs = lines // span
    assert packs % 2 == 0
    shape = jax.ShapeDtypeStruct
    (packed,) = call(
        pack_kernel,
        "pack",
        [shape((packs, points, LANES), BF16)],
        orbitals.size,
        4 * orbitals.size,
        operands=1,
    )(orbitals)
    guests = exchanged(packed)
    tables = spectral_tables(points)
    (response,) = call(
        response_kernel,
        "response",
        [shape((lines, points, padded), F32)],
        4 * lines * points**3,
        4 * lines * points**2,
        operands=2,
    )(coulomb, tables)
    blocks = len(guests) + 1
    high, parts = call(
        functools.partial(image_kernel, members),
        "image",
        [
            shape((packs, points, LANES), BF16),
            shape((2 * packs, points, LANES), BF16),
        ],
        2 * lines * points * padded * (4 * LANES),
        4 * lines * points**2,
        scalars=1,
        operands=blocks + 1,
    )(occupied, packed, *guests, response)
    (overlap,) = call(
        overlap_kernel,
        "overlap",
        [shape((members, LANES), F32)],
        4 * packs * points * LANES**2,
        8 * orbitals.size,
        operands=2,
    )(orbitals, parts)
    overlaps = [overlap] + [swapped(overlap, flip) for flip in range(1, groups)]
    images = [parts] + [swapped(parts, flip) for flip in range(1, near)]
    for grid in range(1, grids):
        across = swapped(high, grid * near)
        images += [across] + [swapped(across, flip) for flip in range(1, near)]
    cells = lines * groups * points

    intersection, weights = call(
        functools.partial(factor_kernel, cells),
        "factor",
        [shape((members, members), F32), shape((4 * CAP * span, 2 * LANES), BF16)],
        FACTOR_COST,
        members**2 * 4,
        operands=1 + groups,
    )(owners, *overlaps)
    routed, intersection = call(
        route_kernel,
        "route",
        [shape((CAP, groups * lines, points), BF16), shape((members, members), F32)],
        2 * CAP * members * groups * lines * points,
        6 * members * groups * lines * points,
        scratch=[
            pltpu.VMEM((groups, CAP, lines, points), BF16),
            pltpu.SemaphoreType.DMA((groups + 1,)),
        ],
        operands=2 + groups,
        remote=True,
    )(intersection, weights, *images)
    return routed[None, None], intersection[None]


def solution(mesh):
    in_specs = (P("band", ("grid", "ham"), None), P(("grid", "ham"), None), P(), P("band", None))
    out_specs = (P("band", ("grid", "ham"), None, None, None), P("band", None, None))
    return jax.shard_map(local, mesh=mesh, in_specs=in_specs, out_specs=out_specs, check_vma=False)
```

```python
import functools
import math

import jax
import jax.numpy as jnp
import numpy as np
from jax import lax
from jax.experimental import pallas as pl
from jax.experimental.pallas import tpu as pltpu
from jax.sharding import PartitionSpec as P

CAP = 8
LANES = 128
HIGHEST = lax.Precision.HIGHEST
VMEM_LIMIT = 48 * 1024 * 1024
FACTOR_COST = 3_000_000_000
NT = ((1,), (1,))
F32, BF16 = jnp.float32, jnp.bfloat16


STEPS = (-1, -2, 2, 1)


def sources(block, count):
    return [(block + step + count) % count for step in STEPS]


def exchanged(value):
    count = lax.axis_size("band")
    assert count % 4 == 0
    tables = [sources(block, count) for block in range(count)]
    return [
        lax.ppermute(value, "band", [(row[turn], block) for block, row in enumerate(tables)])
        for turn in range(4)
    ]


def swapped(value, flip):
    count = lax.axis_size("grid") * lax.axis_size("ham")
    return lax.ppermute(value, ("grid", "ham"), [(group, group ^ flip) for group in range(count)])


def spectral_tables(points):
    midpoint = points // 2
    ids = np.arange(points)
    frequency = np.where(ids <= midpoint, ids, ids - midpoint)
    angles = (ids[:, None] * frequency[None, :] % points) * (2.0 * math.pi / points)
    forward = np.where((ids <= midpoint)[None, :], np.cos(angles), np.sin(angles))
    single = (frequency == 0) | (ids == midpoint)
    inverse = forward.T * (np.where(single, 1.0, 2.0) / points)[:, None]
    mirror = np.zeros((points, points))
    mirror[frequency, ids] += 0.5
    mirror[(points - frequency) % points, ids] += 0.5
    return jnp.asarray(np.stack([forward.T, inverse.T, mirror]).astype(np.float32)).astype(BF16)


def split(value):
    high = value.astype(BF16)
    return high, value - high.astype(F32)


def halves(value):
    high, rest = split(value)
    return high, rest.astype(BF16)


def dot32(a, b, contract=((1,), (0,))):
    return lax.dot_general(a, b, (contract, ((), ())), preferred_element_type=F32)


def dot_exact(a, b, contract=((1,), (0,))):
    return lax.dot_general(
        a, b, (contract, ((), ())), precision=HIGHEST, preferred_element_type=F32
    )


def ids(shape, axis):
    return lax.broadcasted_iota(jnp.int32, shape, axis)


def lane_member(lane, members):
    return lane % members


def lane_quarter(lane, turn):
    return (lane // (LANES // 4)) ^ turn


def lane_line(lane, turn, members):
    per = LANES // 4 // members
    return lane_quarter(lane, turn) * per + lane % (LANES // 4) // members


def own_turn():
    return lax.axis_index("band") % 4


def rows_of(block, pack, span):
    members, _, points = block.shape
    part = block[:, pack * span : (pack + 1) * span, :]
    return part.reshape(members * span, points)


def pack_kernel(orbitals_ref, out_ref):
    members = orbitals_ref.shape[0]
    span = LANES // members
    block = orbitals_ref[...].astype(F32)
    row, lane = ids((LANES, LANES), 0), ids((LANES, LANES), 1)
    source = lane_member(lane, members) * span + lane_line(lane, own_turn(), members)
    order = (row == source).astype(BF16)
    for pack in range(out_ref.shape[0]):
        rows = rows_of(block, pack, span).T.astype(BF16)
        out_ref[pack] = dot32(rows, order).astype(BF16)


def response_kernel(coulomb_ref, tables_ref, out_ref):
    points = coulomb_ref.shape[1]
    multiplier = dot_exact(coulomb_ref[...], tables_ref[2].astype(F32))
    forward = tables_ref[0]
    inverse = tables_ref[1].astype(F32)
    pad = jnp.zeros((points, out_ref.shape[2] - points), F32)
    for line in range(coulomb_ref.shape[0]):
        high, low = halves(inverse * multiplier[line : line + 1, :])
        out_ref[line, :, :points] = dot32(high, forward) + dot32(low, forward)
        out_ref[line, :, points:] = pad


def image_kernel(members, occupied_ref, *refs):
    blocks, (response_ref, high_ref, halves_ref) = refs[:-3], refs[-3:]
    packs, points, _ = blocks[0].shape
    padded = response_ref.shape[2]
    span = LANES // members
    per = span // 4
    total = lax.axis_size("band")
    position = lax.axis_index("band")
    places = [position] + sources(position, total)
    turns = [place % 4 for place in places]
    lane = ids((1, LANES), 1)
    own_line = lane_line(lane, turns[0], members)
    filled = [lane_member(lane, members) < occupied_ref[place] for place in places]
    quarters = [lane_quarter(lane, turn) for turn in turns]
    step = lane % (LANES // 4) // members
    apart, merged = 2, (0, 1, 3, 4)
    spare = padded - points
    cuts = points // spare
    assert cuts * spare == points and LANES % spare == 0
    blank = jnp.zeros((spare, 2 * LANES), BF16)
    kernels = [[[] for _ in range(cuts)] for _ in range(packs)]
    for pack in range(packs):
        tiles = [block[pack] for block in blocks]
        for quarter in range(4):
            here = [(q == quarter) for q in quarters]
            together = tiles[merged[0]]
            for m in merged[1:]:
                together = jnp.where(here[m], tiles[m], together)
            window = jnp.concatenate([together, tiles[apart]], axis=1)
            occupied = sum((here[m] & filled[m]).astype(F32) for m in merged)
            beside = (here[apart] & filled[apart]).astype(F32)
            both = jnp.concatenate([occupied, beside], axis=1)
            steps = jnp.concatenate([step, step], axis=1)
            masked = jnp.concatenate(
                [window * jnp.where(steps == k, both, 0.0).astype(BF16) for k in range(per)], axis=0
            )
            gram = dot32(masked, jnp.concatenate([window, blank], axis=0), NT)
            first = pack * span + quarter * per
            response = response_ref[first : first + per].reshape(per * points, padded)
            weighted = gram * response
            for place in range(0, per * points, spare):
                cut = place // spare % cuts
                part = weighted[place : place + spare]
                tile = cut * spare // LANES * LANES
                _, low = split(part[:, tile : tile + LANES])
                shift = LANES - spare - cut * spare % LANES
                low = pltpu.roll(low, shift, axis=1) if shift else low
                last = jnp.where(lane < LANES - spare, part[:, -LANES:], low)
                part = jnp.concatenate([part[:, :-LANES], last], axis=1)
                kernels[pack][cut].append(part.astype(BF16))
    for pack in range(packs):
        tile = blocks[0][pack]
        image = []
        for cut in range(cuts):
            native = jnp.concatenate([tile, tile[cut * spare : (cut + 1) * spare]], axis=0)
            fields = dot32(jnp.concatenate(kernels[pack][cut], axis=0), native)
            rows = jnp.zeros((spare, LANES), F32)
            for line in range(span):
                rows = jnp.where(own_line == line, fields[line * spare : (line + 1) * spare], rows)
            image.append(rows)
        image = jnp.concatenate(image, axis=0)
        high, low = halves(image)
        high_ref[pack] = high
        halves_ref[pack] = high
        halves_ref[packs + pack] = low


def overlap_kernel(orbitals_ref, halves_ref, out_ref):
    members, _, _ = orbitals_ref.shape
    span = LANES // members
    natives = orbitals_ref[...].astype(F32)
    square = (LANES, LANES)
    same_line = ids(square, 0) % span == lane_line(ids(square, 1), own_turn(), members)
    cross = jnp.zeros(square, F32)
    packs = halves_ref.shape[0] // 2
    for pack in range(packs):
        rows = rows_of(natives, pack, span).astype(BF16)
        both = jnp.concatenate([halves_ref[pack], halves_ref[packs + pack]], axis=1)
        product = dot32(rows, both)
        cross = cross + (product[:, :LANES] + product[:, LANES:])
    out_ref[...] = jnp.where(same_line, cross, 0.0).reshape(members, span, LANES).sum(axis=1)


def factor_kernel(cells, owners_ref, *refs):
    parts, (overlap_ref, weights_ref) = refs[:-2], refs[-2:]
    members = owners_ref.shape[0]
    span = LANES // members
    turn = own_turn()
    sums = [part[...] for part in parts]
    while len(sums) > 1:
        sums = [a + b for a, b in zip(sums[::2], sums[1::2])]
    high, rest = split(sums[0])
    pieces = [high, *halves(rest)]
    across = (members, LANES)
    gather = (ids(across, 0) == lane_member(ids(across, 1), members)).astype(BF16)
    overlap = sum(dot32(piece, gather, NT) for piece in pieces) * (1.0 / cells)
    flipped = sum(dot32(gather, piece, NT) for piece in pieces) * (1.0 / cells)
    overlap_ref[...] = overlap
    rows = CAP * span
    square = (members, members)
    group = lax.axis_index("grid") * lax.axis_size("ham") + lax.axis_index("ham")
    mine = (owners_ref[...] == group).astype(F32)
    eye = (ids(square, 0) == ids(square, 1)).astype(F32)
    mine_row = jnp.sum(mine * eye, axis=0, keepdims=True)
    before = (ids(square, 0) < ids(square, 1)).astype(F32)
    ranking = jnp.sum(mine * before, axis=0, keepdims=True)
    slot = (ids((rows, members), 0) // span).astype(F32)
    placed = (jnp.where(slot == ranking, 1.0, 0.0) * mine_row).astype(BF16)
    wide = (members, LANES)
    row = ids(wide, 0)
    upper = 0.5 * (overlap + flipped)
    columns = [jnp.broadcast_to(upper[:, j : j + 1], wide) for j in range(members)]
    lower = (row == lane_member(ids(wide, 1), members)).astype(F32)
    diagonal = ratio = jnp.zeros(wide, F32)
    for k in range(0, members, 2):
        first, second = columns[k], columns[k + 1]
        a, b, c = first[k : k + 1], first[k + 1 : k + 2], second[k + 1 : k + 2]
        share = b / a
        rest = c - share * b
        diagonal = jnp.where(row == k, a, jnp.where(row == k + 1, rest, diagonal))
        ratio = jnp.where(row == k + 1, share, ratio)
        scale = 1.0 / (a * c - b * b)
        below = row > k + 1
        one = jnp.where(below, (first * c - second * b) * scale, 0.0)
        two = jnp.where(below, (second * a - first * b) * scale, 0.0)
        lower = lower - (one * lower[k : k + 1] + two * lower[k + 1 : k + 2])
        for j in range(k + 2, members):
            column = columns[j]
            columns[j] = column - (one * column[k : k + 1] + two * column[k + 1 : k + 2])
    above = jnp.concatenate([lower[:1], lower[:-1]], axis=0)
    inverse = (lower - ratio * above) / jnp.sqrt(diagonal)
    high, low = halves(inverse)
    same_line = ids((rows, LANES), 0) % span == lane_line(ids((rows, LANES), 1), turn, members)
    blank = jnp.zeros((rows, LANES), BF16)
    chosen = [jnp.where(same_line, dot32(placed, half), 0.0).astype(BF16) for half in (high, low)]
    for i, half in enumerate(chosen + chosen):
        pair = [half, blank] if i < 2 else [blank, half]
        weights_ref[i * rows : (i + 1) * rows, :] = jnp.concatenate(pair, axis=1)


def route_kernel(overlap_ref, weights_ref, *refs):
    parts, (out_hbm, overlap_hbm, staged, semaphores) = refs[:-4], refs[-4:]
    groups = len(parts)
    copies = [pltpu.make_async_copy(overlap_ref, overlap_hbm, semaphores.at[groups])]
    copies[0].start()
    points = staged.shape[3]
    weights = weights_ref[...]
    rows = weights.shape[0] // 4
    span = rows // CAP
    lines = staged.shape[2]
    packs = lines // span
    highs = jnp.concatenate([weights[:rows], weights[2 * rows : 3 * rows]], axis=0)
    group = lax.axis_index("grid") * lax.axis_size("ham") + lax.axis_index("ham")
    for flip, part in enumerate(parts):
        sums = []
        for pack in range(0, packs, 2):
            field = jnp.concatenate([part[pack], part[pack + 1]], axis=1)
            both = dot32(weights, field, NT)
            results = [both[:rows] + both[rows : 2 * rows], both[2 * rows : 3 * rows] + both[3 * rows :]]
            if part.shape[0] > packs:
                place = packs + pack
                rest = dot32(highs, jnp.concatenate([part[place], part[place + 1]], axis=1), NT)
                results = [results[0] + rest[:rows], results[1] + rest[rows:]]
            sums += [result.reshape(CAP, span, points) for result in results]
        staged[flip] = jnp.concatenate(sums, axis=1).astype(BF16)
        start = pl.multiple_of((group ^ flip) * lines, lines)
        target = out_hbm.at[:, pl.ds(start, lines), :]
        copies.append(pltpu.make_async_copy(staged.at[flip], target, semaphores.at[flip]))
        copies[-1].start()
    for copy in copies:
        copy.wait()


def call(kernel, name, shapes, flops, moved, scratch=(), scalars=0, operands=0, remote=False):
    vmem = pl.BlockSpec(memory_space=pltpu.VMEM)
    smem = pl.BlockSpec(memory_space=pltpu.SMEM)
    return pl.pallas_call(
        kernel,
        name=name,
        out_shape=shapes,
        in_specs=[smem] * scalars + [vmem] * operands,
        out_specs=[pl.BlockSpec(memory_space=pl.ANY) if remote else vmem] * len(shapes),
        scratch_shapes=list(scratch),
        compiler_params=pltpu.CompilerParams(vmem_limit_bytes=VMEM_LIMIT),
        cost_estimate=pl.CostEstimate(flops=flops, bytes_accessed=moved, transcendentals=0),
    )


def local(orbitals, coulomb, occupied, owners):
    members, lines, points = orbitals.shape
    grids, near = lax.axis_size("grid"), lax.axis_size("ham")
    groups = grids * near
    padded = -(-points // LANES) * LANES
    span = LANES // members
    packs = lines // span
    assert packs % 2 == 0
    shape = jax.ShapeDtypeStruct
    (packed,) = call(
        pack_kernel,
        "pack",
        [shape((packs, points, LANES), BF16)],
        orbitals.size,
        4 * orbitals.size,
        operands=1,
    )(orbitals)
    guests = exchanged(packed)
    tables = spectral_tables(points)
    (response,) = call(
        response_kernel,
        "response",
        [shape((lines, points, padded), F32)],
        4 * lines * points**3,
        4 * lines * points**2,
        operands=2,
    )(coulomb, tables)
    blocks = len(guests) + 1
    high, parts = call(
        functools.partial(image_kernel, members),
        "image",
        [
            shape((packs, points, LANES), BF16),
            shape((2 * packs, points, LANES), BF16),
        ],
        2 * lines * points * padded * (4 * LANES),
        4 * lines * points**2,
        scalars=1,
        operands=blocks + 1,
    )(occupied, packed, *guests, response)
    (overlap,) = call(
        overlap_kernel,
        "overlap",
        [shape((members, LANES), F32)],
        4 * packs * points * LANES**2,
        8 * orbitals.size,
        operands=2,
    )(orbitals, parts)
    overlaps = [overlap] + [swapped(overlap, flip) for flip in range(1, groups)]
    images = [parts] + [swapped(parts, flip) for flip in range(1, near)]
    for grid in range(1, grids):
        across = swapped(high, grid * near)
        images += [across] + [swapped(across, flip) for flip in range(1, near)]
    cells = lines * groups * points

    intersection, weights = call(
        functools.partial(factor_kernel, cells),
        "factor",
        [shape((members, members), F32), shape((4 * CAP * span, 2 * LANES), BF16)],
        FACTOR_COST,
        members**2 * 4,
        operands=1 + groups,
    )(owners, *overlaps)
    routed, intersection = call(
        route_kernel,
        "route",
        [shape((CAP, groups * lines, points), BF16), shape((members, members), F32)],
        2 * CAP * members * groups * lines * points,
        6 * members * groups * lines * points,
        scratch=[
            pltpu.VMEM((groups, CAP, lines, points), BF16),
            pltpu.SemaphoreType.DMA((groups + 1,)),
        ],
        operands=2 + groups,
        remote=True,
    )(intersection, weights, *images)
    return routed[None, None], intersection[None]


def solution(mesh):
    in_specs = (P("band", ("grid", "ham"), None), P(("grid", "ham"), None), P(), P("band", None))
    out_specs = (P("band", ("grid", "ham"), None, None, None), P("band", None, None))
    return jax.shard_map(local, mesh=mesh, in_specs=in_specs, out_specs=out_specs, check_vma=False)
```

```python
import functools
import math

import jax
import jax.numpy as jnp
import numpy as np
from jax import lax
from jax.experimental import pallas as pl
from jax.experimental.pallas import tpu as pltpu
from jax.sharding import PartitionSpec as P

CAP = 8
LANES = 128
HIGHEST = lax.Precision.HIGHEST
VMEM_LIMIT = 48 * 1024 * 1024
FACTOR_COST = 3_000_000_000
NT = ((1,), (1,))
F32, BF16 = jnp.float32, jnp.bfloat16


TURNS = ((2, True, False), (-1, True, True), (-2, True, True), (1, True, True), (2, False, True))
STEPS = (2, -1, -2, 1)


def sources(block, count):
    return [(block + step + count) % count for step in STEPS]


def exchanged(value):
    count = lax.axis_size("band")
    assert count % 4 == 0
    arrivals = []
    for step, inside, around in TURNS:
        pairs = [((block + step) % count, block) for block in range(count)]
        pairs = [(a, b) for a, b in pairs if (inside if a - b == step else around)]
        arrivals.append(lax.ppermute(value, "band", pairs))
    return arrivals


def swapped(value, flip):
    count = lax.axis_size("grid") * lax.axis_size("ham")
    return lax.ppermute(value, ("grid", "ham"), [(group, group ^ flip) for group in range(count)])


def spectral_tables(points):
    midpoint = points // 2
    ids = np.arange(points)
    frequency = np.where(ids <= midpoint, ids, ids - midpoint)
    angles = (ids[:, None] * frequency[None, :] % points) * (2.0 * math.pi / points)
    forward = np.where((ids <= midpoint)[None, :], np.cos(angles), np.sin(angles))
    single = (frequency == 0) | (ids == midpoint)
    inverse = forward.T * (np.where(single, 1.0, 2.0) / points)[:, None]
    mirror = np.zeros((points, points))
    mirror[frequency, ids] += 0.5
    mirror[(points - frequency) % points, ids] += 0.5
    return jnp.asarray(np.stack([forward.T, inverse.T, mirror]).astype(np.float32)).astype(BF16)


def split(value):
    high = value.astype(BF16)
    return high, value - high.astype(F32)


def halves(value):
    high, rest = split(value)
    return high, rest.astype(BF16)


def dot32(a, b, contract=((1,), (0,))):
    return lax.dot_general(a, b, (contract, ((), ())), preferred_element_type=F32)


def dot_exact(a, b, contract=((1,), (0,))):
    return lax.dot_general(
        a, b, (contract, ((), ())), precision=HIGHEST, preferred_element_type=F32
    )


def ids(shape, axis):
    return lax.broadcasted_iota(jnp.int32, shape, axis)


def lane_member(lane, members):
    return lane % members


def lane_quarter(lane, turn):
    return (lane // (LANES // 4)) ^ turn


def lane_line(lane, turn, members):
    per = LANES // 4 // members
    return lane_quarter(lane, turn) * per + lane % (LANES // 4) // members


def own_turn():
    return lax.axis_index("band") % 4


def rows_of(block, pack, span):
    members, _, points = block.shape
    part = block[:, pack * span : (pack + 1) * span, :]
    return part.reshape(members * span, points)


def pack_kernel(orbitals_ref, out_ref):
    members = orbitals_ref.shape[0]
    span = LANES // members
    block = orbitals_ref[...].astype(F32)
    row, lane = ids((LANES, LANES), 0), ids((LANES, LANES), 1)
    source = lane_member(lane, members) * span + lane_line(lane, own_turn(), members)
    order = (row == source).astype(BF16)
    for pack in range(out_ref.shape[0]):
        rows = rows_of(block, pack, span).T.astype(BF16)
        out_ref[pack] = dot32(rows, order).astype(BF16)


def response_kernel(coulomb_ref, tables_ref, out_ref):
    points = coulomb_ref.shape[1]
    multiplier = dot_exact(coulomb_ref[...], tables_ref[2].astype(F32))
    forward = tables_ref[0]
    inverse = tables_ref[1].astype(F32)
    pad = jnp.zeros((points, out_ref.shape[2] - points), F32)
    for line in range(coulomb_ref.shape[0]):
        high, low = halves(inverse * multiplier[line : line + 1, :])
        out_ref[line, :, :points] = dot32(high, forward) + dot32(low, forward)
        out_ref[line, :, points:] = pad


def image_kernel(members, occupied_ref, *refs):
    blocks, (response_ref, high_ref, halves_ref) = refs[:-3], refs[-3:]
    packs, points, _ = blocks[0].shape
    padded = response_ref.shape[2]
    span = LANES // members
    per = span // 4
    total = lax.axis_size("band")
    position = lax.axis_index("band")
    places = [position] + sources(position, total)
    turns = [place % 4 for place in places]
    lane = ids((1, LANES), 1)
    own_line = lane_line(lane, turns[0], members)
    filled = [lane_member(lane, members) < occupied_ref[place] for place in places]
    quarters = [lane_quarter(lane, turn) for turn in turns]
    step = lane % (LANES // 4) // members
    apart, merged = 1, (0, 2, 3, 4)
    spare = padded - points
    cuts = points // spare
    assert cuts * spare == points and LANES % spare == 0
    blank = jnp.zeros((spare, 2 * LANES), BF16)
    kernels = [[[] for _ in range(cuts)] for _ in range(packs)]
    for pack in range(packs):
        tiles = [block[pack] for block in blocks[:-1]]
        tiles[apart] = tiles[apart] + blocks[-1][pack]
        for quarter in range(4):
            here = [(q == quarter) for q in quarters]
            together = tiles[merged[0]]
            for m in merged[1:]:
                together = jnp.where(here[m], tiles[m], together)
            window = jnp.concatenate([together, tiles[apart]], axis=1)
            occupied = sum((here[m] & filled[m]).astype(F32) for m in merged)
            beside = (here[apart] & filled[apart]).astype(F32)
            both = jnp.concatenate([occupied, beside], axis=1)
            steps = jnp.concatenate([step, step], axis=1)
            masked = jnp.concatenate(
                [window * jnp.where(steps == k, both, 0.0).astype(BF16) for k in range(per)], axis=0
            )
            gram = dot32(masked, jnp.concatenate([window, blank], axis=0), NT)
            first = pack * span + quarter * per
            response = response_ref[first : first + per].reshape(per * points, padded)
            weighted = gram * response
            for place in range(0, per * points, spare):
                cut = place // spare % cuts
                part = weighted[place : place + spare]
                tile = cut * spare // LANES * LANES
                _, low = split(part[:, tile : tile + LANES])
                shift = LANES - spare - cut * spare % LANES
                low = pltpu.roll(low, shift, axis=1) if shift else low
                last = jnp.where(lane < LANES - spare, part[:, -LANES:], low)
                part = jnp.concatenate([part[:, :-LANES], last], axis=1)
                kernels[pack][cut].append(part.astype(BF16))
    for pack in range(packs):
        tile = blocks[0][pack]
        image = []
        for cut in range(cuts):
            native = jnp.concatenate([tile, tile[cut * spare : (cut + 1) * spare]], axis=0)
            fields = dot32(jnp.concatenate(kernels[pack][cut], axis=0), native)
            rows = jnp.zeros((spare, LANES), F32)
            for line in range(span):
                rows = jnp.where(own_line == line, fields[line * spare : (line + 1) * spare], rows)
            image.append(rows)
        image = jnp.concatenate(image, axis=0)
        high, low = halves(image)
        high_ref[pack] = high
        halves_ref[pack] = high
        halves_ref[packs + pack] = low


def overlap_kernel(orbitals_ref, halves_ref, out_ref):
    members, _, _ = orbitals_ref.shape
    span = LANES // members
    natives = orbitals_ref[...].astype(F32)
    square = (LANES, LANES)
    same_line = ids(square, 0) % span == lane_line(ids(square, 1), own_turn(), members)
    cross = jnp.zeros(square, F32)
    packs = halves_ref.shape[0] // 2
    for pack in range(packs):
        rows = rows_of(natives, pack, span).astype(BF16)
        both = jnp.concatenate([halves_ref[pack], halves_ref[packs + pack]], axis=1)
        product = dot32(rows, both)
        cross = cross + (product[:, :LANES] + product[:, LANES:])
    out_ref[...] = jnp.where(same_line, cross, 0.0).reshape(members, span, LANES).sum(axis=1)


def factor_kernel(cells, owners_ref, *refs):
    parts, (overlap_ref, weights_ref) = refs[:-2], refs[-2:]
    members = owners_ref.shape[0]
    span = LANES // members
    turn = own_turn()
    sums = [part[...] for part in parts]
    while len(sums) > 1:
        sums = [a + b for a, b in zip(sums[::2], sums[1::2])]
    high, rest = split(sums[0])
    pieces = [high, *halves(rest)]
    across = (members, LANES)
    gather = (ids(across, 0) == lane_member(ids(across, 1), members)).astype(BF16)
    overlap = sum(dot32(piece, gather, NT) for piece in pieces) * (1.0 / cells)
    flipped = sum(dot32(gather, piece, NT) for piece in pieces) * (1.0 / cells)
    overlap_ref[...] = overlap
    rows = CAP * span
    square = (members, members)
    group = lax.axis_index("grid") * lax.axis_size("ham") + lax.axis_index("ham")
    mine = (owners_ref[...] == group).astype(F32)
    eye = (ids(square, 0) == ids(square, 1)).astype(F32)
    mine_row = jnp.sum(mine * eye, axis=0, keepdims=True)
    before = (ids(square, 0) < ids(square, 1)).astype(F32)
    ranking = jnp.sum(mine * before, axis=0, keepdims=True)
    slot = (ids((rows, members), 0) // span).astype(F32)
    placed = (jnp.where(slot == ranking, 1.0, 0.0) * mine_row).astype(BF16)
    wide = (members, LANES)
    row = ids(wide, 0)
    upper = 0.5 * (overlap + flipped)
    columns = [jnp.broadcast_to(upper[:, j : j + 1], wide) for j in range(members)]
    lower = (row == lane_member(ids(wide, 1), members)).astype(F32)
    diagonal = ratio = jnp.zeros(wide, F32)
    for k in range(0, members, 2):
        first, second = columns[k], columns[k + 1]
        a, b, c = first[k : k + 1], first[k + 1 : k + 2], second[k + 1 : k + 2]
        share = b / a
        rest = c - share * b
        diagonal = jnp.where(row == k, a, jnp.where(row == k + 1, rest, diagonal))
        ratio = jnp.where(row == k + 1, share, ratio)
        scale = 1.0 / (a * c - b * b)
        below = row > k + 1
        one = jnp.where(below, (first * c - second * b) * scale, 0.0)
        two = jnp.where(below, (second * a - first * b) * scale, 0.0)
        lower = lower - (one * lower[k : k + 1] + two * lower[k + 1 : k + 2])
        for j in range(k + 2, members):
            column = columns[j]
            columns[j] = column - (one * column[k : k + 1] + two * column[k + 1 : k + 2])
    above = jnp.concatenate([lower[:1], lower[:-1]], axis=0)
    inverse = (lower - ratio * above) / jnp.sqrt(diagonal)
    high, low = halves(inverse)
    same_line = ids((rows, LANES), 0) % span == lane_line(ids((rows, LANES), 1), turn, members)
    blank = jnp.zeros((rows, LANES), BF16)
    chosen = [jnp.where(same_line, dot32(placed, half), 0.0).astype(BF16) for half in (high, low)]
    for i, half in enumerate(chosen + chosen):
        pair = [half, blank] if i < 2 else [blank, half]
        weights_ref[i * rows : (i + 1) * rows, :] = jnp.concatenate(pair, axis=1)


def route_kernel(overlap_ref, weights_ref, *refs):
    parts, (out_hbm, overlap_hbm, staged, semaphores) = refs[:-4], refs[-4:]
    groups = len(parts)
    copies = [pltpu.make_async_copy(overlap_ref, overlap_hbm, semaphores.at[groups])]
    copies[0].start()
    points = staged.shape[3]
    weights = weights_ref[...]
    rows = weights.shape[0] // 4
    span = rows // CAP
    lines = staged.shape[2]
    packs = lines // span
    highs = jnp.concatenate([weights[:rows], weights[2 * rows : 3 * rows]], axis=0)
    group = lax.axis_index("grid") * lax.axis_size("ham") + lax.axis_index("ham")
    for flip, part in enumerate(parts):
        sums = []
        for pack in range(0, packs, 2):
            field = jnp.concatenate([part[pack], part[pack + 1]], axis=1)
            both = dot32(weights, field, NT)
            results = [both[:rows] + both[rows : 2 * rows], both[2 * rows : 3 * rows] + both[3 * rows :]]
            if part.shape[0] > packs:
                place = packs + pack
                rest = dot32(highs, jnp.concatenate([part[place], part[place + 1]], axis=1), NT)
                results = [results[0] + rest[:rows], results[1] + rest[rows:]]
            sums += [result.reshape(CAP, span, points) for result in results]
        staged[flip] = jnp.concatenate(sums, axis=1).astype(BF16)
        start = pl.multiple_of((group ^ flip) * lines, lines)
        target = out_hbm.at[:, pl.ds(start, lines), :]
        copies.append(pltpu.make_async_copy(staged.at[flip], target, semaphores.at[flip]))
        copies[-1].start()
    for copy in copies:
        copy.wait()


def call(kernel, name, shapes, flops, moved, scratch=(), scalars=0, operands=0, remote=False):
    vmem = pl.BlockSpec(memory_space=pltpu.VMEM)
    smem = pl.BlockSpec(memory_space=pltpu.SMEM)
    return pl.pallas_call(
        kernel,
        name=name,
        out_shape=shapes,
        in_specs=[smem] * scalars + [vmem] * operands,
        out_specs=[pl.BlockSpec(memory_space=pl.ANY) if remote else vmem] * len(shapes),
        scratch_shapes=list(scratch),
        compiler_params=pltpu.CompilerParams(vmem_limit_bytes=VMEM_LIMIT),
        cost_estimate=pl.CostEstimate(flops=flops, bytes_accessed=moved, transcendentals=0),
    )


def local(orbitals, coulomb, occupied, owners):
    members, lines, points = orbitals.shape
    grids, near = lax.axis_size("grid"), lax.axis_size("ham")
    groups = grids * near
    padded = -(-points // LANES) * LANES
    span = LANES // members
    packs = lines // span
    assert packs % 2 == 0
    shape = jax.ShapeDtypeStruct
    (packed,) = call(
        pack_kernel,
        "pack",
        [shape((packs, points, LANES), BF16)],
        orbitals.size,
        4 * orbitals.size,
        operands=1,
    )(orbitals)
    guests = exchanged(packed)
    tables = spectral_tables(points)
    (response,) = call(
        response_kernel,
        "response",
        [shape((lines, points, padded), F32)],
        4 * lines * points**3,
        4 * lines * points**2,
        operands=2,
    )(coulomb, tables)
    blocks = len(guests) + 1
    high, parts = call(
        functools.partial(image_kernel, members),
        "image",
        [
            shape((packs, points, LANES), BF16),
            shape((2 * packs, points, LANES), BF16),
        ],
        2 * lines * points * padded * (4 * LANES),
        4 * lines * points**2,
        scalars=1,
        operands=blocks + 1,
    )(occupied, packed, *guests, response)
    (overlap,) = call(
        overlap_kernel,
        "overlap",
        [shape((members, LANES), F32)],
        4 * packs * points * LANES**2,
        8 * orbitals.size,
        operands=2,
    )(orbitals, parts)
    overlaps = [overlap] + [swapped(overlap, flip) for flip in range(1, groups)]
    images = [parts] + [swapped(parts, flip) for flip in range(1, near)]
    for grid in range(1, grids):
        across = swapped(high, grid * near)
        images += [across] + [swapped(across, flip) for flip in range(1, near)]
    cells = lines * groups * points

    intersection, weights = call(
        functools.partial(factor_kernel, cells),
        "factor",
        [shape((members, members), F32), shape((4 * CAP * span, 2 * LANES), BF16)],
        FACTOR_COST,
        members**2 * 4,
        operands=1 + groups,
    )(owners, *overlaps)
    routed, intersection = call(
        route_kernel,
        "route",
        [shape((CAP, groups * lines, points), BF16), shape((members, members), F32)],
        2 * CAP * members * groups * lines * points,
        6 * members * groups * lines * points,
        scratch=[
            pltpu.VMEM((groups, CAP, lines, points), BF16),
            pltpu.SemaphoreType.DMA((groups + 1,)),
        ],
        operands=2 + groups,
        remote=True,
    )(intersection, weights, *images)
    return routed[None, None], intersection[None]


def solution(mesh):
    in_specs = (P("band", ("grid", "ham"), None), P(("grid", "ham"), None), P(), P("band", None))
    out_specs = (P("band", ("grid", "ham"), None, None, None), P("band", None, None))
    return jax.shard_map(local, mesh=mesh, in_specs=in_specs, out_specs=out_specs, check_vma=False)
```

```python
import functools
import math

import jax
import jax.numpy as jnp
import numpy as np
from jax import lax
from jax.experimental import pallas as pl
from jax.experimental.pallas import tpu as pltpu
from jax.sharding import PartitionSpec as P

CAP = 8
LANES = 128
HIGHEST = lax.Precision.HIGHEST
VMEM_LIMIT = 48 * 1024 * 1024
FACTOR_COST = 3_000_000_000
NT = ((1,), (1,))
F32, BF16 = jnp.float32, jnp.bfloat16


STEPS = (-1, -2, 2, 1)


def sources(block, count):
    return [(block + step + count) % count for step in STEPS]


def exchanged(value):
    count = lax.axis_size("band")
    assert count % 4 == 0
    tables = [sources(block, count) for block in range(count)]
    return [
        lax.ppermute(value, "band", [(row[turn], block) for block, row in enumerate(tables)])
        for turn in range(4)
    ]


def swapped(value, flip):
    count = lax.axis_size("grid") * lax.axis_size("ham")
    return lax.ppermute(value, ("grid", "ham"), [(group, group ^ flip) for group in range(count)])


def spectral_tables(points):
    midpoint = points // 2
    ids = np.arange(points)
    frequency = np.where(ids <= midpoint, ids, ids - midpoint)
    angles = (ids[:, None] * frequency[None, :] % points) * (2.0 * math.pi / points)
    forward = np.where((ids <= midpoint)[None, :], np.cos(angles), np.sin(angles))
    single = (frequency == 0) | (ids == midpoint)
    inverse = forward.T * (np.where(single, 1.0, 2.0) / points)[:, None]
    mirror = np.zeros((points, points))
    mirror[frequency, ids] += 0.5
    mirror[(points - frequency) % points, ids] += 0.5
    return jnp.asarray(np.stack([forward.T, inverse.T, mirror]).astype(np.float32)).astype(BF16)


def split(value):
    high = value.astype(BF16)
    return high, value - high.astype(F32)


def halves(value):
    high, rest = split(value)
    return high, rest.astype(BF16)


def dot32(a, b, contract=((1,), (0,))):
    return lax.dot_general(a, b, (contract, ((), ())), preferred_element_type=F32)


def dot_exact(a, b, contract=((1,), (0,))):
    return lax.dot_general(
        a, b, (contract, ((), ())), precision=HIGHEST, preferred_element_type=F32
    )


def ids(shape, axis):
    return lax.broadcasted_iota(jnp.int32, shape, axis)


def lane_member(lane, members):
    return lane % members


def lane_quarter(lane, turn):
    return (lane // (LANES // 4)) ^ turn


def lane_line(lane, turn, members):
    per = LANES // 4 // members
    return lane_quarter(lane, turn) * per + lane % (LANES // 4) // members


def own_turn():
    return lax.axis_index("band") % 4


def rows_of(block, pack, span):
    members, _, points = block.shape
    part = block[:, pack * span : (pack + 1) * span, :]
    return part.reshape(members * span, points)


def pack_kernel(orbitals_ref, out_ref):
    members = orbitals_ref.shape[0]
    span = LANES // members
    block = orbitals_ref[...].astype(F32)
    row, lane = ids((LANES, LANES), 0), ids((LANES, LANES), 1)
    source = lane_member(lane, members) * span + lane_line(lane, own_turn(), members)
    order = (row == source).astype(BF16)
    for pack in range(out_ref.shape[0]):
        rows = rows_of(block, pack, span).T.astype(BF16)
        out_ref[pack] = dot32(rows, order).astype(BF16)


def response_kernel(coulomb_ref, tables_ref, out_ref):
    points = coulomb_ref.shape[1]
    multiplier = dot_exact(coulomb_ref[...], tables_ref[2].astype(F32))
    forward = tables_ref[0]
    inverse = tables_ref[1].astype(F32)
    pad = jnp.zeros((points, out_ref.shape[2] - points), F32)
    for line in range(coulomb_ref.shape[0]):
        high, low = halves(inverse * multiplier[line : line + 1, :])
        out_ref[line, :, :points] = dot32(high, forward) + dot32(low, forward)
        out_ref[line, :, points:] = pad


def image_kernel(members, occupied_ref, *refs):
    blocks, (response_ref, high_ref, halves_ref) = refs[:-3], refs[-3:]
    packs, points, _ = blocks[0].shape
    padded = response_ref.shape[2]
    span = LANES // members
    per = span // 4
    total = lax.axis_size("band")
    position = lax.axis_index("band")
    places = [position] + sources(position, total)
    turns = [place % 4 for place in places]
    lane = ids((1, LANES), 1)
    own_line = lane_line(lane, turns[0], members)
    filled = [lane_member(lane, members) < occupied_ref[place] for place in places]
    quarters = [lane_quarter(lane, turn) for turn in turns]
    step = lane % (LANES // 4) // members
    apart, merged = 2, (0, 1, 3, 4)
    spare = padded - points
    cuts = points // spare
    assert cuts * spare == points and LANES % spare == 0
    blank = jnp.zeros((spare, 2 * LANES), BF16)
    kernels = [[[] for _ in range(cuts)] for _ in range(packs)]
    for pack in range(packs):
        tiles = [block[pack] for block in blocks]
        for quarter in range(4):
            here = [(q == quarter) for q in quarters]
            together = tiles[merged[0]]
            for m in merged[1:]:
                together = jnp.where(here[m], tiles[m], together)
            window = jnp.concatenate([together, tiles[apart]], axis=1)
            occupied = sum((here[m] & filled[m]).astype(F32) for m in merged)
            beside = (here[apart] & filled[apart]).astype(F32)
            both = jnp.concatenate([occupied, beside], axis=1)
            steps = jnp.concatenate([step, step], axis=1)
            masked = jnp.concatenate(
                [window * jnp.where(steps == k, both, 0.0).astype(BF16) for k in range(per)], axis=0
            )
            gram = dot32(masked, jnp.concatenate([window, blank], axis=0), NT)
            first = pack * span + quarter * per
            response = response_ref[first : first + per].reshape(per * points, padded)
            weighted = gram * response
            for place in range(0, per * points, spare):
                cut = place // spare % cuts
                part = weighted[place : place + spare]
                tile = cut * spare // LANES * LANES
                _, low = split(part[:, tile : tile + LANES])
                shift = LANES - spare - cut * spare % LANES
                low = pltpu.roll(low, shift, axis=1) if shift else low
                last = jnp.where(lane < LANES - spare, part[:, -LANES:], low)
                part = jnp.concatenate([part[:, :-LANES], last], axis=1)
                kernels[pack][cut].append(part.astype(BF16))
    for pack in range(packs):
        tile = blocks[0][pack]
        image = []
        for cut in range(cuts):
            native = jnp.concatenate([tile, tile[cut * spare : (cut + 1) * spare]], axis=0)
            fields = dot32(jnp.concatenate(kernels[pack][cut], axis=0), native)
            rows = jnp.zeros((spare, LANES), F32)
            for line in range(span):
                rows = jnp.where(own_line == line, fields[line * spare : (line + 1) * spare], rows)
            image.append(rows)
        image = jnp.concatenate(image, axis=0)
        high, low = halves(image)
        high_ref[pack] = high
        halves_ref[pack] = high
        halves_ref[packs + pack] = low


def overlap_kernel(orbitals_ref, halves_ref, out_ref):
    members, _, _ = orbitals_ref.shape
    span = LANES // members
    natives = orbitals_ref[...].astype(F32)
    square = (LANES, LANES)
    same_line = ids(square, 0) % span == lane_line(ids(square, 1), own_turn(), members)
    cross = jnp.zeros(square, F32)
    packs = halves_ref.shape[0] // 2
    for pack in range(packs):
        rows = rows_of(natives, pack, span).astype(BF16)
        both = jnp.concatenate([halves_ref[pack], halves_ref[packs + pack]], axis=1)
        product = dot32(rows, both)
        cross = cross + (product[:, :LANES] + product[:, LANES:])
    out_ref[...] = jnp.where(same_line, cross, 0.0).reshape(members, span, LANES).sum(axis=1)


def factor_kernel(cells, owners_ref, *refs):
    parts, (overlap_ref, weights_ref) = refs[:-2], refs[-2:]
    members = owners_ref.shape[0]
    span = LANES // members
    turn = own_turn()
    sums = [part[...] for part in parts]
    while len(sums) > 1:
        sums = [a + b for a, b in zip(sums[::2], sums[1::2])]
    high, rest = split(sums[0])
    pieces = [high, *halves(rest)]
    across = (members, LANES)
    gather = (ids(across, 0) == lane_member(ids(across, 1), members)).astype(BF16)
    overlap = sum(dot32(piece, gather, NT) for piece in pieces) * (1.0 / cells)
    flipped = sum(dot32(gather, piece, NT) for piece in pieces) * (1.0 / cells)
    overlap_ref[...] = overlap
    rows = CAP * span
    square = (members, members)
    group = lax.axis_index("grid") * lax.axis_size("ham") + lax.axis_index("ham")
    mine = (owners_ref[...] == group).astype(F32)
    eye = (ids(square, 0) == ids(square, 1)).astype(F32)
    mine_row = jnp.sum(mine * eye, axis=0, keepdims=True)
    before = (ids(square, 0) < ids(square, 1)).astype(F32)
    ranking = jnp.sum(mine * before, axis=0, keepdims=True)
    slot = (ids((rows, members), 0) // span).astype(F32)
    placed = (jnp.where(slot == ranking, 1.0, 0.0) * mine_row).astype(BF16)
    wide = (members, LANES)
    row = ids(wide, 0)
    upper = 0.5 * (overlap + flipped)
    columns = [jnp.broadcast_to(upper[:, j : j + 1], wide) for j in range(members)]
    lower = (row == lane_member(ids(wide, 1), members)).astype(F32)
    diagonal = ratio = jnp.zeros(wide, F32)
    for k in range(0, members, 2):
        first, second = columns[k], columns[k + 1]
        a, b, c = first[k : k + 1], first[k + 1 : k + 2], second[k + 1 : k + 2]
        share = b / a
        rest = c - share * b
        diagonal = jnp.where(row == k, a, jnp.where(row == k + 1, rest, diagonal))
        ratio = jnp.where(row == k + 1, share, ratio)
        scale = 1.0 / (a * c - b * b)
        below = row > k + 1
        one = jnp.where(below, (first * c - second * b) * scale, 0.0)
        two = jnp.where(below, (second * a - first * b) * scale, 0.0)
        lower = lower - (one * lower[k : k + 1] + two * lower[k + 1 : k + 2])
        for j in range(k + 2, members):
            column = columns[j]
            columns[j] = column - (one * column[k : k + 1] + two * column[k + 1 : k + 2])
    above = jnp.concatenate([lower[:1], lower[:-1]], axis=0)
    inverse = (lower - ratio * above) / jnp.sqrt(diagonal)
    high, low = halves(inverse)
    same_line = ids((rows, LANES), 0) % span == lane_line(ids((rows, LANES), 1), turn, members)
    blank = jnp.zeros((rows, LANES), BF16)
    chosen = [jnp.where(same_line, dot32(placed, half), 0.0).astype(BF16) for half in (high, low)]
    for i, half in enumerate(chosen + chosen):
        pair = [half, blank] if i < 2 else [blank, half]
        weights_ref[i * rows : (i + 1) * rows, :] = jnp.concatenate(pair, axis=1)


def send_rows(flips, weights_ref, parts, out_hbm, staged, semaphores):
    points = staged.shape[3]
    weights = weights_ref[...]
    rows = weights.shape[0] // 4
    span = rows // CAP
    lines = staged.shape[2]
    packs = lines // span
    highs = jnp.concatenate([weights[:rows], weights[2 * rows : 3 * rows]], axis=0)
    group = lax.axis_index("grid") * lax.axis_size("ham") + lax.axis_index("ham")
    copies = []
    for place, (flip, part) in enumerate(zip(flips, parts)):
        sums = []
        for pack in range(0, packs, 2):
            field = jnp.concatenate([part[pack], part[pack + 1]], axis=1)
            both = dot32(weights, field, NT)
            results = [both[:rows] + both[rows : 2 * rows], both[2 * rows : 3 * rows] + both[3 * rows :]]
            if part.shape[0] > packs:
                low = packs + pack
                rest = dot32(highs, jnp.concatenate([part[low], part[low + 1]], axis=1), NT)
                results = [results[0] + rest[:rows], results[1] + rest[rows:]]
            sums += [result.reshape(CAP, span, points) for result in results]
        staged[place] = jnp.concatenate(sums, axis=1).astype(BF16)
        start = pl.multiple_of((group ^ flip) * lines, lines)
        target = out_hbm.at[:, pl.ds(start, lines), :]
        copies.append(pltpu.make_async_copy(staged.at[place], target, semaphores.at[place]))
        copies[-1].start()
    return copies


def early_kernel(flips, overlap_ref, weights_ref, *refs):
    parts, (out_hbm, overlap_hbm, staged, semaphores) = refs[:-4], refs[-4:]
    copies = [pltpu.make_async_copy(overlap_ref, overlap_hbm, semaphores.at[len(flips)])]
    copies[0].start()
    copies += send_rows(flips, weights_ref, parts, out_hbm, staged, semaphores)
    for copy in copies:
        copy.wait()


def late_kernel(flips, begun_hbm, weights_ref, *refs):
    parts, (out_hbm, staged, semaphores) = refs[:-3], refs[-3:]
    del begun_hbm
    for copy in send_rows(flips, weights_ref, parts, out_hbm, staged, semaphores):
        copy.wait()


def call(kernel, name, shapes, flops, moved, scratch=(), scalars=0, operands=0, remote=False, begun=False):
    vmem = pl.BlockSpec(memory_space=pltpu.VMEM)
    smem = pl.BlockSpec(memory_space=pltpu.SMEM)
    far = pl.BlockSpec(memory_space=pl.ANY)
    return pl.pallas_call(
        kernel,
        name=name,
        out_shape=shapes,
        in_specs=[smem] * scalars + [far] * begun + [vmem] * operands,
        out_specs=[far if remote else vmem] * len(shapes),
        input_output_aliases={0: 0} if begun else {},
        scratch_shapes=list(scratch),
        compiler_params=pltpu.CompilerParams(vmem_limit_bytes=VMEM_LIMIT),
        cost_estimate=pl.CostEstimate(flops=flops, bytes_accessed=moved, transcendentals=0),
    )


def local(orbitals, coulomb, occupied, owners):
    members, lines, points = orbitals.shape
    grids, near = lax.axis_size("grid"), lax.axis_size("ham")
    groups = grids * near
    padded = -(-points // LANES) * LANES
    span = LANES // members
    packs = lines // span
    assert packs % 2 == 0
    shape = jax.ShapeDtypeStruct
    (packed,) = call(
        pack_kernel,
        "pack",
        [shape((packs, points, LANES), BF16)],
        orbitals.size,
        4 * orbitals.size,
        operands=1,
    )(orbitals)
    guests = exchanged(packed)
    tables = spectral_tables(points)
    (response,) = call(
        response_kernel,
        "response",
        [shape((lines, points, padded), F32)],
        4 * lines * points**3,
        4 * lines * points**2,
        operands=2,
    )(coulomb, tables)
    blocks = len(guests) + 1
    high, parts = call(
        functools.partial(image_kernel, members),
        "image",
        [
            shape((packs, points, LANES), BF16),
            shape((2 * packs, points, LANES), BF16),
        ],
        2 * lines * points * padded * (4 * LANES),
        4 * lines * points**2,
        scalars=1,
        operands=blocks + 1,
    )(occupied, packed, *guests, response)
    (overlap,) = call(
        overlap_kernel,
        "overlap",
        [shape((members, LANES), F32)],
        4 * packs * points * LANES**2,
        8 * orbitals.size,
        operands=2,
    )(orbitals, parts)
    others = [swapped(overlap, flip) for flip in reversed(range(1, groups))]
    overlaps = [overlap] + others[::-1]
    images = [parts] + [swapped(parts, flip) for flip in range(1, near)]
    for grid in range(1, grids):
        across = swapped(high, grid * near)
        images += [across] + [swapped(across, flip) for flip in range(1, near)]
    cells = lines * groups * points

    intersection, weights = call(
        functools.partial(factor_kernel, cells),
        "factor",
        [shape((members, members), F32), shape((4 * CAP * span, 2 * LANES), BF16)],
        FACTOR_COST,
        members**2 * 4,
        operands=1 + groups,
    )(owners, *overlaps)
    direct = [flip for flip in range(groups) if flip < near or flip % near == 0]
    passed = [flip for flip in range(groups) if flip not in direct]

    def route(kernel, name, flips, shapes, **more):
        return call(
            functools.partial(kernel, flips),
            name,
            [shape((CAP, groups * lines, points), BF16)] + shapes,
            2 * CAP * members * len(flips) * lines * points,
            6 * members * len(flips) * lines * points,
            scratch=[
                pltpu.VMEM((len(flips), CAP, lines, points), BF16),
                pltpu.SemaphoreType.DMA((len(flips) + 1,)),
            ],
            remote=True,
            **more,
        )

    routed, intersection = route(
        early_kernel, "early", direct, [shape((members, members), F32)], operands=2 + len(direct)
    )(intersection, weights, *[images[flip] for flip in direct])
    if passed:
        (routed,) = route(
            late_kernel, "late", passed, [], operands=1 + len(passed), begun=True
        )(routed, weights, *[images[flip] for flip in passed])
    return routed[None, None], intersection[None]


def solution(mesh):
    in_specs = (P("band", ("grid", "ham"), None), P(("grid", "ham"), None), P(), P("band", None))
    out_specs = (P("band", ("grid", "ham"), None, None, None), P("band", None, None))
    return jax.shard_map(local, mesh=mesh, in_specs=in_specs, out_specs=out_specs, check_vma=False)
```

```python
import functools
import math

import jax
import jax.numpy as jnp
import numpy as np
from jax import lax
from jax.experimental import pallas as pl
from jax.experimental.pallas import tpu as pltpu
from jax.sharding import PartitionSpec as P

CAP = 8
LANES = 128
HIGHEST = lax.Precision.HIGHEST
VMEM_LIMIT = 48 * 1024 * 1024
FACTOR_COST = 3_000_000_000
NT = ((1,), (1,))
F32, BF16 = jnp.float32, jnp.bfloat16


STEPS = (-2, -1, 2, 1)


def sources(block, count):
    return [(block + step + count) % count for step in STEPS]


def exchanged(value):
    count = lax.axis_size("band")
    assert count % 4 == 0
    tables = [sources(block, count) for block in range(count)]
    return [
        lax.ppermute(value, "band", [(row[turn], block) for block, row in enumerate(tables)])
        for turn in range(4)
    ]


def swapped(value, flip):
    count = lax.axis_size("grid") * lax.axis_size("ham")
    return lax.ppermute(value, ("grid", "ham"), [(group, group ^ flip) for group in range(count)])


def spectral_tables(points):
    midpoint = points // 2
    ids = np.arange(points)
    frequency = np.where(ids <= midpoint, ids, ids - midpoint)
    angles = (ids[:, None] * frequency[None, :] % points) * (2.0 * math.pi / points)
    forward = np.where((ids <= midpoint)[None, :], np.cos(angles), np.sin(angles))
    single = (frequency == 0) | (ids == midpoint)
    inverse = forward.T * (np.where(single, 1.0, 2.0) / points)[:, None]
    mirror = np.zeros((points, points))
    mirror[frequency, ids] += 0.5
    mirror[(points - frequency) % points, ids] += 0.5
    return jnp.asarray(np.stack([forward.T, inverse.T, mirror]).astype(np.float32)).astype(BF16)


def split(value):
    high = value.astype(BF16)
    return high, value - high.astype(F32)


def halves(value):
    high, rest = split(value)
    return high, rest.astype(BF16)


def dot32(a, b, contract=((1,), (0,))):
    return lax.dot_general(a, b, (contract, ((), ())), preferred_element_type=F32)


def dot_exact(a, b, contract=((1,), (0,))):
    return lax.dot_general(
        a, b, (contract, ((), ())), precision=HIGHEST, preferred_element_type=F32
    )


def ids(shape, axis):
    return lax.broadcasted_iota(jnp.int32, shape, axis)


def lane_member(lane, members):
    return lane % members


def lane_quarter(lane, turn):
    return (lane // (LANES // 4)) ^ turn


def lane_line(lane, turn, members):
    per = LANES // 4 // members
    return lane_quarter(lane, turn) * per + lane % (LANES // 4) // members


def own_turn():
    return lax.axis_index("band") % 4


def rows_of(block, pack, span):
    members, _, points = block.shape
    part = block[:, pack * span : (pack + 1) * span, :]
    return part.reshape(members * span, points)


def pack_kernel(orbitals_ref, out_ref):
    members = orbitals_ref.shape[0]
    span = LANES // members
    block = orbitals_ref[...].astype(F32)
    row, lane = ids((LANES, LANES), 0), ids((LANES, LANES), 1)
    source = lane_member(lane, members) * span + lane_line(lane, own_turn(), members)
    order = (row == source).astype(BF16)
    for pack in range(out_ref.shape[0]):
        rows = rows_of(block, pack, span).T.astype(BF16)
        out_ref[pack] = dot32(rows, order).astype(BF16)


def response_kernel(coulomb_ref, tables_ref, out_ref):
    points = coulomb_ref.shape[1]
    multiplier = dot_exact(coulomb_ref[...], tables_ref[2].astype(F32))
    forward = tables_ref[0]
    inverse = tables_ref[1].astype(F32)
    pad = jnp.zeros((points, out_ref.shape[2] - points), F32)
    for line in range(coulomb_ref.shape[0]):
        high, low = halves(inverse * multiplier[line : line + 1, :])
        out_ref[line, :, :points] = dot32(high, forward) + dot32(low, forward)
        out_ref[line, :, points:] = pad


def image_kernel(members, occupied_ref, *refs):
    blocks, (response_ref, high_ref, halves_ref) = refs[:-3], refs[-3:]
    packs, points, _ = blocks[0].shape
    padded = response_ref.shape[2]
    span = LANES // members
    per = span // 4
    total = lax.axis_size("band")
    position = lax.axis_index("band")
    places = [position] + sources(position, total)
    turns = [place % 4 for place in places]
    lane = ids((1, LANES), 1)
    own_line = lane_line(lane, turns[0], members)
    filled = [lane_member(lane, members) < occupied_ref[place] for place in places]
    quarters = [lane_quarter(lane, turn) for turn in turns]
    step = lane % (LANES // 4) // members
    apart, merged = 1, (0, 2, 3, 4)
    spare = padded - points
    cuts = points // spare
    assert cuts * spare == points and LANES % spare == 0
    blank = jnp.zeros((spare, 2 * LANES), BF16)
    kernels = [[[] for _ in range(cuts)] for _ in range(packs)]
    for pack in range(packs):
        tiles = [block[pack] for block in blocks]
        for quarter in range(4):
            here = [(q == quarter) for q in quarters]
            together = tiles[merged[0]]
            for m in merged[1:]:
                together = jnp.where(here[m], tiles[m], together)
            window = jnp.concatenate([together, tiles[apart]], axis=1)
            occupied = sum((here[m] & filled[m]).astype(F32) for m in merged)
            beside = (here[apart] & filled[apart]).astype(F32)
            both = jnp.concatenate([occupied, beside], axis=1)
            steps = jnp.concatenate([step, step], axis=1)
            masked = jnp.concatenate(
                [window * jnp.where(steps == k, both, 0.0).astype(BF16) for k in range(per)], axis=0
            )
            gram = dot32(masked, jnp.concatenate([window, blank], axis=0), NT)
            first = pack * span + quarter * per
            response = response_ref[first : first + per].reshape(per * points, padded)
            weighted = gram * response
            for place in range(0, per * points, spare):
                cut = place // spare % cuts
                part = weighted[place : place + spare]
                tile = cut * spare // LANES * LANES
                _, low = split(part[:, tile : tile + LANES])
                shift = LANES - spare - cut * spare % LANES
                low = pltpu.roll(low, shift, axis=1) if shift else low
                last = jnp.where(lane < LANES - spare, part[:, -LANES:], low)
                part = jnp.concatenate([part[:, :-LANES], last], axis=1)
                kernels[pack][cut].append(part.astype(BF16))
    for pack in range(packs):
        tile = blocks[0][pack]
        image = []
        for cut in range(cuts):
            native = jnp.concatenate([tile, tile[cut * spare : (cut + 1) * spare]], axis=0)
            fields = dot32(jnp.concatenate(kernels[pack][cut], axis=0), native)
            rows = jnp.zeros((spare, LANES), F32)
            for line in range(span):
                rows = jnp.where(own_line == line, fields[line * spare : (line + 1) * spare], rows)
            image.append(rows)
        image = jnp.concatenate(image, axis=0)
        high, low = halves(image)
        high_ref[pack] = high
        halves_ref[pack] = high
        halves_ref[packs + pack] = low


def overlap_kernel(orbitals_ref, halves_ref, out_ref):
    members, _, _ = orbitals_ref.shape
    span = LANES // members
    natives = orbitals_ref[...].astype(F32)
    square = (LANES, LANES)
    same_line = ids(square, 0) % span == lane_line(ids(square, 1), own_turn(), members)
    cross = jnp.zeros(square, F32)
    packs = halves_ref.shape[0] // 2
    for pack in range(packs):
        rows = rows_of(natives, pack, span).astype(BF16)
        both = jnp.concatenate([halves_ref[pack], halves_ref[packs + pack]], axis=1)
        product = dot32(rows, both)
        cross = cross + (product[:, :LANES] + product[:, LANES:])
    out_ref[...] = jnp.where(same_line, cross, 0.0).reshape(members, span, LANES).sum(axis=1)


def factor_kernel(cells, owners_ref, *refs):
    parts, (overlap_ref, weights_ref) = refs[:-2], refs[-2:]
    members = owners_ref.shape[0]
    span = LANES // members
    turn = own_turn()
    sums = [part[...] for part in parts]
    while len(sums) > 1:
        sums = [a + b for a, b in zip(sums[::2], sums[1::2])]
    high, rest = split(sums[0])
    pieces = [high, *halves(rest)]
    across = (members, LANES)
    gather = (ids(across, 0) == lane_member(ids(across, 1), members)).astype(BF16)
    overlap = sum(dot32(piece, gather, NT) for piece in pieces) * (1.0 / cells)
    flipped = sum(dot32(gather, piece, NT) for piece in pieces) * (1.0 / cells)
    overlap_ref[...] = overlap
    rows = CAP * span
    square = (members, members)
    group = lax.axis_index("grid") * lax.axis_size("ham") + lax.axis_index("ham")
    mine = (owners_ref[...] == group).astype(F32)
    eye = (ids(square, 0) == ids(square, 1)).astype(F32)
    mine_row = jnp.sum(mine * eye, axis=0, keepdims=True)
    before = (ids(square, 0) < ids(square, 1)).astype(F32)
    ranking = jnp.sum(mine * before, axis=0, keepdims=True)
    slot = (ids((rows, members), 0) // span).astype(F32)
    placed = (jnp.where(slot == ranking, 1.0, 0.0) * mine_row).astype(BF16)
    wide = (members, LANES)
    row = ids(wide, 0)
    upper = 0.5 * (overlap + flipped)
    columns = [jnp.broadcast_to(upper[:, j : j + 1], wide) for j in range(members)]
    lower = (row == lane_member(ids(wide, 1), members)).astype(F32)
    diagonal = ratio = jnp.zeros(wide, F32)
    for k in range(0, members, 2):
        first, second = columns[k], columns[k + 1]
        a, b, c = first[k : k + 1], first[k + 1 : k + 2], second[k + 1 : k + 2]
        share = b / a
        rest = c - share * b
        diagonal = jnp.where(row == k, a, jnp.where(row == k + 1, rest, diagonal))
        ratio = jnp.where(row == k + 1, share, ratio)
        scale = 1.0 / (a * c - b * b)
        below = row > k + 1
        one = jnp.where(below, (first * c - second * b) * scale, 0.0)
        two = jnp.where(below, (second * a - first * b) * scale, 0.0)
        lower = lower - (one * lower[k : k + 1] + two * lower[k + 1 : k + 2])
        for j in range(k + 2, members):
            column = columns[j]
            columns[j] = column - (one * column[k : k + 1] + two * column[k + 1 : k + 2])
    above = jnp.concatenate([lower[:1], lower[:-1]], axis=0)
    inverse = (lower - ratio * above) / jnp.sqrt(diagonal)
    high, low = halves(inverse)
    same_line = ids((rows, LANES), 0) % span == lane_line(ids((rows, LANES), 1), turn, members)
    blank = jnp.zeros((rows, LANES), BF16)
    chosen = [jnp.where(same_line, dot32(placed, half), 0.0).astype(BF16) for half in (high, low)]
    for i, half in enumerate(chosen + chosen):
        pair = [half, blank] if i < 2 else [blank, half]
        weights_ref[i * rows : (i + 1) * rows, :] = jnp.concatenate(pair, axis=1)


def route_kernel(overlap_ref, weights_ref, *refs):
    parts, (out_hbm, overlap_hbm, staged, semaphores) = refs[:-4], refs[-4:]
    groups = len(parts)
    copies = [pltpu.make_async_copy(overlap_ref, overlap_hbm, semaphores.at[groups])]
    copies[0].start()
    points = staged.shape[3]
    weights = weights_ref[...]
    rows = weights.shape[0] // 4
    span = rows // CAP
    lines = staged.shape[2]
    packs = lines // span
    highs = jnp.concatenate([weights[:rows], weights[2 * rows : 3 * rows]], axis=0)
    group = lax.axis_index("grid") * lax.axis_size("ham") + lax.axis_index("ham")
    for flip, part in enumerate(parts):
        sums = []
        for pack in range(0, packs, 2):
            field = jnp.concatenate([part[pack], part[pack + 1]], axis=1)
            both = dot32(weights, field, NT)
            results = [both[:rows] + both[rows : 2 * rows], both[2 * rows : 3 * rows] + both[3 * rows :]]
            if part.shape[0] > packs:
                place = packs + pack
                rest = dot32(highs, jnp.concatenate([part[place], part[place + 1]], axis=1), NT)
                results = [results[0] + rest[:rows], results[1] + rest[rows:]]
            sums += [result.reshape(CAP, span, points) for result in results]
        staged[flip] = jnp.concatenate(sums, axis=1).astype(BF16)
        start = pl.multiple_of((group ^ flip) * lines, lines)
        target = out_hbm.at[:, pl.ds(start, lines), :]
        copies.append(pltpu.make_async_copy(staged.at[flip], target, semaphores.at[flip]))
        copies[-1].start()
    for copy in copies:
        copy.wait()


def call(kernel, name, shapes, flops, moved, scratch=(), scalars=0, operands=0, remote=False):
    vmem = pl.BlockSpec(memory_space=pltpu.VMEM)
    smem = pl.BlockSpec(memory_space=pltpu.SMEM)
    return pl.pallas_call(
        kernel,
        name=name,
        out_shape=shapes,
        in_specs=[smem] * scalars + [vmem] * operands,
        out_specs=[pl.BlockSpec(memory_space=pl.ANY) if remote else vmem] * len(shapes),
        scratch_shapes=list(scratch),
        compiler_params=pltpu.CompilerParams(vmem_limit_bytes=VMEM_LIMIT),
        cost_estimate=pl.CostEstimate(flops=flops, bytes_accessed=moved, transcendentals=0),
    )


def local(orbitals, coulomb, occupied, owners):
    members, lines, points = orbitals.shape
    grids, near = lax.axis_size("grid"), lax.axis_size("ham")
    groups = grids * near
    padded = -(-points // LANES) * LANES
    span = LANES // members
    packs = lines // span
    assert packs % 2 == 0
    shape = jax.ShapeDtypeStruct
    (packed,) = call(
        pack_kernel,
        "pack",
        [shape((packs, points, LANES), BF16)],
        orbitals.size,
        4 * orbitals.size,
        operands=1,
    )(orbitals)
    guests = exchanged(packed)
    tables = spectral_tables(points)
    (response,) = call(
        response_kernel,
        "response",
        [shape((lines, points, padded), F32)],
        4 * lines * points**3,
        4 * lines * points**2,
        operands=2,
    )(coulomb, tables)
    blocks = len(guests) + 1
    high, parts = call(
        functools.partial(image_kernel, members),
        "image",
        [
            shape((packs, points, LANES), BF16),
            shape((2 * packs, points, LANES), BF16),
        ],
        2 * lines * points * padded * (4 * LANES),
        4 * lines * points**2,
        scalars=1,
        operands=blocks + 1,
    )(occupied, packed, *guests, response)
    (overlap,) = call(
        overlap_kernel,
        "overlap",
        [shape((members, LANES), F32)],
        4 * packs * points * LANES**2,
        8 * orbitals.size,
        operands=2,
    )(orbitals, parts)
    overlaps = [overlap] + [swapped(overlap, flip) for flip in range(1, groups)]
    images = [parts] + [swapped(parts, flip) for flip in range(1, near)]
    for grid in range(1, grids):
        across = swapped(high, grid * near)
        images += [across] + [swapped(across, flip) for flip in range(1, near)]
    cells = lines * groups * points

    intersection, weights = call(
        functools.partial(factor_kernel, cells),
        "factor",
        [shape((members, members), F32), shape((4 * CAP * span, 2 * LANES), BF16)],
        FACTOR_COST,
        members**2 * 4,
        operands=1 + groups,
    )(owners, *overlaps)
    routed, intersection = call(
        route_kernel,
        "route",
        [shape((CAP, groups * lines, points), BF16), shape((members, members), F32)],
        2 * CAP * members * groups * lines * points,
        6 * members * groups * lines * points,
        scratch=[
            pltpu.VMEM((groups, CAP, lines, points), BF16),
            pltpu.SemaphoreType.DMA((groups + 1,)),
        ],
        operands=2 + groups,
        remote=True,
    )(intersection, weights, *images)
    return routed[None, None], intersection[None]


def solution(mesh):
    in_specs = (P("band", ("grid", "ham"), None), P(("grid", "ham"), None), P(), P("band", None))
    out_specs = (P("band", ("grid", "ham"), None, None, None), P("band", None, None))
    return jax.shard_map(local, mesh=mesh, in_specs=in_specs, out_specs=out_specs, check_vma=False)
```

```python
import functools
import math

import jax
import jax.numpy as jnp
import numpy as np
from jax import lax
from jax.experimental import pallas as pl
from jax.experimental.pallas import tpu as pltpu
from jax.sharding import PartitionSpec as P

CAP = 8
LANES = 128
HIGHEST = lax.Precision.HIGHEST
VMEM_LIMIT = 48 * 1024 * 1024
FACTOR_COST = 3_000_000_000
NT = ((1,), (1,))
F32, BF16 = jnp.float32, jnp.bfloat16


STEPS = (-1, -2, 2, 1)


def sources(block, count):
    return [(block + step + count) % count for step in STEPS]


def exchanged(value):
    count = lax.axis_size("band")
    assert count % 4 == 0
    tables = [sources(block, count) for block in range(count)]
    return [
        lax.ppermute(value, "band", [(row[turn], block) for block, row in enumerate(tables)])
        for turn in range(4)
    ]


def swapped(value, flip):
    count = lax.axis_size("grid") * lax.axis_size("ham")
    return lax.ppermute(value, ("grid", "ham"), [(group, group ^ flip) for group in range(count)])


def spectral_tables(points):
    midpoint = points // 2
    ids = np.arange(points)
    frequency = np.where(ids <= midpoint, ids, ids - midpoint)
    angles = (ids[:, None] * frequency[None, :] % points) * (2.0 * math.pi / points)
    forward = np.where((ids <= midpoint)[None, :], np.cos(angles), np.sin(angles))
    single = (frequency == 0) | (ids == midpoint)
    inverse = forward.T * (np.where(single, 1.0, 2.0) / points)[:, None]
    mirror = np.zeros((points, points))
    mirror[frequency, ids] += 0.5
    mirror[(points - frequency) % points, ids] += 0.5
    return jnp.asarray(np.stack([forward.T, inverse.T, mirror]).astype(np.float32)).astype(BF16)


def split(value):
    high = value.astype(BF16)
    return high, value - high.astype(F32)


def halves(value):
    high, rest = split(value)
    return high, rest.astype(BF16)


def dot32(a, b, contract=((1,), (0,))):
    return lax.dot_general(a, b, (contract, ((), ())), preferred_element_type=F32)


def dot_exact(a, b, contract=((1,), (0,))):
    return lax.dot_general(
        a, b, (contract, ((), ())), precision=HIGHEST, preferred_element_type=F32
    )


def ids(shape, axis):
    return lax.broadcasted_iota(jnp.int32, shape, axis)


def lane_member(lane, members):
    return lane % members


def lane_quarter(lane, turn):
    return (lane // (LANES // 4)) ^ turn


def lane_line(lane, turn, members):
    per = LANES // 4 // members
    return lane_quarter(lane, turn) * per + lane % (LANES // 4) // members


def own_turn():
    return lax.axis_index("band") % 4


def rows_of(block, pack, span):
    members, _, points = block.shape
    part = block[:, pack * span : (pack + 1) * span, :]
    return part.reshape(members * span, points)


def pack_kernel(orbitals_ref, out_ref):
    members = orbitals_ref.shape[0]
    span = LANES // members
    block = orbitals_ref[...].astype(F32)
    row, lane = ids((LANES, LANES), 0), ids((LANES, LANES), 1)
    source = lane_member(lane, members) * span + lane_line(lane, own_turn(), members)
    order = (row == source).astype(BF16)
    for pack in range(out_ref.shape[0]):
        rows = rows_of(block, pack, span).T.astype(BF16)
        out_ref[pack] = dot32(rows, order).astype(BF16)


def response_kernel(coulomb_ref, tables_ref, out_ref):
    points = coulomb_ref.shape[1]
    multiplier = dot_exact(coulomb_ref[...], tables_ref[2].astype(F32))
    forward = tables_ref[0]
    inverse = tables_ref[1].astype(F32)
    pad = jnp.zeros((points, out_ref.shape[2] - points), F32)
    for line in range(coulomb_ref.shape[0]):
        high, low = halves(inverse * multiplier[line : line + 1, :])
        out_ref[line, :, :points] = dot32(high, forward) + dot32(low, forward)
        out_ref[line, :, points:] = pad


def image_kernel(members, occupied_ref, *refs):
    blocks, (response_ref, high_ref, halves_ref) = refs[:-3], refs[-3:]
    packs, points, _ = blocks[0].shape
    padded = response_ref.shape[2]
    span = LANES // members
    per = span // 4
    total = lax.axis_size("band")
    position = lax.axis_index("band")
    places = [position] + sources(position, total)
    turns = [place % 4 for place in places]
    lane = ids((1, LANES), 1)
    own_line = lane_line(lane, turns[0], members)
    filled = [lane_member(lane, members) < occupied_ref[place] for place in places]
    quarters = [lane_quarter(lane, turn) for turn in turns]
    step = lane % (LANES // 4) // members
    apart, merged = 2, (0, 1, 3, 4)
    spare = padded - points
    cuts = points // spare
    assert cuts * spare == points and LANES % spare == 0
    blank = jnp.zeros((spare, 2 * LANES), BF16)
    kernels = [[[] for _ in range(cuts)] for _ in range(packs)]
    for pack in range(packs):
        tiles = [block[pack] for block in blocks]
        for quarter in range(4):
            here = [(q == quarter) for q in quarters]
            together = tiles[merged[0]]
            for m in merged[1:]:
                together = jnp.where(here[m], tiles[m], together)
            window = jnp.concatenate([together, tiles[apart]], axis=1)
            occupied = sum((here[m] & filled[m]).astype(F32) for m in merged)
            beside = (here[apart] & filled[apart]).astype(F32)
            both = jnp.concatenate([occupied, beside], axis=1)
            steps = jnp.concatenate([step, step], axis=1)
            masked = jnp.concatenate(
                [window * jnp.where(steps == k, both, 0.0).astype(BF16) for k in range(per)], axis=0
            )
            gram = dot32(masked, jnp.concatenate([window, blank], axis=0), NT)
            first = pack * span + quarter * per
            response = response_ref[first : first + per].reshape(per * points, padded)
            weighted = gram * response
            for place in range(0, per * points, spare):
                cut = place // spare % cuts
                part = weighted[place : place + spare]
                tile = cut * spare // LANES * LANES
                _, low = split(part[:, tile : tile + LANES])
                shift = LANES - spare - cut * spare % LANES
                low = pltpu.roll(low, shift, axis=1) if shift else low
                last = jnp.where(lane < LANES - spare, part[:, -LANES:], low)
                part = jnp.concatenate([part[:, :-LANES], last], axis=1)
                kernels[pack][cut].append(part.astype(BF16))
    for pack in range(packs):
        tile = blocks[0][pack]
        image = []
        for cut in range(cuts):
            native = jnp.concatenate([tile, tile[cut * spare : (cut + 1) * spare]], axis=0)
            fields = dot32(jnp.concatenate(kernels[pack][cut], axis=0), native)
            rows = jnp.zeros((spare, LANES), F32)
            for line in range(span):
                rows = jnp.where(own_line == line, fields[line * spare : (line + 1) * spare], rows)
            image.append(rows)
        image = jnp.concatenate(image, axis=0)
        high, low = halves(image)
        high_ref[pack] = high
        halves_ref[pack] = high
        halves_ref[packs + pack] = low


def overlap_kernel(orbitals_ref, halves_ref, out_ref):
    members, _, _ = orbitals_ref.shape
    span = LANES // members
    natives = orbitals_ref[...].astype(F32)
    square = (LANES, LANES)
    same_line = ids(square, 0) % span == lane_line(ids(square, 1), own_turn(), members)
    cross = jnp.zeros(square, F32)
    packs = halves_ref.shape[0] // 2
    for pack in range(packs):
        rows = rows_of(natives, pack, span).astype(BF16)
        both = jnp.concatenate([halves_ref[pack], halves_ref[packs + pack]], axis=1)
        product = dot32(rows, both)
        cross = cross + (product[:, :LANES] + product[:, LANES:])
    out_ref[...] = jnp.where(same_line, cross, 0.0).reshape(members, span, LANES).sum(axis=1)


def factor_kernel(cells, owners_ref, *refs):
    parts, (overlap_ref, weights_ref) = refs[:-2], refs[-2:]
    members = owners_ref.shape[0]
    span = LANES // members
    turn = own_turn()
    sums = [part[...] for part in parts]
    while len(sums) > 1:
        sums = [a + b for a, b in zip(sums[::2], sums[1::2])]
    high, rest = split(sums[0])
    pieces = [high, *halves(rest)]
    across = (members, LANES)
    gather = (ids(across, 0) == lane_member(ids(across, 1), members)).astype(BF16)
    overlap = sum(dot32(piece, gather, NT) for piece in pieces) * (1.0 / cells)
    flipped = sum(dot32(gather, piece, NT) for piece in pieces) * (1.0 / cells)
    overlap_ref[...] = overlap
    rows = CAP * span
    square = (members, members)
    group = lax.axis_index("grid") * lax.axis_size("ham") + lax.axis_index("ham")
    mine = (owners_ref[...] == group).astype(F32)
    eye = (ids(square, 0) == ids(square, 1)).astype(F32)
    mine_row = jnp.sum(mine * eye, axis=0, keepdims=True)
    before = (ids(square, 0) < ids(square, 1)).astype(F32)
    ranking = jnp.sum(mine * before, axis=0, keepdims=True)
    slot = (ids((rows, members), 0) // span).astype(F32)
    placed = (jnp.where(slot == ranking, 1.0, 0.0) * mine_row).astype(BF16)
    wide = (members, LANES)
    row = ids(wide, 0)
    upper = 0.5 * (overlap + flipped)
    columns = [jnp.broadcast_to(upper[:, j : j + 1], wide) for j in range(members)]
    lower = (row == lane_member(ids(wide, 1), members)).astype(F32)
    diagonal = ratio = jnp.zeros(wide, F32)
    for k in range(0, members, 2):
        first, second = columns[k], columns[k + 1]
        a, b, c = first[k : k + 1], first[k + 1 : k + 2], second[k + 1 : k + 2]
        share = b / a
        rest = c - share * b
        diagonal = jnp.where(row == k, a, jnp.where(row == k + 1, rest, diagonal))
        ratio = jnp.where(row == k + 1, share, ratio)
        scale = 1.0 / (a * c - b * b)
        below = row > k + 1
        one = jnp.where(below, (first * c - second * b) * scale, 0.0)
        two = jnp.where(below, (second * a - first * b) * scale, 0.0)
        lower = lower - (one * lower[k : k + 1] + two * lower[k + 1 : k + 2])
        for j in range(k + 2, members):
            column = columns[j]
            columns[j] = column - (one * column[k : k + 1] + two * column[k + 1 : k + 2])
    above = jnp.concatenate([lower[:1], lower[:-1]], axis=0)
    inverse = (lower - ratio * above) / jnp.sqrt(diagonal)
    high, low = halves(inverse)
    same_line = ids((rows, LANES), 0) % span == lane_line(ids((rows, LANES), 1), turn, members)
    blank = jnp.zeros((rows, LANES), BF16)
    chosen = [jnp.where(same_line, dot32(placed, half), 0.0).astype(BF16) for half in (high, low)]
    for i, half in enumerate(chosen + chosen):
        pair = [half, blank] if i < 2 else [blank, half]
        weights_ref[i * rows : (i + 1) * rows, :] = jnp.concatenate(pair, axis=1)


def route_kernel(overlap_ref, weights_ref, *refs):
    parts, (out_hbm, overlap_hbm, staged, semaphores) = refs[:-4], refs[-4:]
    groups = len(parts)
    copies = [pltpu.make_async_copy(overlap_ref, overlap_hbm, semaphores.at[groups])]
    copies[0].start()
    points = staged.shape[3]
    weights = weights_ref[...]
    rows = weights.shape[0] // 4
    span = rows // CAP
    lines = staged.shape[2]
    packs = lines // span
    highs = jnp.concatenate([weights[:rows], weights[2 * rows : 3 * rows]], axis=0)
    group = lax.axis_index("grid") * lax.axis_size("ham") + lax.axis_index("ham")
    for flip, part in enumerate(parts):
        sums = []
        for pack in range(0, packs, 2):
            field = jnp.concatenate([part[pack], part[pack + 1]], axis=1)
            both = dot32(weights, field, NT)
            results = [both[:rows] + both[rows : 2 * rows], both[2 * rows : 3 * rows] + both[3 * rows :]]
            if part.shape[0] > packs:
                place = packs + pack
                rest = dot32(highs, jnp.concatenate([part[place], part[place + 1]], axis=1), NT)
                results = [results[0] + rest[:rows], results[1] + rest[rows:]]
            sums += [result.reshape(CAP, span, points) for result in results]
        staged[flip] = jnp.concatenate(sums, axis=1).astype(BF16)
        start = pl.multiple_of((group ^ flip) * lines, lines)
        target = out_hbm.at[:, pl.ds(start, lines), :]
        copies.append(pltpu.make_async_copy(staged.at[flip], target, semaphores.at[flip]))
        copies[-1].start()
    for copy in copies:
        copy.wait()


def call(kernel, name, shapes, flops, moved, scratch=(), scalars=0, operands=0, remote=False):
    vmem = pl.BlockSpec(memory_space=pltpu.VMEM)
    smem = pl.BlockSpec(memory_space=pltpu.SMEM)
    return pl.pallas_call(
        kernel,
        name=name,
        out_shape=shapes,
        in_specs=[smem] * scalars + [vmem] * operands,
        out_specs=[pl.BlockSpec(memory_space=pl.ANY) if remote else vmem] * len(shapes),
        scratch_shapes=list(scratch),
        compiler_params=pltpu.CompilerParams(vmem_limit_bytes=VMEM_LIMIT),
        cost_estimate=pl.CostEstimate(flops=flops, bytes_accessed=moved, transcendentals=0),
    )


def local(orbitals, coulomb, occupied, owners):
    members, lines, points = orbitals.shape
    grids, near = lax.axis_size("grid"), lax.axis_size("ham")
    groups = grids * near
    padded = -(-points // LANES) * LANES
    span = LANES // members
    packs = lines // span
    assert packs % 2 == 0
    shape = jax.ShapeDtypeStruct
    (packed,) = call(
        pack_kernel,
        "pack",
        [shape((packs, points, LANES), BF16)],
        orbitals.size,
        4 * orbitals.size,
        operands=1,
    )(orbitals)
    guests = exchanged(packed)
    tables = spectral_tables(points)
    (response,) = call(
        response_kernel,
        "response",
        [shape((lines, points, padded), F32)],
        4 * lines * points**3,
        4 * lines * points**2,
        operands=2,
    )(coulomb, tables)
    blocks = len(guests) + 1
    high, parts = call(
        functools.partial(image_kernel, members),
        "image",
        [
            shape((packs, points, LANES), BF16),
            shape((2 * packs, points, LANES), BF16),
        ],
        2 * lines * points * padded * (4 * LANES),
        4 * lines * points**2,
        scalars=1,
        operands=blocks + 1,
    )(occupied, packed, *guests, response)
    (overlap,) = call(
        overlap_kernel,
        "overlap",
        [shape((members, LANES), F32)],
        4 * packs * points * LANES**2,
        8 * orbitals.size,
        operands=2,
    )(orbitals, parts)
    overlaps = [overlap] + [swapped(overlap, flip) for flip in range(1, groups)]
    images = [parts] + [swapped(high, flip) for flip in range(1, near)]
    for grid in range(1, grids):
        across = swapped(high, grid * near)
        images += [across] + [swapped(across, flip) for flip in range(1, near)]
    cells = lines * groups * points

    intersection, weights = call(
        functools.partial(factor_kernel, cells),
        "factor",
        [shape((members, members), F32), shape((4 * CAP * span, 2 * LANES), BF16)],
        FACTOR_COST,
        members**2 * 4,
        operands=1 + groups,
    )(owners, *overlaps)
    routed, intersection = call(
        route_kernel,
        "route",
        [shape((CAP, groups * lines, points), BF16), shape((members, members), F32)],
        2 * CAP * members * groups * lines * points,
        6 * members * groups * lines * points,
        scratch=[
            pltpu.VMEM((groups, CAP, lines, points), BF16),
            pltpu.SemaphoreType.DMA((groups + 1,)),
        ],
        operands=2 + groups,
        remote=True,
    )(intersection, weights, *images)
    return routed[None, None], intersection[None]


def solution(mesh):
    in_specs = (P("band", ("grid", "ham"), None), P(("grid", "ham"), None), P(), P("band", None))
    out_specs = (P("band", ("grid", "ham"), None, None, None), P("band", None, None))
    return jax.shard_map(local, mesh=mesh, in_specs=in_specs, out_specs=out_specs, check_vma=False)
```

```python
import functools
import math

import jax
import jax.numpy as jnp
import numpy as np
from jax import lax
from jax.experimental import pallas as pl
from jax.experimental.pallas import tpu as pltpu
from jax.sharding import PartitionSpec as P

CAP = 8
LANES = 128
HIGHEST = lax.Precision.HIGHEST
VMEM_LIMIT = 48 * 1024 * 1024
FACTOR_COST = 3_000_000_000
NT = ((1,), (1,))
F32, BF16 = jnp.float32, jnp.bfloat16


STEPS = (-1, -2, 2, 1)


def sources(block, count):
    return [(block + step + count) % count for step in STEPS]


def exchanged(value):
    count = lax.axis_size("band")
    assert count % 4 == 0
    tables = [sources(block, count) for block in range(count)]
    return [
        lax.ppermute(value, "band", [(row[turn], block) for block, row in enumerate(tables)])
        for turn in range(4)
    ]


def swapped(value, flip):
    count = lax.axis_size("grid") * lax.axis_size("ham")
    return lax.ppermute(value, ("grid", "ham"), [(group, group ^ flip) for group in range(count)])


def spectral_tables(points):
    midpoint = points // 2
    ids = np.arange(points)
    frequency = np.where(ids <= midpoint, ids, ids - midpoint)
    angles = (ids[:, None] * frequency[None, :] % points) * (2.0 * math.pi / points)
    forward = np.where((ids <= midpoint)[None, :], np.cos(angles), np.sin(angles))
    single = (frequency == 0) | (ids == midpoint)
    inverse = forward.T * (np.where(single, 1.0, 2.0) / points)[:, None]
    mirror = np.zeros((points, points))
    mirror[frequency, ids] += 0.5
    mirror[(points - frequency) % points, ids] += 0.5
    return jnp.asarray(np.stack([forward.T, inverse.T, mirror]).astype(np.float32)).astype(BF16)


def split(value):
    high = value.astype(BF16)
    return high, value - high.astype(F32)


def halves(value):
    high, rest = split(value)
    return high, rest.astype(BF16)


def dot32(a, b, contract=((1,), (0,))):
    return lax.dot_general(a, b, (contract, ((), ())), preferred_element_type=F32)


def dot_exact(a, b, contract=((1,), (0,))):
    return lax.dot_general(
        a, b, (contract, ((), ())), precision=HIGHEST, preferred_element_type=F32
    )


def ids(shape, axis):
    return lax.broadcasted_iota(jnp.int32, shape, axis)


def lane_member(lane, members):
    return lane % members


def lane_quarter(lane, turn):
    return (lane // (LANES // 4)) ^ turn


def lane_line(lane, turn, members):
    per = LANES // 4 // members
    return lane_quarter(lane, turn) * per + lane % (LANES // 4) // members


def own_turn():
    return lax.axis_index("band") % 4


def rows_of(block, pack, span):
    members, _, points = block.shape
    part = block[:, pack * span : (pack + 1) * span, :]
    return part.reshape(members * span, points)


def pack_kernel(orbitals_ref, out_ref):
    members = orbitals_ref.shape[0]
    span = LANES // members
    block = orbitals_ref[...].astype(F32)
    row, lane = ids((LANES, LANES), 0), ids((LANES, LANES), 1)
    source = lane_member(lane, members) * span + lane_line(lane, own_turn(), members)
    order = (row == source).astype(BF16)
    for pack in range(out_ref.shape[0]):
        rows = rows_of(block, pack, span).T.astype(BF16)
        out_ref[pack] = dot32(rows, order).astype(BF16)


def response_kernel(coulomb_ref, tables_ref, out_ref):
    points = coulomb_ref.shape[1]
    multiplier = dot_exact(coulomb_ref[...], tables_ref[2].astype(F32))
    forward = tables_ref[0]
    inverse = tables_ref[1].astype(F32)
    pad = jnp.zeros((points, out_ref.shape[2] - points), F32)
    for line in range(coulomb_ref.shape[0]):
        high, low = halves(inverse * multiplier[line : line + 1, :])
        out_ref[line, :, :points] = dot32(high, forward) + dot32(low, forward)
        out_ref[line, :, points:] = pad


def image_kernel(members, occupied_ref, *refs):
    blocks, (response_ref, high_ref, halves_ref) = refs[:-3], refs[-3:]
    packs, points, _ = blocks[0].shape
    padded = response_ref.shape[2]
    span = LANES // members
    per = span // 4
    total = lax.axis_size("band")
    position = lax.axis_index("band")
    places = [position] + sources(position, total)
    turns = [place % 4 for place in places]
    lane = ids((1, LANES), 1)
    own_line = lane_line(lane, turns[0], members)
    filled = [lane_member(lane, members) < occupied_ref[place] for place in places]
    quarters = [lane_quarter(lane, turn) for turn in turns]
    step = lane % (LANES // 4) // members
    apart, merged = 2, (0, 1, 3, 4)
    spare = padded - points
    cuts = points // spare
    assert cuts * spare == points and LANES % spare == 0
    blank = jnp.zeros((spare, 2 * LANES), BF16)
    kernels = [[[] for _ in range(cuts)] for _ in range(packs)]
    for pack in range(packs):
        tiles = [block[pack] for block in blocks]
        for quarter in range(4):
            here = [(q == quarter) for q in quarters]
            together = tiles[merged[0]]
            for m in merged[1:]:
                together = jnp.where(here[m], tiles[m], together)
            window = jnp.concatenate([together, tiles[apart]], axis=1)
            occupied = sum((here[m] & filled[m]).astype(F32) for m in merged)
            beside = (here[apart] & filled[apart]).astype(F32)
            both = jnp.concatenate([occupied, beside], axis=1)
            steps = jnp.concatenate([step, step], axis=1)
            masked = jnp.concatenate(
                [window * jnp.where(steps == k, both, 0.0).astype(BF16) for k in range(per)], axis=0
            )
            gram = dot32(masked, jnp.concatenate([window, blank], axis=0), NT)
            first = pack * span + quarter * per
            response = response_ref[first : first + per].reshape(per * points, padded)
            weighted = gram * response
            for place in range(0, per * points, spare):
                cut = place // spare % cuts
                part = weighted[place : place + spare]
                tile = cut * spare // LANES * LANES
                _, low = split(part[:, tile : tile + LANES])
                shift = LANES - spare - cut * spare % LANES
                low = pltpu.roll(low, shift, axis=1) if shift else low
                last = jnp.where(lane < LANES - spare, part[:, -LANES:], low)
                part = jnp.concatenate([part[:, :-LANES], last], axis=1)
                kernels[pack][cut].append(part.astype(BF16))
    for pack in range(packs):
        tile = blocks[0][pack]
        image = []
        for cut in range(cuts):
            native = jnp.concatenate([tile, tile[cut * spare : (cut + 1) * spare]], axis=0)
            fields = dot32(jnp.concatenate(kernels[pack][cut], axis=0), native)
            rows = jnp.zeros((spare, LANES), F32)
            for line in range(span):
                rows = jnp.where(own_line == line, fields[line * spare : (line + 1) * spare], rows)
            image.append(rows)
        image = jnp.concatenate(image, axis=0)
        high, low = halves(image)
        high_ref[pack] = high
        halves_ref[pack] = high
        halves_ref[packs + pack] = low


def overlap_kernel(orbitals_ref, halves_ref, out_ref):
    members, _, _ = orbitals_ref.shape
    span = LANES // members
    natives = orbitals_ref[...].astype(F32)
    square = (LANES, LANES)
    same_line = ids(square, 0) % span == lane_line(ids(square, 1), own_turn(), members)
    cross = jnp.zeros(square, F32)
    packs = halves_ref.shape[0] // 2
    for pack in range(packs):
        rows = rows_of(natives, pack, span).astype(BF16)
        both = jnp.concatenate([halves_ref[pack], halves_ref[packs + pack]], axis=1)
        product = dot32(rows, both)
        cross = cross + (product[:, :LANES] + product[:, LANES:])
    out_ref[...] = jnp.where(same_line, cross, 0.0).reshape(members, span, LANES).sum(axis=1)


def factor_kernel(cells, owners_ref, *refs):
    parts, (overlap_ref, weights_ref) = refs[:-2], refs[-2:]
    members = owners_ref.shape[0]
    span = LANES // members
    turn = own_turn()
    sums = [part[...] for part in reversed(parts)]
    while len(sums) > 1:
        sums = [a + b for a, b in zip(sums[::2], sums[1::2])]
    high, rest = split(sums[0])
    pieces = [high, *halves(rest)]
    across = (members, LANES)
    gather = (ids(across, 0) == lane_member(ids(across, 1), members)).astype(BF16)
    overlap = sum(dot32(piece, gather, NT) for piece in pieces) * (1.0 / cells)
    flipped = sum(dot32(gather, piece, NT) for piece in pieces) * (1.0 / cells)
    overlap_ref[...] = overlap
    rows = CAP * span
    square = (members, members)
    group = lax.axis_index("grid") * lax.axis_size("ham") + lax.axis_index("ham")
    mine = (owners_ref[...] == group).astype(F32)
    eye = (ids(square, 0) == ids(square, 1)).astype(F32)
    mine_row = jnp.sum(mine * eye, axis=0, keepdims=True)
    before = (ids(square, 0) < ids(square, 1)).astype(F32)
    ranking = jnp.sum(mine * before, axis=0, keepdims=True)
    slot = (ids((rows, members), 0) // span).astype(F32)
    placed = (jnp.where(slot == ranking, 1.0, 0.0) * mine_row).astype(BF16)
    wide = (members, LANES)
    row = ids(wide, 0)
    upper = 0.5 * (overlap + flipped)
    columns = [jnp.broadcast_to(upper[:, j : j + 1], wide) for j in range(members)]
    lower = (row == lane_member(ids(wide, 1), members)).astype(F32)
    diagonal = ratio = jnp.zeros(wide, F32)
    for k in range(0, members, 2):
        first, second = columns[k], columns[k + 1]
        a, b, c = first[k : k + 1], first[k + 1 : k + 2], second[k + 1 : k + 2]
        share = b / a
        rest = c - share * b
        diagonal = jnp.where(row == k, a, jnp.where(row == k + 1, rest, diagonal))
        ratio = jnp.where(row == k + 1, share, ratio)
        scale = 1.0 / (a * c - b * b)
        below = row > k + 1
        one = jnp.where(below, (first * c - second * b) * scale, 0.0)
        two = jnp.where(below, (second * a - first * b) * scale, 0.0)
        lower = lower - (one * lower[k : k + 1] + two * lower[k + 1 : k + 2])
        for j in range(k + 2, members):
            column = columns[j]
            columns[j] = column - (one * column[k : k + 1] + two * column[k + 1 : k + 2])
    above = jnp.concatenate([lower[:1], lower[:-1]], axis=0)
    inverse = (lower - ratio * above) / jnp.sqrt(diagonal)
    high, low = halves(inverse)
    same_line = ids((rows, LANES), 0) % span == lane_line(ids((rows, LANES), 1), turn, members)
    blank = jnp.zeros((rows, LANES), BF16)
    chosen = [jnp.where(same_line, dot32(placed, half), 0.0).astype(BF16) for half in (high, low)]
    for i, half in enumerate(chosen + chosen):
        pair = [half, blank] if i < 2 else [blank, half]
        weights_ref[i * rows : (i + 1) * rows, :] = jnp.concatenate(pair, axis=1)


def route_kernel(overlap_ref, weights_ref, *refs):
    parts, (out_hbm, overlap_hbm, staged, semaphores) = refs[:-4], refs[-4:]
    groups = len(parts)
    copies = [pltpu.make_async_copy(overlap_ref, overlap_hbm, semaphores.at[groups])]
    copies[0].start()
    points = staged.shape[3]
    weights = weights_ref[...]
    rows = weights.shape[0] // 4
    span = rows // CAP
    lines = staged.shape[2]
    packs = lines // span
    highs = jnp.concatenate([weights[:rows], weights[2 * rows : 3 * rows]], axis=0)
    group = lax.axis_index("grid") * lax.axis_size("ham") + lax.axis_index("ham")
    for flip, part in enumerate(parts):
        sums = []
        for pack in range(0, packs, 2):
            field = jnp.concatenate([part[pack], part[pack + 1]], axis=1)
            both = dot32(weights, field, NT)
            results = [both[:rows] + both[rows : 2 * rows], both[2 * rows : 3 * rows] + both[3 * rows :]]
            if part.shape[0] > packs:
                place = packs + pack
                rest = dot32(highs, jnp.concatenate([part[place], part[place + 1]], axis=1), NT)
                results = [results[0] + rest[:rows], results[1] + rest[rows:]]
            sums += [result.reshape(CAP, span, points) for result in results]
        staged[flip] = jnp.concatenate(sums, axis=1).astype(BF16)
        start = pl.multiple_of((group ^ flip) * lines, lines)
        target = out_hbm.at[:, pl.ds(start, lines), :]
        copies.append(pltpu.make_async_copy(staged.at[flip], target, semaphores.at[flip]))
        copies[-1].start()
    for copy in copies:
        copy.wait()


def call(kernel, name, shapes, flops, moved, scratch=(), scalars=0, operands=0, remote=False):
    vmem = pl.BlockSpec(memory_space=pltpu.VMEM)
    smem = pl.BlockSpec(memory_space=pltpu.SMEM)
    return pl.pallas_call(
        kernel,
        name=name,
        out_shape=shapes,
        in_specs=[smem] * scalars + [vmem] * operands,
        out_specs=[pl.BlockSpec(memory_space=pl.ANY) if remote else vmem] * len(shapes),
        scratch_shapes=list(scratch),
        compiler_params=pltpu.CompilerParams(vmem_limit_bytes=VMEM_LIMIT),
        cost_estimate=pl.CostEstimate(flops=flops, bytes_accessed=moved, transcendentals=0),
    )


def local(orbitals, coulomb, occupied, owners):
    members, lines, points = orbitals.shape
    grids, near = lax.axis_size("grid"), lax.axis_size("ham")
    groups = grids * near
    padded = -(-points // LANES) * LANES
    span = LANES // members
    packs = lines // span
    assert packs % 2 == 0
    shape = jax.ShapeDtypeStruct
    (packed,) = call(
        pack_kernel,
        "pack",
        [shape((packs, points, LANES), BF16)],
        orbitals.size,
        4 * orbitals.size,
        operands=1,
    )(orbitals)
    guests = exchanged(packed)
    tables = spectral_tables(points)
    (response,) = call(
        response_kernel,
        "response",
        [shape((lines, points, padded), F32)],
        4 * lines * points**3,
        4 * lines * points**2,
        operands=2,
    )(coulomb, tables)
    blocks = len(guests) + 1
    high, parts = call(
        functools.partial(image_kernel, members),
        "image",
        [
            shape((packs, points, LANES), BF16),
            shape((2 * packs, points, LANES), BF16),
        ],
        2 * lines * points * padded * (4 * LANES),
        4 * lines * points**2,
        scalars=1,
        operands=blocks + 1,
    )(occupied, packed, *guests, response)
    (overlap,) = call(
        overlap_kernel,
        "overlap",
        [shape((members, LANES), F32)],
        4 * packs * points * LANES**2,
        8 * orbitals.size,
        operands=2,
    )(orbitals, parts)
    overlaps = [swapped(overlap, flip) for flip in reversed(range(1, groups))] + [overlap]
    images = [parts] + [swapped(parts, flip) for flip in range(1, near)]
    for grid in range(1, grids):
        across = swapped(high, grid * near)
        images += [across] + [swapped(across, flip) for flip in range(1, near)]
    cells = lines * groups * points

    intersection, weights = call(
        functools.partial(factor_kernel, cells),
        "factor",
        [shape((members, members), F32), shape((4 * CAP * span, 2 * LANES), BF16)],
        FACTOR_COST,
        members**2 * 4,
        operands=1 + groups,
    )(owners, *overlaps)
    routed, intersection = call(
        route_kernel,
        "route",
        [shape((CAP, groups * lines, points), BF16), shape((members, members), F32)],
        2 * CAP * members * groups * lines * points,
        6 * members * groups * lines * points,
        scratch=[
            pltpu.VMEM((groups, CAP, lines, points), BF16),
            pltpu.SemaphoreType.DMA((groups + 1,)),
        ],
        operands=2 + groups,
        remote=True,
    )(intersection, weights, *images)
    return routed[None, None], intersection[None]


def solution(mesh):
    in_specs = (P("band", ("grid", "ham"), None), P(("grid", "ham"), None), P(), P("band", None))
    out_specs = (P("band", ("grid", "ham"), None, None, None), P("band", None, None))
    return jax.shard_map(local, mesh=mesh, in_specs=in_specs, out_specs=out_specs, check_vma=False)
```

```python
import functools
import math

import jax
import jax.numpy as jnp
import numpy as np
from jax import lax
from jax.experimental import pallas as pl
from jax.experimental.pallas import tpu as pltpu
from jax.sharding import PartitionSpec as P

CAP = 8
LANES = 128
HIGHEST = lax.Precision.HIGHEST
VMEM_LIMIT = 48 * 1024 * 1024
FACTOR_COST = 3_000_000_000
NT = ((1,), (1,))
F32, BF16 = jnp.float32, jnp.bfloat16


STEPS = (-1, -2, 2, 1)


def sources(block, count):
    return [(block + step + count) % count for step in STEPS]


def exchanged(value):
    count = lax.axis_size("band")
    assert count % 4 == 0
    tables = [sources(block, count) for block in range(count)]
    return [
        lax.ppermute(value, "band", [(row[turn], block) for block, row in enumerate(tables)])
        for turn in range(4)
    ]


def swapped(value, flip):
    count = lax.axis_size("grid") * lax.axis_size("ham")
    return lax.ppermute(value, ("grid", "ham"), [(group, group ^ flip) for group in range(count)])


def spectral_tables(points):
    midpoint = points // 2
    ids = np.arange(points)
    frequency = np.where(ids <= midpoint, ids, ids - midpoint)
    angles = (ids[:, None] * frequency[None, :] % points) * (2.0 * math.pi / points)
    forward = np.where((ids <= midpoint)[None, :], np.cos(angles), np.sin(angles))
    single = (frequency == 0) | (ids == midpoint)
    inverse = forward.T * (np.where(single, 1.0, 2.0) / points)[:, None]
    mirror = np.zeros((points, points))
    mirror[frequency, ids] += 0.5
    mirror[(points - frequency) % points, ids] += 0.5
    return jnp.asarray(np.stack([forward.T, inverse.T, mirror]).astype(np.float32)).astype(BF16)


def split(value):
    high = value.astype(BF16)
    return high, value - high.astype(F32)


def halves(value):
    high, rest = split(value)
    return high, rest.astype(BF16)


def dot32(a, b, contract=((1,), (0,))):
    return lax.dot_general(a, b, (contract, ((), ())), preferred_element_type=F32)


def dot_exact(a, b, contract=((1,), (0,))):
    return lax.dot_general(
        a, b, (contract, ((), ())), precision=HIGHEST, preferred_element_type=F32
    )


def ids(shape, axis):
    return lax.broadcasted_iota(jnp.int32, shape, axis)


def lane_member(lane, members):
    return lane % members


def lane_quarter(lane, turn):
    return (lane // (LANES // 4)) ^ turn


def lane_line(lane, turn, members):
    per = LANES // 4 // members
    return lane_quarter(lane, turn) * per + lane % (LANES // 4) // members


def own_turn():
    return lax.axis_index("band") % 4


def rows_of(block, pack, span):
    members, _, points = block.shape
    part = block[:, pack * span : (pack + 1) * span, :]
    return part.reshape(members * span, points)


def pack_kernel(orbitals_ref, out_ref):
    members = orbitals_ref.shape[0]
    span = LANES // members
    block = orbitals_ref[...].astype(F32)
    row, lane = ids((LANES, LANES), 0), ids((LANES, LANES), 1)
    source = lane_member(lane, members) * span + lane_line(lane, own_turn(), members)
    order = (row == source).astype(BF16)
    for pack in range(out_ref.shape[0]):
        rows = rows_of(block, pack, span).T.astype(BF16)
        out_ref[pack] = dot32(rows, order).astype(BF16)


def response_kernel(coulomb_ref, tables_ref, out_ref):
    points = coulomb_ref.shape[1]
    multiplier = dot_exact(coulomb_ref[...], tables_ref[2].astype(F32))
    forward = tables_ref[0]
    inverse = tables_ref[1].astype(F32)
    pad = jnp.zeros((points, out_ref.shape[2] - points), F32)
    for line in range(coulomb_ref.shape[0]):
        high, low = halves(inverse * multiplier[line : line + 1, :])
        out_ref[line, :, :points] = dot32(high, forward) + dot32(low, forward)
        out_ref[line, :, points:] = pad


def image_kernel(members, occupied_ref, *refs):
    blocks, (response_ref, high_ref, halves_ref) = refs[:-3], refs[-3:]
    packs, points, _ = blocks[0].shape
    padded = response_ref.shape[2]
    span = LANES // members
    per = span // 4
    total = lax.axis_size("band")
    position = lax.axis_index("band")
    places = [position] + sources(position, total)
    turns = [place % 4 for place in places]
    lane = ids((1, LANES), 1)
    own_line = lane_line(lane, turns[0], members)
    filled = [lane_member(lane, members) < occupied_ref[place] for place in places]
    quarters = [lane_quarter(lane, turn) for turn in turns]
    step = lane % (LANES // 4) // members
    apart, merged = 2, (0, 1, 3, 4)
    spare = padded - points
    cuts = points // spare
    assert cuts * spare == points and LANES % spare == 0
    blank = jnp.zeros((spare, 2 * LANES), BF16)
    kernels = [[[] for _ in range(cuts)] for _ in range(packs)]
    for pack in range(packs):
        tiles = [block[pack] for block in blocks]
        for quarter in range(4):
            here = [(q == quarter) for q in quarters]
            together = tiles[merged[0]]
            for m in merged[1:]:
                together = jnp.where(here[m], tiles[m], together)
            window = jnp.concatenate([together, tiles[apart]], axis=1)
            occupied = sum((here[m] & filled[m]).astype(F32) for m in merged)
            beside = (here[apart] & filled[apart]).astype(F32)
            both = jnp.concatenate([occupied, beside], axis=1)
            steps = jnp.concatenate([step, step], axis=1)
            masked = jnp.concatenate(
                [window * jnp.where(steps == k, both, 0.0).astype(BF16) for k in range(per)], axis=0
            )
            gram = dot32(masked, jnp.concatenate([window, blank], axis=0), NT)
            first = pack * span + quarter * per
            response = response_ref[first : first + per].reshape(per * points, padded)
            weighted = gram * response
            for place in range(0, per * points, spare):
                cut = place // spare % cuts
                part = weighted[place : place + spare]
                tile = cut * spare // LANES * LANES
                _, low = split(part[:, tile : tile + LANES])
                shift = LANES - spare - cut * spare % LANES
                low = pltpu.roll(low, shift, axis=1) if shift else low
                last = jnp.where(lane < LANES - spare, part[:, -LANES:], low)
                part = jnp.concatenate([part[:, :-LANES], last], axis=1)
                kernels[pack][cut].append(part.astype(BF16))
    for pack in range(packs):
        tile = blocks[0][pack]
        image = []
        for cut in range(cuts):
            native = jnp.concatenate([tile, tile[cut * spare : (cut + 1) * spare]], axis=0)
            fields = dot32(jnp.concatenate(kernels[pack][cut], axis=0), native)
            rows = jnp.zeros((spare, LANES), F32)
            for line in range(span):
                rows = jnp.where(own_line == line, fields[line * spare : (line + 1) * spare], rows)
            image.append(rows)
        image = jnp.concatenate(image, axis=0)
        high, low = halves(image)
        high_ref[pack] = high
        halves_ref[pack] = high
        halves_ref[packs + pack] = low


def overlap_kernel(orbitals_ref, halves_ref, out_ref):
    members, _, _ = orbitals_ref.shape
    span = LANES // members
    natives = orbitals_ref[...].astype(F32)
    square = (LANES, LANES)
    same_line = ids(square, 0) % span == lane_line(ids(square, 1), own_turn(), members)
    cross = jnp.zeros(square, F32)
    packs = halves_ref.shape[0] // 2
    for pack in range(packs):
        rows = rows_of(natives, pack, span).astype(BF16)
        both = jnp.concatenate([halves_ref[pack], halves_ref[packs + pack]], axis=1)
        product = dot32(rows, both)
        cross = cross + (product[:, :LANES] + product[:, LANES:])
    out_ref[...] = jnp.where(same_line, cross, 0.0).reshape(members, span, LANES).sum(axis=1)


def factor_kernel(cells, turns, owners_ref, *refs):
    parts, (overlap_ref, weights_ref) = refs[:-2], refs[-2:]
    members = owners_ref.shape[0]
    span = LANES // members
    turn = own_turn()
    sums = [parts[place][...] for place in [len(turns)] + [turns.index(f) for f in range(1, len(parts))]]
    while len(sums) > 1:
        sums = [a + b for a, b in zip(sums[::2], sums[1::2])]
    high, rest = split(sums[0])
    pieces = [high, *halves(rest)]
    across = (members, LANES)
    gather = (ids(across, 0) == lane_member(ids(across, 1), members)).astype(BF16)
    overlap = sum(dot32(piece, gather, NT) for piece in pieces) * (1.0 / cells)
    flipped = sum(dot32(gather, piece, NT) for piece in pieces) * (1.0 / cells)
    overlap_ref[...] = overlap
    rows = CAP * span
    square = (members, members)
    group = lax.axis_index("grid") * lax.axis_size("ham") + lax.axis_index("ham")
    mine = (owners_ref[...] == group).astype(F32)
    eye = (ids(square, 0) == ids(square, 1)).astype(F32)
    mine_row = jnp.sum(mine * eye, axis=0, keepdims=True)
    before = (ids(square, 0) < ids(square, 1)).astype(F32)
    ranking = jnp.sum(mine * before, axis=0, keepdims=True)
    slot = (ids((rows, members), 0) // span).astype(F32)
    placed = (jnp.where(slot == ranking, 1.0, 0.0) * mine_row).astype(BF16)
    wide = (members, LANES)
    row = ids(wide, 0)
    upper = 0.5 * (overlap + flipped)
    columns = [jnp.broadcast_to(upper[:, j : j + 1], wide) for j in range(members)]
    lower = (row == lane_member(ids(wide, 1), members)).astype(F32)
    diagonal = ratio = jnp.zeros(wide, F32)
    for k in range(0, members, 2):
        first, second = columns[k], columns[k + 1]
        a, b, c = first[k : k + 1], first[k + 1 : k + 2], second[k + 1 : k + 2]
        share = b / a
        rest = c - share * b
        diagonal = jnp.where(row == k, a, jnp.where(row == k + 1, rest, diagonal))
        ratio = jnp.where(row == k + 1, share, ratio)
        scale = 1.0 / (a * c - b * b)
        below = row > k + 1
        one = jnp.where(below, (first * c - second * b) * scale, 0.0)
        two = jnp.where(below, (second * a - first * b) * scale, 0.0)
        lower = lower - (one * lower[k : k + 1] + two * lower[k + 1 : k + 2])
        for j in range(k + 2, members):
            column = columns[j]
            columns[j] = column - (one * column[k : k + 1] + two * column[k + 1 : k + 2])
    above = jnp.concatenate([lower[:1], lower[:-1]], axis=0)
    inverse = (lower - ratio * above) / jnp.sqrt(diagonal)
    high, low = halves(inverse)
    same_line = ids((rows, LANES), 0) % span == lane_line(ids((rows, LANES), 1), turn, members)
    blank = jnp.zeros((rows, LANES), BF16)
    chosen = [jnp.where(same_line, dot32(placed, half), 0.0).astype(BF16) for half in (high, low)]
    for i, half in enumerate(chosen + chosen):
        pair = [half, blank] if i < 2 else [blank, half]
        weights_ref[i * rows : (i + 1) * rows, :] = jnp.concatenate(pair, axis=1)


def route_kernel(overlap_ref, weights_ref, *refs):
    parts, (out_hbm, overlap_hbm, staged, semaphores) = refs[:-4], refs[-4:]
    groups = len(parts)
    copies = [pltpu.make_async_copy(overlap_ref, overlap_hbm, semaphores.at[groups])]
    copies[0].start()
    points = staged.shape[3]
    weights = weights_ref[...]
    rows = weights.shape[0] // 4
    span = rows // CAP
    lines = staged.shape[2]
    packs = lines // span
    highs = jnp.concatenate([weights[:rows], weights[2 * rows : 3 * rows]], axis=0)
    group = lax.axis_index("grid") * lax.axis_size("ham") + lax.axis_index("ham")
    for flip, part in enumerate(parts):
        sums = []
        for pack in range(0, packs, 2):
            field = jnp.concatenate([part[pack], part[pack + 1]], axis=1)
            both = dot32(weights, field, NT)
            results = [both[:rows] + both[rows : 2 * rows], both[2 * rows : 3 * rows] + both[3 * rows :]]
            if part.shape[0] > packs:
                place = packs + pack
                rest = dot32(highs, jnp.concatenate([part[place], part[place + 1]], axis=1), NT)
                results = [results[0] + rest[:rows], results[1] + rest[rows:]]
            sums += [result.reshape(CAP, span, points) for result in results]
        staged[flip] = jnp.concatenate(sums, axis=1).astype(BF16)
        start = pl.multiple_of((group ^ flip) * lines, lines)
        target = out_hbm.at[:, pl.ds(start, lines), :]
        copies.append(pltpu.make_async_copy(staged.at[flip], target, semaphores.at[flip]))
        copies[-1].start()
    for copy in copies:
        copy.wait()


def call(kernel, name, shapes, flops, moved, scratch=(), scalars=0, operands=0, remote=False):
    vmem = pl.BlockSpec(memory_space=pltpu.VMEM)
    smem = pl.BlockSpec(memory_space=pltpu.SMEM)
    return pl.pallas_call(
        kernel,
        name=name,
        out_shape=shapes,
        in_specs=[smem] * scalars + [vmem] * operands,
        out_specs=[pl.BlockSpec(memory_space=pl.ANY) if remote else vmem] * len(shapes),
        scratch_shapes=list(scratch),
        compiler_params=pltpu.CompilerParams(vmem_limit_bytes=VMEM_LIMIT),
        cost_estimate=pl.CostEstimate(flops=flops, bytes_accessed=moved, transcendentals=0),
    )


def local(orbitals, coulomb, occupied, owners):
    members, lines, points = orbitals.shape
    grids, near = lax.axis_size("grid"), lax.axis_size("ham")
    groups = grids * near
    padded = -(-points // LANES) * LANES
    span = LANES // members
    packs = lines // span
    assert packs % 2 == 0
    shape = jax.ShapeDtypeStruct
    (packed,) = call(
        pack_kernel,
        "pack",
        [shape((packs, points, LANES), BF16)],
        orbitals.size,
        4 * orbitals.size,
        operands=1,
    )(orbitals)
    guests = exchanged(packed)
    tables = spectral_tables(points)
    (response,) = call(
        response_kernel,
        "response",
        [shape((lines, points, padded), F32)],
        4 * lines * points**3,
        4 * lines * points**2,
        operands=2,
    )(coulomb, tables)
    blocks = len(guests) + 1
    high, parts = call(
        functools.partial(image_kernel, members),
        "image",
        [
            shape((packs, points, LANES), BF16),
            shape((2 * packs, points, LANES), BF16),
        ],
        2 * lines * points * padded * (4 * LANES),
        4 * lines * points**2,
        scalars=1,
        operands=blocks + 1,
    )(occupied, packed, *guests, response)
    (overlap,) = call(
        overlap_kernel,
        "overlap",
        [shape((members, LANES), F32)],
        4 * packs * points * LANES**2,
        8 * orbitals.size,
        operands=2,
    )(orbitals, parts)
    turns = [*range(near, groups), *range(1, near)]
    overlaps = [swapped(overlap, flip) for flip in turns] + [overlap]
    images = [parts] + [swapped(parts, flip) for flip in range(1, near)]
    for grid in range(1, grids):
        across = swapped(high, grid * near)
        images += [across] + [swapped(across, flip) for flip in range(1, near)]
    cells = lines * groups * points

    intersection, weights = call(
        functools.partial(factor_kernel, cells, turns),
        "factor",
        [shape((members, members), F32), shape((4 * CAP * span, 2 * LANES), BF16)],
        FACTOR_COST,
        members**2 * 4,
        operands=1 + groups,
    )(owners, *overlaps)
    routed, intersection = call(
        route_kernel,
        "route",
        [shape((CAP, groups * lines, points), BF16), shape((members, members), F32)],
        2 * CAP * members * groups * lines * points,
        6 * members * groups * lines * points,
        scratch=[
            pltpu.VMEM((groups, CAP, lines, points), BF16),
            pltpu.SemaphoreType.DMA((groups + 1,)),
        ],
        operands=2 + groups,
        remote=True,
    )(intersection, weights, *images)
    return routed[None, None], intersection[None]


def solution(mesh):
    in_specs = (P("band", ("grid", "ham"), None), P(("grid", "ham"), None), P(), P("band", None))
    out_specs = (P("band", ("grid", "ham"), None, None, None), P("band", None, None))
    return jax.shard_map(local, mesh=mesh, in_specs=in_specs, out_specs=out_specs, check_vma=False)
```
